32 devices in a mesh: grp: 2 (over y), freq: 16 (over z, x, core).
Axes of the slice: x: 2, y: 2, z: 4, core: 2. Of those that a mesh axis runs over, the one named last changes fastest.
Arguments:
- source_field: bfloat16 [4, 16, 512, 256], P('grp', 'freq'), parts along dimension 0, may hold values from -6 to 6
- receiver_field: bfloat16 [4, 16, 512, 256], P('grp', 'freq'), parts along dimension 0, may hold values from -6 to 6
- slowness_slabs: bfloat16 [32, 768, 512], P(('grp', 'freq')), parts along dimension 0, may hold values from 0.3984375 to 1.1953125
- slab_map: int32 [4], P('grp'), parts along dimension 0, may hold values from 0 to 15
- reference_gaps: float32 [4, 3], P('grp'), parts along dimension 0, may hold values from 0.1 to 0.3
- reference_index: int32 [4, 512, 256], P('grp'), parts along dimension 0, may hold values from 0 to 1
- frequency_bins: int32 [16], replicated, may hold values from 10 to 120
- shot_corner: int32 [4], P('grp'), parts along dimension 0, may hold values from 0 to 256
Outputs:
- image: float32 [4, 512, 256, 256], P('grp', 'freq'), parts along dimension 0
The draws below stay inside these ranges and needn't reach their ends.
There are 2 independent parts, one for each index of `grp`. The reference program is written for one: setup_inputs(seed, part) draws one part's arguments, and reference() takes and returns one part's arrays. A program takes and returns all parts, laid end to end along the dimension named above; an argument that names none is the same for every part. Nothing has to cross between parts.
All inputs are finite; a program needn't handle non-finite values.
Results may differ from the reference program's by a relative error of at most 0.014.
Values may be sent and summed in bfloat16 or wider, within the bound.
No kernel may reach another device: no remote copies, remote signals or barrier semaphores. Data moves between devices by JAX's collectives and lax.ppermute only.
A program may use at most 128 MiB of HBM per device.

```python
import math
import jax
import jax.numpy as jnp
from jax import lax

NX = 512
NY = 256
LAGS = 256
NREF = 3
DEPTHS = 2
SPAN = 256
NW = 16
SLABS = 16
MX = 768
MY = 512


def place_ends(values, key, smallest, high):
    dims = values.shape
    spot = [jax.random.randint(jax.random.fold_in(key, axis), (), 0, dims[axis]) for axis in range(len(dims))]
    values = values.at[tuple(spot)].set(smallest)
    longest = dims.index(max(dims))
    spot[longest] = (spot[longest] + 1) % dims[longest]
    return values.at[tuple(spot)].set(high)


def steps_of(key, dims, pieces, low, largest):
    level = 1.0
    for dim, blocks in pieces:
        steps = jax.random.uniform(jax.random.fold_in(jax.random.fold_in(key, 6), dim), (blocks,), jnp.float32, low / len(pieces), largest / len(pieces))
        level = level * jnp.repeat(jnp.exp(steps), dims[dim] // blocks).reshape((-1,) + (1,) * (len(dims) - 1 - dim))
    return level


def normal_values(stream_key, shape, spread, reach, shards=(), held_as=jnp.bfloat16):
    level = steps_of(stream_key, shape, shards, -0.22, 0.18) if shards else 1.0
    result = jax.random.normal(stream_key, shape, jnp.float32) * spread * level
    return jnp.minimum(jnp.maximum(result, -reach), reach).astype(held_as)


def setup_inputs(seed: int = 0, part: int = 0) -> dict:
    keys = jax.random.split(jax.random.key(seed), 9)
    part_splits = jax.random.split(jax.random.fold_in(keys[8], part), 9)
    source_field = normal_values(part_splits[0], (2, NW, NX, NY), 1.0, 6.0, ((1, 16),))
    receiver_field = normal_values(part_splits[1], (2, NW, NX, NY), 1.0, 6.0, ((1, 16),))
    slowness_slabs = jnp.clip(0.3984375 + 0.796875 * jax.random.uniform(part_splits[2], (SLABS, MX, MY), jnp.float32) ** steps_of(part_splits[2], (SLABS, MX, MY), ((0, 16),), -0.2, 0.2), 0.3984375, 1.1953125).astype(jnp.bfloat16)
    slab_map = jax.random.randint(part_splits[3], (DEPTHS,), 0, SLABS).astype(jnp.int32)
    reference_gaps = jnp.clip(jnp.exp(jax.random.uniform(part_splits[4], (DEPTHS, NREF), jnp.float32, math.log(0.1), math.log(0.3))), 0.1, 0.3)
    reference_index = place_ends(jax.random.randint(part_splits[5], (DEPTHS, NX, NY), 0, NREF - 1), jax.random.fold_in(part_splits[5], 1), 0, (NREF - 1) - 1).astype(jnp.int32)
    frequency_bins = place_ends(jax.random.randint(keys[6], (NW,), 10, 121), jax.random.fold_in(keys[6], 1), 10, 120).astype(jnp.int32)
    shot_corner = jax.random.randint(part_splits[7], (2,), 0, SPAN + 1).astype(jnp.int32)
    return {"source_field": source_field, "receiver_field": receiver_field, "slowness_slabs": slowness_slabs, "slab_map": slab_map, "reference_gaps": reference_gaps, "reference_index": reference_index, "frequency_bins": frequency_bins, "shot_corner": shot_corner}


cell_width = 0.0125
layer_thick = 0.0125
bin_hertz = 0.5
period_bins = 500
slow_base = 0.3

def transform_table(length, forward):
    grid_steps = jnp.arange(length, dtype=jnp.int32)
    phases = jnp.mod(grid_steps[:, None] * grid_steps[None, :], length).astype(jnp.float32)
    angles = phases * (2.0 * math.pi / length)
    norm_scale = 1.0 / math.sqrt(length)
    cosine = jnp.cos(angles) * norm_scale
    sine_part = jnp.sin(angles) * norm_scale
    if forward:
        cross_term = -sine_part
    else:
        cross_term = sine_part
    return jnp.stack([jnp.stack([cosine, cross_term]), jnp.stack([-cross_term, cosine])]).astype(jnp.bfloat16)

def wave_numbers(length):
    grid_steps = jnp.arange(length, dtype=jnp.int32)
    folded = jnp.where(grid_steps < length // 2, grid_steps, grid_steps - length).astype(jnp.float32)
    return folded * (2.0 * math.pi / (length * cell_width))

def lag_table(frequency_bins, lag_count):
    offsets = jnp.arange(lag_count, dtype=jnp.int32) - lag_count // 2
    cycles = jnp.mod(frequency_bins[:, None] * offsets[None, :], period_bins).astype(jnp.float32)
    angles = cycles * (2.0 * math.pi / period_bins)
    return jnp.stack([jnp.cos(angles), -jnp.sin(angles)]).astype(jnp.bfloat16)

def phase_factors(angular, references, squares):
    radicand = (angular * references[:, None, None]) ** 2 - squares[None]
    vertical = jnp.sqrt(jnp.maximum(radicand, 0.0))
    fading = jnp.exp(-jnp.sqrt(jnp.maximum(-radicand, 0.0)) * layer_thick)
    return (fading * jnp.cos(vertical * layer_thick), fading * jnp.sin(vertical * layer_thick))

def rotate(field_pair, turn_angle):
    return jnp.stack([jnp.cos(turn_angle) * field_pair[0] - jnp.sin(turn_angle) * field_pair[1], jnp.cos(turn_angle) * field_pair[1] + jnp.sin(turn_angle) * field_pair[0]])

def extrapolate(field, angular, slowness, references, bracket, direction, tables, squares):
    forward_x, forward_y, inverse_x, inverse_y = tables
    half_done = jnp.einsum('cxy,cdyk->dxk', field.astype(jnp.float32), forward_y).astype(jnp.bfloat16)
    spectrum = jnp.einsum('cdxk,cxy->dky', forward_x, half_done.astype(jnp.float32))
    cos_part, sin_part = phase_factors(angular, references, squares)
    sin_part = direction * sin_part
    shifted = jnp.stack([cos_part * spectrum[0] - sin_part * spectrum[1], cos_part * spectrum[1] + sin_part * spectrum[0]], axis=1).astype(jnp.bfloat16)
    returned = jnp.einsum('cdxk,jcxy->jdky', inverse_x, shifted.astype(jnp.float32)).astype(jnp.bfloat16)
    refocused = jnp.einsum('jcxy,cdyk->jdxk', returned.astype(jnp.float32), inverse_y)
    lower_pair = bracket == 0
    lower_field = jnp.where(lower_pair[None], refocused[0], refocused[1])
    upper_field = jnp.where(lower_pair[None], refocused[1], refocused[2])
    slow_low = jnp.where(lower_pair, references[0], references[1])
    slow_high = jnp.where(lower_pair, references[1], references[2])
    weight = jnp.clip((slowness - slow_low) / (slow_high - slow_low), 0.0, 1.0)
    turn_low = direction * angular * layer_thick * (slowness - slow_low)
    turn_high = direction * angular * layer_thick * (slowness - slow_high)
    mixed = (1.0 - weight) * rotate(lower_field, turn_low) + weight * rotate(upper_field, turn_high)
    return mixed.astype(jnp.bfloat16)

def reference(source_field, receiver_field, slowness_slabs, slab_map, reference_gaps, reference_index, frequency_bins, shot_corner):
    tables = (transform_table(NX, True).astype(jnp.float32), transform_table(NY, True).astype(jnp.float32), transform_table(NX, False).astype(jnp.float32), transform_table(NY, False).astype(jnp.float32))
    wave_x = wave_numbers(NX)
    wave_y = wave_numbers(NY)
    squares = wave_x[:, None] ** 2 + wave_y[None, :] ** 2
    omegas = frequency_bins.astype(jnp.float32) * (2.0 * math.pi * bin_hertz)
    slow_list = []
    ref_list = []
    for depth_step in range(DEPTHS):
        slab = lax.dynamic_index_in_dim(slowness_slabs, slab_map[depth_step].astype(jnp.int32), 0, keepdims=False)
        window = lax.dynamic_slice(slab, (shot_corner[0].astype(jnp.int32), shot_corner[1].astype(jnp.int32)), (NX, NY))
        slow_list.append(window.astype(jnp.float32))
        ref_list.append(slow_base + jnp.cumsum(reference_gaps[depth_step]))

    def one_frequency(inputs):
        source, receiver, angular = inputs
        crosses = []
        for depth_step in range(DEPTHS):
            source = extrapolate(source, angular, slow_list[depth_step], ref_list[depth_step], reference_index[depth_step], 1.0, tables, squares)
            receiver = extrapolate(receiver, angular, slow_list[depth_step], ref_list[depth_step], reference_index[depth_step], -1.0, tables, squares)
            src_values = source.astype(jnp.float32)
            rec_values = receiver.astype(jnp.float32)
            real_part = src_values[0] * rec_values[0] + src_values[1] * rec_values[1]
            imag_part = src_values[0] * rec_values[1] - src_values[1] * rec_values[0]
            crosses.append(jnp.stack([real_part, imag_part]).astype(jnp.bfloat16))
        return jnp.stack(crosses)
    crosses = lax.map(one_frequency, (jnp.moveaxis(source_field, 1, 0), jnp.moveaxis(receiver_field, 1, 0), omegas))
    lag_weights = lag_table(frequency_bins, LAGS).astype(jnp.float32)
    images = []
    for depth_step in range(DEPTHS):
        summed = jnp.einsum('wcxy,cwl->xyl', crosses[:, depth_step].astype(jnp.float32), lag_weights)
        images.append(summed * NW ** (-0.5))
    return jnp.stack(images)
```

```python
import functools
import math

import jax
import jax.numpy as jnp
import numpy as np
from jax import lax
from jax.experimental import pallas as pl
from jax.experimental.pallas import tpu as pltpu
from jax.sharding import PartitionSpec as P

LAGS = 256

cell_width = 0.0125
layer_thick = 0.0125
bin_hertz = 0.5
period_bins = 500
slow_base = 0.3

VMEM = pltpu.VMEM
SMEM = pltpu.SMEM
f32 = jnp.float32
bf16 = jnp.bfloat16


def real_table(length):
    half = length // 2
    steps = np.arange(length, dtype=np.int64)
    wave = np.concatenate([np.arange(half), [half], np.arange(1, half)])
    phases = np.mod(steps[:, None] * wave[None, :], length).astype(np.float32)
    angles = phases * np.float32(2.0 * math.pi / length)
    scale = np.float32(1.0 / math.sqrt(length))
    is_cos = np.arange(length) <= half
    table = np.where(is_cos[None, :], np.cos(angles), np.sin(angles)) * scale
    twice = np.where((wave == 0) | (wave == half), 1.0, 2.0)
    forward = jnp.asarray(table.astype(np.float32)).astype(bf16)
    inverse = (forward.astype(f32) * jnp.asarray(twice[None, :], f32)).astype(bf16)
    return forward, inverse


def sin_cos(angle):
    turns = jnp.floor(angle * (2.0 / math.pi) + 0.5)
    rest = angle - turns * 1.5707397460937500
    rest = rest - turns * 5.6580702948965924e-05
    quadrant = turns.astype(jnp.int32)
    square = rest * rest
    sine = rest + rest * square * (
        -1.6666654611e-1 + square * (8.3321608736e-3 - square * 1.9515295891e-4)
    )
    cosine = (
        1.0
        - 0.5 * square
        + square
        * square
        * (4.166664568298827e-2 + square * (-1.388731625493765e-3 + square * 2.443315711809948e-5))
    )
    odd = (quadrant & 1) == 1
    out_sin = jnp.where(odd, cosine, sine)
    out_cos = jnp.where(odd, sine, cosine)
    out_sin = jnp.where((quadrant & 2) == 2, -out_sin, out_sin)
    out_cos = jnp.where(((quadrant + 1) & 2) == 2, -out_cos, out_cos)
    return out_sin, out_cos


def references_of(gaps_ref, depth):
    first = slow_base + gaps_ref[depth, 0]
    second = first + gaps_ref[depth, 1]
    third = second + gaps_ref[depth, 2]
    return first, second, third


def angular_of(bins_ref):
    return bins_ref[lax.axis_index("freq")].astype(f32) * (2.0 * math.pi * bin_hertz)


def phase_block(reach, base_turn, squares):
    radicand = reach - squares
    root = jnp.sqrt(jnp.abs(radicand)) * layer_thick
    travelling = radicand > 0.0
    fading = jnp.where(travelling, 1.0, jnp.exp(-root))
    sine, cosine = sin_cos(jnp.where(travelling, root, 0.0) - base_turn)
    return fading * cosine, fading * sine


def make_phases(cos_ref, sin_ref, angular, reference):
    rows, cols = cos_ref.shape
    half = rows // 2
    reach = (angular * reference) * (angular * reference)
    base_turn = angular * layer_thick * reference
    step_x = 2.0 * math.pi / (rows * cell_width)
    step_y = 2.0 * math.pi / (cols * cell_width)
    lane = lax.broadcasted_iota(jnp.int32, (8, cols), 1)
    wave_y = jnp.where(lane <= cols // 2, lane, lane - cols // 2).astype(f32) * step_y
    square_y = wave_y * wave_y
    tall = 64

    def body(block, carry):
        start = pl.multiple_of(block * tall, tall)
        row = lax.broadcasted_iota(jnp.int32, (tall, cols), 0) + start
        wave_x = row.astype(f32) * step_x
        cosine, sine = phase_block(
            reach, base_turn, wave_x * wave_x + jnp.concatenate([square_y] * (tall // 8), axis=0)
        )
        cos_ref[pl.ds(start, tall), :] = cosine
        sin_ref[pl.ds(start, tall), :] = sine
        cos_ref[pl.ds(half + start, tall), :] = cosine
        sin_ref[pl.ds(half + start, tall), :] = sine
        return carry

    lax.fori_loop(0, half // tall, body, 0)
    edge = (half * step_x) ** 2
    cosine, sine = phase_block(reach, base_turn, edge + square_y)
    top = lax.broadcasted_iota(jnp.int32, (8, cols), 0) == 0
    cos_ref[half : half + 8, :] = jnp.where(top, cosine, cos_ref[half : half + 8, :])
    sin_ref[half : half + 8, :] = jnp.where(top, sine, sin_ref[half : half + 8, :])


def dot(left, right):
    return jnp.dot(left, right, preferred_element_type=f32)


def march(
    wave_ref, angular, references, tables, half_ref, spec_ref, cos_ref, sin_ref, shift_ref, out_ref
):
    forward_x, forward_y, inverse_x = tables
    for plane in range(4):
        half_ref[plane] = dot(wave_ref[plane], forward_y[...]).astype(bf16)
    for plane in range(4):
        spec_ref[plane] = dot(forward_x[...], half_ref[plane])
    for j in range(3):
        make_phases(cos_ref.at[j], sin_ref.at[j], angular, references[j])
    for j in range(3):
        for field in range(2):
            real, imag = spec_ref[2 * field], spec_ref[2 * field + 1]
            cosine, sine = cos_ref[j], sin_ref[j]
            shift_ref[j, 2 * field] = (cosine * real - sine * imag).astype(bf16)
            shift_ref[j, 2 * field + 1] = (cosine * imag + sine * real).astype(bf16)
        for plane in range(4):
            out_ref[j, plane] = dot(inverse_x[...], shift_ref[j, plane]).astype(bf16)


def blend(
    returned_ref, slow_ref, bracket_ref, depth, angular, references, inverse_y, wave_ref, cross_ref
):
    rows, cols = slow_ref.shape[1:]
    tile = cross_ref.shape[3]
    tall = max(tile, 64)
    low, mid, high = references
    ones = jnp.ones((8, cols), f32)
    slope_low = (1.0 / (ones * (mid - low)))[:1]
    slope_high = (1.0 / (ones * (high - mid)))[:1]

    def body(block, carry):
        start = pl.multiple_of(block * tall, tall)
        here = pl.ds(start, tall)
        slow = slow_ref[depth, here, :].astype(f32)
        lower = bracket_ref[depth, here, :] == 0
        weight = jnp.where(lower, (slow - low) * slope_low, (slow - mid) * slope_high)
        weight = jnp.minimum(jnp.maximum(weight, 0.0), 1.0)
        sine, cosine = sin_cos(slow * (angular * layer_thick))
        halves = []
        for plane in range(4):
            parts = [dot(returned_ref[j, plane, here, :], inverse_y[...]) for j in range(3)]
            bottom = jnp.where(lower, parts[0], parts[1])
            top = jnp.where(lower, parts[1], parts[2])
            halves.append(bottom + weight * (top - bottom))
        fresh = []
        for field in range(2):
            real, imag = halves[2 * field], halves[2 * field + 1]
            fresh.append((cosine * real - sine * imag).astype(bf16))
            fresh.append((cosine * imag + sine * real).astype(bf16))
        for plane in range(4):
            wave_ref[plane, here, :] = fresh[plane]
        s_real, s_imag, r_real, r_imag = [value.astype(f32) for value in fresh]
        cross_real = (s_real * r_real - s_imag * r_imag).astype(bf16)
        cross_imag = (s_real * r_imag + s_imag * r_real).astype(bf16)
        for part in range(tall // tile):
            spot = block * (tall // tile) + part
            cross_ref[spot, depth, 0] = cross_real[part * tile : (part + 1) * tile]
            cross_ref[spot, depth, 1] = cross_imag[part * tile : (part + 1) * tile]
        return carry

    lax.fori_loop(0, rows // tall, body, 0)


def window_kernel(map_ref, corner_ref, slab_ref, keep_ref, send_ref, turned_ref, *, slab_count):
    depth = pl.program_id(0)
    rank = lax.axis_index("freq")
    core, side = rank % 2, (rank // 2) % 2
    quarter, cols = keep_ref.shape[2:]
    wide = slab_ref.shape[2]
    turn = lax.rem(wide - corner_ref[1], wide)
    turned_ref[: slab_ref.shape[1], :] = pltpu.roll(slab_ref[0].astype(f32), turn, 1)[:, :cols]
    mine = map_ref[depth] // slab_count == rank
    above = lax.rem(corner_ref[0], 8)
    first_row = corner_ref[0] - above
    tall = quarter + 8
    for other_core in range(2):
        target = keep_ref if other_core == 0 else send_ref
        for other_side in range(2):
            spot = 2 * ((core + other_core) % 2) + (side + other_side) % 2
            block = turned_ref[pl.ds(pl.multiple_of(first_row + spot * quarter, 8), tall), :]
            block = pltpu.roll(block, lax.rem(tall - above, tall), 0)[:quarter]
            target[other_side, 0] = jnp.where(mine, block, 0.0).astype(bf16)


def first_kernel(
    bins_ref,
    gaps_ref,
    source_ref,
    receiver_ref,
    forward_x,
    forward_y,
    inverse_x,
    out_ref,
    wave_ref,
    half_ref,
    spec_ref,
    cos_ref,
    sin_ref,
    shift_ref,
):
    wave_ref[0] = source_ref[0, 0]
    wave_ref[1] = source_ref[1, 0]
    wave_ref[2] = receiver_ref[0, 0]
    wave_ref[3] = -receiver_ref[1, 0]
    march(
        wave_ref,
        angular_of(bins_ref),
        references_of(gaps_ref, 0),
        (forward_x, forward_y, inverse_x),
        half_ref,
        spec_ref,
        cos_ref,
        sin_ref,
        shift_ref,
        out_ref,
    )


def second_kernel(
    bins_ref,
    gaps_ref,
    returned_ref,
    quarter_refs,
    bracket_ref,
    forward_x,
    forward_y,
    inverse_x,
    inverse_y,
    cross_ref,
    slow_ref,
    wave_ref,
    half_ref,
    spec_ref,
    cos_ref,
    sin_ref,
    shift_ref,
    later_ref,
    *,
    depths,
):
    rank = lax.axis_index("freq")
    core, side = rank % 2, (rank // 2) % 2
    quarter = quarter_refs[0].shape[1]
    for index, (other_core, other_side) in enumerate(((0, 0), (0, 1), (1, 0), (1, 1))):
        spot = 2 * ((core + other_core) % 2) + (side + other_side) % 2
        start = pl.multiple_of(spot * quarter, quarter)
        for depth in range(depths):
            slow_ref[depth, pl.ds(start, quarter), :] = quarter_refs[index][depth]
    angular = angular_of(bins_ref)
    for depth in range(depths):
        references = references_of(gaps_ref, depth)
        if depth:
            march(
                wave_ref,
                angular,
                references,
                (forward_x, forward_y, inverse_x),
                half_ref,
                spec_ref,
                cos_ref,
                sin_ref,
                shift_ref,
                later_ref,
            )
        blend(
            later_ref if depth else returned_ref,
            slow_ref,
            bracket_ref,
            depth,
            angular,
            references,
            inverse_y,
            wave_ref,
            cross_ref,
        )


def image_kernel(cross_ref, lag_ref, out_ref, weight_ref, *, scale):
    bins, _, pair, tall, cols = cross_ref.shape
    depth_of = bins * pair * tall
    lags = lag_ref.shape[2]

    @pl.when((pl.program_id(0) == 0) & (pl.program_id(1) == 0))
    def _():
        table = jnp.broadcast_to(
            lag_ref[...].reshape(bins * pair, 1, lags), (bins * pair, tall, lags)
        ).reshape(depth_of, lags)
        place = lax.broadcasted_iota(jnp.int32, (depth_of, lags), 0) % tall
        for row in range(tall):
            weight_ref[:, row * lags : (row + 1) * lags] = jnp.where(
                place == row, table, 0.0
            ).astype(bf16)

    left = cross_ref[...].astype(f32).reshape(depth_of, cols).T.astype(bf16)
    for row in range(tall):
        out_ref[0, row] = dot(left, weight_ref[:, row * lags : (row + 1) * lags]) * scale


def plain(shape_list):
    return [pl.BlockSpec(memory_space=VMEM) for _ in range(shape_list)]


def shards(
    source_field,
    receiver_field,
    slowness_slabs,
    slab_map,
    reference_gaps,
    reference_index,
    frequency_bins,
    shot_corner,
    *,
    ranks,
):
    rows, cols = source_field.shape[2:]
    depths = slab_map.shape[0]
    slab_count = slowness_slabs.shape[0]
    quarter = rows // 4
    tile = rows // ranks
    bins = frequency_bins.shape[0]
    slab_shape = slowness_slabs.shape[1:]
    forward_x, inverse_x = real_table(rows)
    forward_x = forward_x.T
    forward_y, inverse_y = real_table(cols)
    inverse_y = inverse_y.T

    keep, send = pl.pallas_call(
        functools.partial(window_kernel, slab_count=slab_count),
        grid_spec=pltpu.PrefetchScalarGridSpec(
            num_scalar_prefetch=2,
            grid=(depths,),
            in_specs=[
                pl.BlockSpec((1,) + slab_shape, lambda d, slabs, corner: (slabs[d] % slab_count, 0, 0))
            ],
            out_specs=[
                pl.BlockSpec((2, 1, quarter, cols), lambda d, slabs, corner: (0, d, 0, 0))
            ]
            * 2,
            scratch_shapes=[VMEM((slab_shape[0] + 8, cols), f32)],
        ),
        out_shape=[jax.ShapeDtypeStruct((2, depths, quarter, cols), bf16)] * 2,
        compiler_params=pltpu.CompilerParams(vmem_limit_bytes=32 << 20),
        name="window",
    )(slab_map, shot_corner, slowness_slabs)

    def swap(value, bit):
        return lax.ppermute(value, "freq", [(i, i ^ bit) for i in range(ranks)])

    held = keep + swap(send, 1)
    quarters = held[0] + swap(held[1], 2)
    bit = 4
    while bit < ranks:
        quarters = quarters + swap(quarters, bit)
        bit *= 2
    beside = swap(quarters, 2)
    across = swap(quarters, 1)
    corner_ways = swap(beside, 1)

    march_scratch = [
        VMEM((4, rows, cols), bf16),
        VMEM((4, rows, cols), bf16),
        VMEM((4, rows, cols), f32),
        VMEM((3, rows, cols), f32),
        VMEM((3, rows, cols), f32),
        VMEM((3, 4, rows, cols), bf16),
    ]
    smem = pl.BlockSpec(memory_space=SMEM)
    flops = 2 * 4 * (1 + 3) * rows * rows * cols
    returned = pl.pallas_call(
        first_kernel,
        in_specs=[smem, smem] + plain(5),
        out_specs=pl.BlockSpec(memory_space=VMEM),
        out_shape=jax.ShapeDtypeStruct((3, 4, rows, cols), bf16),
        scratch_shapes=march_scratch,
        compiler_params=pltpu.CompilerParams(vmem_limit_bytes=40 << 20),
        cost_estimate=pl.CostEstimate(flops=4 * flops, bytes_accessed=8 << 20, transcendentals=0),
        name="first",
    )(
        frequency_bins,
        reference_gaps,
        source_field,
        receiver_field,
        forward_x,
        forward_y,
        inverse_x,
    )

    def second(bins_ref, gaps_ref, returned_ref, q0, q1, q2, q3, *rest):
        second_kernel(bins_ref, gaps_ref, returned_ref, (q0, q1, q2, q3), *rest, depths=depths)

    crosses = pl.pallas_call(
        second,
        in_specs=[smem, smem] + plain(10),
        out_specs=pl.BlockSpec(memory_space=VMEM),
        out_shape=jax.ShapeDtypeStruct((ranks, depths, 2, tile, cols), bf16),
        scratch_shapes=[VMEM((depths, rows, cols), bf16)]
        + march_scratch
        + [VMEM((3, 4, rows, cols), bf16)],
        compiler_params=pltpu.CompilerParams(vmem_limit_bytes=50 << 20),
        name="second",
    )(
        frequency_bins,
        reference_gaps,
        returned,
        quarters,
        beside,
        across,
        corner_ways,
        reference_index,
        forward_x,
        forward_y,
        inverse_x,
        inverse_y,
    )

    offsets = jnp.arange(LAGS, dtype=jnp.int32) - LAGS // 2
    cycles = jnp.mod(frequency_bins[:, None] * offsets[None, :], period_bins).astype(f32)
    angles = cycles * (2.0 * math.pi / period_bins)
    lag_weights = jnp.stack([jnp.cos(angles), jnp.sin(angles)], axis=1).astype(bf16)

    arrived = lax.all_to_all(crosses, "freq", split_axis=0, concat_axis=0, tiled=True)
    scale = bins ** (-0.5)
    tall = 8
    if tile % (2 * tall):
        summed = jnp.einsum(
            "wdcab,wcl->dabl", arrived, lag_weights, preferred_element_type=f32
        )
        return summed * scale
    return pl.pallas_call(
        functools.partial(image_kernel, scale=scale),
        grid=(depths, tile // tall),
        in_specs=[
            pl.BlockSpec((bins, 1, 2, tall, cols), lambda d, t: (0, d, 0, t, 0)),
            pl.BlockSpec((bins, 2, LAGS), lambda d, t: (0, 0, 0)),
        ],
        out_specs=pl.BlockSpec((1, tall, cols, LAGS), lambda d, t: (d, t, 0, 0)),
        out_shape=jax.ShapeDtypeStruct((depths, tile, cols, LAGS), f32),
        scratch_shapes=[VMEM((bins * 2 * tall, tall * LAGS), bf16)],
        compiler_params=pltpu.CompilerParams(vmem_limit_bytes=32 << 20),
        name="image",
    )(arrived, lag_weights.astype(f32))


def solution(mesh):
    placed = (
        P("grp", "freq", None, None),
        P("grp", "freq", None, None),
        P(("grp", "freq"), None, None),
        P("grp"),
        P("grp", None),
        P("grp", None, None),
        P(),
        P("grp"),
    )
    return jax.shard_map(
        functools.partial(shards, ranks=mesh.shape["freq"]),
        mesh=mesh,
        in_specs=placed,
        out_specs=P("grp", "freq", None, None),
        check_vma=False,
    )
```

```python
import functools
import math

import jax
import jax.numpy as jnp
import numpy as np
from jax import lax
from jax.experimental import pallas as pl
from jax.experimental.pallas import tpu as pltpu
from jax.sharding import PartitionSpec as P

LAGS = 256

cell_width = 0.0125
layer_thick = 0.0125
bin_hertz = 0.5
period_bins = 500
slow_base = 0.3

VMEM = pltpu.VMEM
SMEM = pltpu.SMEM
f32 = jnp.float32
bf16 = jnp.bfloat16


def real_table(length):
    half = length // 2
    steps = np.arange(length, dtype=np.int64)
    wave = np.concatenate([np.arange(half), [half], np.arange(1, half)])
    phases = np.mod(steps[:, None] * wave[None, :], length).astype(np.float32)
    angles = phases * np.float32(2.0 * math.pi / length)
    scale = np.float32(1.0 / math.sqrt(length))
    is_cos = np.arange(length) <= half
    table = np.where(is_cos[None, :], np.cos(angles), np.sin(angles)) * scale
    twice = np.where((wave == 0) | (wave == half), 1.0, 2.0)
    forward = jnp.asarray(table.astype(np.float32)).astype(bf16)
    inverse = (forward.astype(f32) * jnp.asarray(twice[None, :], f32)).astype(bf16)
    return forward, inverse


def sin_cos(angle):
    turns = jnp.floor(angle * (2.0 / math.pi) + 0.5)
    rest = angle - turns * 1.5707397460937500
    rest = rest - turns * 5.6580702948965924e-05
    quadrant = turns.astype(jnp.int32)
    square = rest * rest
    sine = rest + rest * square * (
        -1.6666654611e-1 + square * (8.3321608736e-3 - square * 1.9515295891e-4)
    )
    cosine = (
        1.0
        - 0.5 * square
        + square
        * square
        * (4.166664568298827e-2 + square * (-1.388731625493765e-3 + square * 2.443315711809948e-5))
    )
    odd = (quadrant & 1) == 1
    out_sin = jnp.where(odd, cosine, sine)
    out_cos = jnp.where(odd, sine, cosine)
    out_sin = jnp.where((quadrant & 2) == 2, -out_sin, out_sin)
    out_cos = jnp.where(((quadrant + 1) & 2) == 2, -out_cos, out_cos)
    return out_sin, out_cos


def references_of(gaps_ref, depth):
    first = slow_base + gaps_ref[depth, 0]
    second = first + gaps_ref[depth, 1]
    third = second + gaps_ref[depth, 2]
    return first, second, third


def scalars_of(held_ref, depth):
    rows = [held_ref[row : row + 1] for row in (0, *range(1 + 3 * depth, 4 + 3 * depth))]
    return rows[0], tuple(rows[1:])


def angular_of(bins_ref):
    return bins_ref[lax.axis_index("freq")].astype(f32) * (2.0 * math.pi * bin_hertz)


def phase_block(reach, base_turn, squares):
    radicand = reach - squares
    root = jnp.sqrt(jnp.abs(radicand)) * layer_thick
    travelling = radicand > 0.0
    fading = jnp.where(travelling, 1.0, jnp.exp(-root))
    sine, cosine = sin_cos(jnp.where(travelling, root, 0.0) - base_turn)
    return fading * cosine, fading * sine


def make_phases(cos_ref, sin_ref, angular, reference):
    rows, cols = cos_ref.shape
    half = rows // 2
    reach = (angular * reference) * (angular * reference)
    base_turn = angular * layer_thick * reference
    step_x = 2.0 * math.pi / (rows * cell_width)
    step_y = 2.0 * math.pi / (cols * cell_width)
    lane = lax.broadcasted_iota(jnp.int32, (8, cols), 1)
    wave_y = jnp.where(lane <= cols // 2, lane, lane - cols // 2).astype(f32) * step_y
    square_y = wave_y * wave_y
    tall = 64

    def body(block, carry):
        start = pl.multiple_of(block * tall, tall)
        row = lax.broadcasted_iota(jnp.int32, (tall, cols), 0) + start
        wave_x = row.astype(f32) * step_x
        cosine, sine = phase_block(
            reach, base_turn, wave_x * wave_x + jnp.concatenate([square_y] * (tall // 8), axis=0)
        )
        cos_ref[pl.ds(start, tall), :] = cosine
        sin_ref[pl.ds(start, tall), :] = sine
        cos_ref[pl.ds(half + start, tall), :] = cosine
        sin_ref[pl.ds(half + start, tall), :] = sine
        return carry

    lax.fori_loop(0, half // tall, body, 0)
    edge = (half * step_x) ** 2
    cosine, sine = phase_block(reach, base_turn, edge + square_y)
    top = lax.broadcasted_iota(jnp.int32, (8, cols), 0) == 0
    cos_ref[half : half + 8, :] = jnp.where(top, cosine, cos_ref[half : half + 8, :])
    sin_ref[half : half + 8, :] = jnp.where(top, sine, sin_ref[half : half + 8, :])


def dot(left, right):
    return jnp.dot(left, right, preferred_element_type=f32)


def march(plane_of, signs, tables, scalars, scratch, out_ref, ready=(None, None, None)):
    forward_x, forward_y, inverse_x = tables
    angular, references = scalars
    half_ref, spec_ref, cos_ref, sin_ref, shift_ref = scratch
    for j in range(3):
        make_phases(cos_ref.at[j], sin_ref.at[j], angular, references[j])
    for wait in ready[0] or ():
        wait()
    for plane in range(4):
        half = dot(plane_of(plane), forward_y[...])
        half_ref[plane] = (half if signs[plane] > 0 else -half).astype(bf16)
    for wait in ready[1] or ():
        wait()
    for plane in range(4):
        spec_ref[plane] = dot(forward_x[...], half_ref[plane])
    for wait in ready[2] or ():
        wait()
    for j in range(3):
        for field in range(2):
            real, imag = spec_ref[2 * field], spec_ref[2 * field + 1]
            cosine, sine = cos_ref[j], sin_ref[j]
            shift_ref[j, 2 * field] = (cosine * real - sine * imag).astype(bf16)
            shift_ref[j, 2 * field + 1] = (cosine * imag + sine * real).astype(bf16)
        for plane in range(4):
            out_ref[j, plane] = dot(inverse_x[...], shift_ref[j, plane]).astype(bf16)


BLEND_ROWS = 64


def blend(returned_ref, slow_of, bracket_ref, inverse_y, scalars, parts, put_wave, put_cross, starts):
    rows, cols = bracket_ref.shape
    tall = BLEND_ROWS
    chunk = 16
    angular, (low, mid, high) = scalars
    slope_low = 1.0 / (mid - low)
    slope_high = 1.0 / (high - mid)
    blocks = rows // tall

    def first_row(block):
        return pl.multiple_of(block * tall if starts is None else starts[block], tall)

    def fill(part_ref, block):
        left = returned_ref[:, :, pl.ds(first_row(block), tall), :].reshape(12 * tall, cols)
        part_ref[...] = dot(left, inverse_y[...]).reshape(12, tall, cols)

    def mix(part_ref, block):
        start = first_row(block)
        crossed = []
        for piece in range(tall // chunk):
            within = slice(piece * chunk, (piece + 1) * chunk)
            here = pl.ds(start + piece * chunk, chunk)
            slow = slow_of(block, here, within).astype(f32)
            lower = bracket_ref[here, :] == 0
            weight = jnp.where(lower, (slow - low) * slope_low, (slow - mid) * slope_high)
            weight = jnp.minimum(jnp.maximum(weight, 0.0), 1.0)
            sine, cosine = sin_cos(slow * (angular * layer_thick))
            halves = []
            for plane in range(4):
                first, second, third = [part_ref[4 * j + plane, within] for j in range(3)]
                bottom = jnp.where(lower, first, second)
                top = jnp.where(lower, second, third)
                halves.append(bottom + weight * (top - bottom))
            fresh = []
            for field in range(2):
                real, imag = halves[2 * field], halves[2 * field + 1]
                fresh.append((cosine * real - sine * imag).astype(bf16))
                fresh.append((cosine * imag + sine * real).astype(bf16))
            if put_wave is not None:
                for plane in range(4):
                    put_wave(block, here, within, plane, fresh[plane])
            s_real, s_imag, r_real, r_imag = [value.astype(f32) for value in fresh]
            crossed.append(
                (
                    (s_real * r_real - s_imag * r_imag).astype(bf16),
                    (s_real * r_imag + s_imag * r_real).astype(bf16),
                )
            )
        for side in range(2):
            put_cross(block, side, jnp.concatenate([pair[side] for pair in crossed], axis=0))

    even, odd = parts
    if starts is not None:
        fill(even, 0)
        for block in range(len(starts)):
            if block + 1 < len(starts):
                fill(odd if block % 2 == 0 else even, block + 1)
            mix(even if block % 2 == 0 else odd, block)
        return
    fill(even, 0)

    def body(step, carry):
        fill(odd, 2 * step + 1)
        mix(even, 2 * step)
        fill(even, jnp.minimum(2 * step + 2, blocks - 1))
        mix(odd, 2 * step + 1)
        return carry

    lax.fori_loop(0, blocks // 2, body, 0)


def put_tiles(cross_ref, first, side, values):
    tile = cross_ref.shape[2]
    for part in range(values.shape[0] // tile):
        cross_ref[first + part, side] = values[part * tile : (part + 1) * tile]


def spots():
    rank = lax.axis_index("freq")
    core, side = rank % 2, (rank // 2) % 2
    return [
        2 * ((core + other_core) % 2) + (side + other_side) % 2
        for other_core, other_side in ((0, 0), (0, 1), (1, 0), (1, 1))
    ]


def window_kernel(
    map_hbm, corner_hbm, slab_hbm, keep_ref, send_ref, map_ref, corner_ref, slab_ref, sems
):
    depths, quarter, cols = keep_ref.shape[1:]
    slab_count = slab_hbm.shape[0]
    tall, wide = slab_hbm.shape[1:]
    copies = [
        pltpu.make_async_copy(map_hbm, map_ref, sems.at[0]),
        pltpu.make_async_copy(corner_hbm, corner_ref, sems.at[1]),
    ]
    for copy in copies:
        copy.start()
    if slab_count == 1:
        whole = pltpu.make_async_copy(slab_hbm.at[0], slab_ref.at[0], sems.at[2])
        whole.start()
    for copy in copies:
        copy.wait()
    if slab_count == 1:
        whole.wait()
    rank = lax.axis_index("freq")
    core, side = rank % 2, (rank // 2) % 2
    rows = 4 * quarter
    first_row = jnp.minimum((corner_ref[0] // 16) * 16, tall - rows - 16)
    first_col = jnp.minimum((corner_ref[1] // 128) * 128, wide - cols - 128)
    above = corner_ref[0] - first_row
    before = corner_ref[1] - first_col
    reach = quarter + 16
    span = cols + 128
    for depth in range(depths):
        slab = map_ref[depth]
        mine = slab // slab_count == rank

        @pl.when(mine)
        def _():
            if slab_count == 1:
                here = slab_ref.at[0]
            else:
                here = slab_ref.at[0]
                copy = pltpu.make_async_copy(
                    slab_hbm.at[lax.rem(slab, slab_count)], here, sems.at[2]
                )
                copy.start()
                copy.wait()
            for other_core in range(2):
                target = send_ref if other_core else keep_ref
                for other_side in range(2):
                    spot = 2 * ((core + other_core) % 2) + (side + other_side) % 2
                    block = here[
                        pl.ds(pl.multiple_of(first_row + spot * quarter, 16), reach),
                        pl.ds(pl.multiple_of(first_col, 128), span),
                    ].astype(f32)
                    block = pltpu.roll(block, lax.rem(span - before, span), 1)[:, :cols]
                    block = pltpu.roll(block, lax.rem(reach - above, reach), 0)[:quarter]
                    target[other_side, depth] = block.astype(bf16)

        @pl.when(jnp.logical_not(mine))
        def _():
            for other_side in range(2):
                keep_ref[other_side, depth] = jnp.zeros((quarter, cols), bf16)
                send_ref[other_side, depth] = jnp.zeros((quarter, cols), bf16)


def first_kernel(
    bins_hbm,
    gaps_hbm,
    source_hbm,
    receiver_hbm,
    forward_x_hbm,
    forward_y_hbm,
    inverse_x_hbm,
    bracket_hbm,
    inverse_y_hbm,
    out_ref,
    bracket_ref,
    inverse_y,
    held_ref,
    bins_ref,
    gaps_ref,
    wave_ref,
    forward_x,
    forward_y,
    inverse_x,
    sems,
    *scratch,
):
    pairs = [
        (bins_hbm, bins_ref),
        (gaps_hbm, gaps_ref),
        (forward_y_hbm, forward_y),
        (source_hbm.at[:, 0], wave_ref.at[0:2]),
        (receiver_hbm.at[:, 0], wave_ref.at[2:4]),
        (forward_x_hbm, forward_x),
        (inverse_x_hbm, inverse_x),
        (bracket_hbm.at[0], bracket_ref),
        (inverse_y_hbm, inverse_y),
    ]
    copies = [
        pltpu.make_async_copy(source, target, sems.at[index])
        for index, (source, target) in enumerate(pairs)
    ]
    for copy in copies:
        copy.start()
    copies[0].wait()
    copies[1].wait()
    angular = angular_of(bins_ref)
    held_ref[0:1] = jnp.full((1, held_ref.shape[1]), angular, f32)
    for depth in range(gaps_ref.shape[0]):
        for j, reference in enumerate(references_of(gaps_ref, depth)):
            row = 1 + 3 * depth + j
            held_ref[row : row + 1] = jnp.full((1, held_ref.shape[1]), reference, f32)
    march(
        lambda plane: wave_ref[plane],
        (1, 1, 1, -1),
        (forward_x, forward_y, inverse_x),
        (angular, references_of(gaps_ref, 0)),
        scratch,
        out_ref,
        ready=([copy.wait for copy in copies[2:5]], [copies[5].wait], [copies[6].wait]),
    )
    for copy in copies[7:]:
        copy.wait()


def mix_starts(which):
    quarter_spots = spots()
    return lambda quarter: [
        quarter_spots[index] * quarter + offset
        for index in which
        for offset in range(0, quarter, BLEND_ROWS)
    ]


def near_kernel(
    held_ref, returned_ref, q0, q2, bracket_ref, inverse_y, wave_ref, cross_ref, even, odd
):
    quarter = q0.shape[1]
    each = quarter // BLEND_ROWS
    tile = cross_ref.shape[2]
    own = (q0, q2)

    def put_wave(block, here, within, plane, values):
        part = slice((block % each) * BLEND_ROWS + within.start, (block % each) * BLEND_ROWS + within.stop)
        wave_ref[block // each, plane, part] = values

    blend(
        returned_ref,
        lambda block, here, within: own[block // each][
            0, (block % each) * BLEND_ROWS + within.start : (block % each) * BLEND_ROWS + within.stop
        ],
        bracket_ref,
        inverse_y,
        scalars_of(held_ref, 0),
        (even, odd),
        put_wave,
        lambda block, side, values: put_tiles(cross_ref, block * BLEND_ROWS // tile, side, values),
        mix_starts((0, 2))(quarter),
    )


def far_kernel(
    held_ref,
    returned_ref,
    q1,
    q3,
    bracket_ref,
    inverse_y,
    near_wave,
    near_cross,
    wave_ref,
    cross_ref,
    even,
    odd,
):
    quarter = q1.shape[1]
    each = quarter // BLEND_ROWS
    tile = cross_ref.shape[2]
    tiles = quarter // tile
    quarter_spots = spots()
    for index, spot in enumerate((quarter_spots[0], quarter_spots[2])):
        start = pl.multiple_of(spot * quarter, quarter)
        wave_ref[:, pl.ds(start, quarter), :] = near_wave[index]
        cross_ref[pl.ds(spot * tiles, tiles)] = near_cross[index * tiles : (index + 1) * tiles]
    own = (q1, q3)
    starts = mix_starts((1, 3))(quarter)

    def put_wave(block, here, within, plane, values):
        wave_ref[plane, here, :] = values

    def put_cross(block, side, values):
        put_tiles(cross_ref, starts[block] // tile, side, values)

    blend(
        returned_ref,
        lambda block, here, within: own[block // each][
            0, (block % each) * BLEND_ROWS + within.start : (block % each) * BLEND_ROWS + within.stop
        ],
        bracket_ref,
        inverse_y,
        scalars_of(held_ref, 0),
        (even, odd),
        put_wave,
        put_cross,
        starts,
    )


def later_kernel(
    held_ref,
    wave_ref,
    q0,
    q1,
    q2,
    q3,
    bracket_hbm,
    forward_x_hbm,
    forward_y_hbm,
    inverse_x_hbm,
    inverse_y,
    *rest,
    depth,
    last,
):
    if last:
        fresh_ref = None
    else:
        fresh_ref, rest = rest[0], rest[1:]
    cross_ref, bracket_ref, forward_x, forward_y, inverse_x, sems = rest[:6]
    slow_ref, returned_ref, even, odd = rest[6:10]
    pairs = [
        (forward_y_hbm, forward_y),
        (forward_x_hbm, forward_x),
        (inverse_x_hbm, inverse_x),
        (bracket_hbm.at[depth], bracket_ref),
    ]
    copies = [
        pltpu.make_async_copy(source, target, sems.at[index])
        for index, (source, target) in enumerate(pairs)
    ]
    for copy in copies:
        copy.start()
    scalars = scalars_of(held_ref, depth)
    quarter = q0.shape[1]
    for spot, value in zip(spots(), (q0, q1, q2, q3)):
        slow_ref[pl.ds(pl.multiple_of(spot * quarter, quarter), quarter), :] = value[depth]
    march(
        lambda plane: wave_ref[plane],
        (1, 1, 1, 1),
        (forward_x, forward_y, inverse_x),
        scalars,
        rest[10:],
        returned_ref,
        ready=tuple([copy.wait] for copy in copies[:3]),
    )
    copies[3].wait()
    tile = cross_ref.shape[2]

    def put_wave(block, here, within, plane, values):
        fresh_ref[plane, here, :] = values

    blend(
        returned_ref,
        lambda block, here, within: slow_ref[here, :],
        bracket_ref,
        inverse_y,
        scalars,
        (even, odd),
        None if last else put_wave,
        lambda block, side, values: put_tiles(
            cross_ref, block * (BLEND_ROWS // tile), side, values
        ),
        None,
    )


IMAGE_ROWS = 8


def lag_kernel(lag_ref, weight_ref):
    bins, pair, lags = lag_ref.shape
    height = bins * pair * IMAGE_ROWS
    table = jnp.broadcast_to(
        lag_ref[...].reshape(bins * pair, 1, lags), (bins * pair, IMAGE_ROWS, lags)
    ).reshape(height, lags)
    place = lax.broadcasted_iota(jnp.int32, (height, lags), 0) % IMAGE_ROWS
    for row in range(IMAGE_ROWS):
        weight_ref[:, row * lags : (row + 1) * lags] = jnp.where(place == row, table, 0.0).astype(
            bf16
        )


def image_kernel(*refs, scale, depth, aliased):
    cross_ref, weight_ref = refs[:2]
    out_hbm, made_ref, sems = refs[2 + aliased :]
    bins, pair, tile, cols = cross_ref.shape
    lags = made_ref.shape[2]
    copies = []
    for group in range(tile // IMAGE_ROWS):
        rows = cross_ref[:, :, group * IMAGE_ROWS : (group + 1) * IMAGE_ROWS, :].astype(f32)
        left = rows.reshape(bins * pair * IMAGE_ROWS, cols).T.astype(bf16)
        for row in range(IMAGE_ROWS):
            place = group * IMAGE_ROWS + row
            made_ref[place] = dot(left, weight_ref[:, row * lags : (row + 1) * lags]) * scale
            copies.append(
                pltpu.make_async_copy(
                    made_ref.at[place], out_hbm.at[depth, place], sems.at[place]
                )
            )
            copies[-1].start()
    for copy in copies:
        copy.wait()


def pin(value):
    return pltpu.with_memory_space_constraint(value, pltpu.HBM)


def shards(
    source_field,
    receiver_field,
    slowness_slabs,
    slab_map,
    reference_gaps,
    reference_index,
    frequency_bins,
    shot_corner,
    *,
    ranks,
):
    rows, cols = source_field.shape[2:]
    depths = slab_map.shape[0]
    slab_count = slowness_slabs.shape[0]
    quarter = rows // 4
    tile = rows // ranks
    bins = frequency_bins.shape[0]
    slab_shape = slowness_slabs.shape[1:]
    forward_x, inverse_x = real_table(rows)
    forward_x = forward_x.T
    forward_y, inverse_y = real_table(cols)
    inverse_y = inverse_y.T

    hbm = pl.BlockSpec(memory_space=pltpu.HBM)
    vmem = pl.BlockSpec(memory_space=VMEM)
    dma = pltpu.SemaphoreType.DMA

    keep, send = pl.pallas_call(
        window_kernel,
        in_specs=[hbm] * 3,
        out_specs=[vmem] * 2,
        out_shape=[jax.ShapeDtypeStruct((2, depths, quarter, cols), bf16)] * 2,
        scratch_shapes=[
            SMEM(slab_map.shape, jnp.int32),
            SMEM(shot_corner.shape, jnp.int32),
            VMEM((1,) + slab_shape, bf16),
            dma((3,)),
        ],
        compiler_params=pltpu.CompilerParams(vmem_limit_bytes=16 << 20),
        name="window",
    )(pin(slab_map), pin(shot_corner), pin(slowness_slabs))

    def swap(value, bit, odd_bit=None):
        odd_bit = bit if odd_bit is None else odd_bit
        return lax.ppermute(
            value, "freq", [(i, i ^ (odd_bit if i & 1 else bit)) for i in range(ranks)]
        )

    held = keep + swap(send, 1)
    quarters = held[0] + swap(held[1], 2)
    bits = [1 << k for k in range(2, ranks.bit_length() - 1)]
    hops = list(zip(bits, bits[::-1]))
    for hop in hops[:-1]:
        quarters = quarters + swap(quarters, *hop)
    early_bins, quarters = lax.optimization_barrier((frequency_bins, quarters))

    march_scratch = [
        VMEM((4, rows, cols), bf16),
        VMEM((4, rows, cols), f32),
        VMEM((3, rows, cols), f32),
        VMEM((3, rows, cols), f32),
        VMEM((3, 4, rows, cols), bf16),
    ]
    flops = 2 * 4 * (1 + 3) * rows * rows * cols
    returned, bracket, kept_inverse, held_scalars = pl.pallas_call(
        first_kernel,
        in_specs=[hbm] * 9,
        out_specs=[vmem] * 4,
        out_shape=[
            jax.ShapeDtypeStruct((3, 4, rows, cols), bf16),
            jax.ShapeDtypeStruct((rows, cols), jnp.int32),
            jax.ShapeDtypeStruct((cols, cols), bf16),
            jax.ShapeDtypeStruct((8 * pl.cdiv(1 + 3 * depths, 8), cols), f32),
        ],
        scratch_shapes=[
            SMEM(frequency_bins.shape, jnp.int32),
            SMEM(reference_gaps.shape, f32),
            VMEM((4, rows, cols), bf16),
            VMEM((rows, rows), bf16),
            VMEM((cols, cols), bf16),
            VMEM((rows, rows), bf16),
            dma((9,)),
        ]
        + march_scratch,
        compiler_params=pltpu.CompilerParams(vmem_limit_bytes=28 << 20),
        cost_estimate=pl.CostEstimate(flops=flops, bytes_accessed=8 << 20, transcendentals=0),
        name="first",
    )(
        *[
            pin(value)
            for value in (
                early_bins,
                reference_gaps,
                source_field,
                receiver_field,
                forward_x,
                forward_y,
                inverse_x,
                reference_index,
                inverse_y,
            )
        ]
    )

    if hops:
        quarters = quarters + swap(quarters, *hops[-1])
    quarters, returned = lax.optimization_barrier((quarters, returned))

    across = swap(quarters, 1)
    beside = swap(quarters, 2)

    blend_scratch = [VMEM((12, BLEND_ROWS, cols), f32)] * 2
    wave_shape = jax.ShapeDtypeStruct((4, rows, cols), bf16)
    cross_shape = jax.ShapeDtypeStruct((ranks, 2, tile, cols), bf16)
    near_wave, near_cross = pl.pallas_call(
        near_kernel,
        in_specs=[vmem] * 6,
        out_specs=[vmem] * 2,
        out_shape=[
            jax.ShapeDtypeStruct((2, 4, quarter, cols), bf16),
            jax.ShapeDtypeStruct((ranks // 2, 2, tile, cols), bf16),
        ],
        scratch_shapes=blend_scratch,
        compiler_params=pltpu.CompilerParams(vmem_limit_bytes=16 << 20),
        cost_estimate=pl.CostEstimate(
            flops=flops // 4, bytes_accessed=1 << 20, transcendentals=0
        ),
        name="near",
    )(held_scalars, returned, quarters, across, bracket, kept_inverse)
    beside, near_wave, near_cross = lax.optimization_barrier((beside, near_wave, near_cross))
    corner_ways = swap(beside, 1)
    wave, cross = pl.pallas_call(
        far_kernel,
        in_specs=[vmem] * 8,
        out_specs=[vmem] * 2,
        out_shape=[wave_shape, cross_shape],
        scratch_shapes=blend_scratch,
        compiler_params=pltpu.CompilerParams(vmem_limit_bytes=20 << 20),
        cost_estimate=pl.CostEstimate(
            flops=flops // 4, bytes_accessed=1 << 20, transcendentals=0
        ),
        name="far",
    )(
        held_scalars,
        returned,
        beside,
        corner_ways,
        bracket,
        kept_inverse,
        near_wave,
        near_cross,
    )
    crosses = [cross]
    for depth in range(1, depths):
        last = depth == depths - 1
        got = pl.pallas_call(
            functools.partial(later_kernel, depth=depth, last=last),
            in_specs=[vmem] * 6 + [hbm] * 4 + [vmem],
            out_specs=[vmem] * (2 - last),
            out_shape=[wave_shape] * (1 - last) + [cross_shape],
            scratch_shapes=[
                VMEM((rows, cols), jnp.int32),
                VMEM((rows, rows), bf16),
                VMEM((cols, cols), bf16),
                VMEM((rows, rows), bf16),
                dma((4,)),
                VMEM((rows, cols), bf16),
                VMEM((3, 4, rows, cols), bf16),
            ]
            + blend_scratch
            + march_scratch,
            compiler_params=pltpu.CompilerParams(vmem_limit_bytes=32 << 20),
            cost_estimate=pl.CostEstimate(
                flops=2 * flops, bytes_accessed=8 << 20, transcendentals=0
            ),
            name="later",
        )(
            held_scalars,
            wave,
            quarters,
            beside,
            across,
            corner_ways,
            pin(reference_index),
            pin(forward_x),
            pin(forward_y),
            pin(inverse_x),
            kept_inverse,
        )
        if not last:
            wave = got[0]
        crosses.append(got[-1])

    offsets = jnp.arange(LAGS, dtype=jnp.int32) - LAGS // 2
    cycles = jnp.mod(frequency_bins[:, None] * offsets[None, :], period_bins).astype(f32)
    angles = cycles * (2.0 * math.pi / period_bins)
    lag_weights = jnp.stack([jnp.cos(angles), jnp.sin(angles)], axis=1).astype(bf16)

    scale = bins ** (-0.5)
    arrivals = [
        lax.all_to_all(cross, "freq", split_axis=0, concat_axis=0, tiled=True) for cross in crosses
    ]
    if tile % (2 * IMAGE_ROWS):
        summed = jnp.einsum(
            "dwcab,wcl->dabl", jnp.stack(arrivals), lag_weights, preferred_element_type=f32
        )
        return summed * scale
    height = bins * 2 * IMAGE_ROWS
    weights = pl.pallas_call(
        lag_kernel,
        in_specs=[vmem],
        out_specs=vmem,
        out_shape=jax.ShapeDtypeStruct((height, IMAGE_ROWS * LAGS), bf16),
        compiler_params=pltpu.CompilerParams(vmem_limit_bytes=16 << 20),
        name="lag",
    )(lag_weights.astype(f32))
    image = None
    for depth, arrived in enumerate(arrivals):
        aliased = image is not None
        image = pl.pallas_call(
            functools.partial(image_kernel, scale=scale, depth=depth, aliased=aliased),
            in_specs=[vmem, vmem] + [hbm] * aliased,
            out_specs=hbm,
            out_shape=jax.ShapeDtypeStruct((depths, tile, cols, LAGS), f32),
            scratch_shapes=[VMEM((tile, cols, LAGS), f32), dma((tile,))],
            input_output_aliases={2: 0} if aliased else {},
            compiler_params=pltpu.CompilerParams(vmem_limit_bytes=28 << 20),
            name="image",
        )(arrived, weights, *([image] if aliased else []))
    return image


def solution(mesh):
    placed = (
        P("grp", "freq", None, None),
        P("grp", "freq", None, None),
        P(("grp", "freq"), None, None),
        P("grp"),
        P("grp", None),
        P("grp", None, None),
        P(),
        P("grp"),
    )
    return jax.shard_map(
        functools.partial(shards, ranks=mesh.shape["freq"]),
        mesh=mesh,
        in_specs=placed,
        out_specs=P("grp", "freq", None, None),
        check_vma=False,
    )
```

```python
import functools
import math

import jax
import jax.numpy as jnp
import numpy as np
from jax import lax
from jax.experimental import pallas as pl
from jax.experimental.pallas import tpu as pltpu
from jax.sharding import PartitionSpec as P

LAGS = 256

cell_width = 0.0125
layer_thick = 0.0125
bin_hertz = 0.5
period_bins = 500
slow_base = 0.3

VMEM = pltpu.VMEM
SMEM = pltpu.SMEM
f32 = jnp.float32
bf16 = jnp.bfloat16


def real_table(length):
    half = length // 2
    steps = np.arange(length, dtype=np.int64)
    wave = np.concatenate([np.arange(half), [half], np.arange(1, half)])
    phases = np.mod(steps[:, None] * wave[None, :], length).astype(np.float32)
    angles = phases * np.float32(2.0 * math.pi / length)
    scale = np.float32(1.0 / math.sqrt(length))
    is_cos = np.arange(length) <= half
    table = np.where(is_cos[None, :], np.cos(angles), np.sin(angles)) * scale
    twice = np.where((wave == 0) | (wave == half), 1.0, 2.0)
    forward = jnp.asarray(table.astype(np.float32)).astype(bf16)
    inverse = (forward.astype(f32) * jnp.asarray(twice[None, :], f32)).astype(bf16)
    return forward, inverse


def sin_cos(angle):
    turns = jnp.floor(angle * (2.0 / math.pi) + 0.5)
    rest = angle - turns * 1.5707397460937500
    rest = rest - turns * 5.6580702948965924e-05
    quadrant = turns.astype(jnp.int32)
    square = rest * rest
    sine = rest + rest * square * (
        -1.6666654611e-1 + square * (8.3321608736e-3 - square * 1.9515295891e-4)
    )
    cosine = (
        1.0
        - 0.5 * square
        + square
        * square
        * (4.166664568298827e-2 + square * (-1.388731625493765e-3 + square * 2.443315711809948e-5))
    )
    odd = (quadrant & 1) == 1
    out_sin = jnp.where(odd, cosine, sine)
    out_cos = jnp.where(odd, sine, cosine)
    out_sin = jnp.where((quadrant & 2) == 2, -out_sin, out_sin)
    out_cos = jnp.where(((quadrant + 1) & 2) == 2, -out_cos, out_cos)
    return out_sin, out_cos


def references_of(gaps_ref, depth):
    first = slow_base + gaps_ref[depth, 0]
    second = first + gaps_ref[depth, 1]
    third = second + gaps_ref[depth, 2]
    return first, second, third


def scalars_of(held_ref, depth):
    rows = [held_ref[row : row + 1] for row in (0, *range(1 + 3 * depth, 4 + 3 * depth))]
    return rows[0], tuple(rows[1:])


def angular_of(bins_ref):
    return bins_ref[lax.axis_index("freq")].astype(f32) * (2.0 * math.pi * bin_hertz)


def phase_block(reach, base_turn, squares):
    radicand = reach - squares
    root = jnp.sqrt(jnp.abs(radicand)) * layer_thick
    travelling = radicand > 0.0
    fading = jnp.where(travelling, 1.0, jnp.exp(-root))
    sine, cosine = sin_cos(jnp.where(travelling, root, 0.0) - base_turn)
    return fading * cosine, fading * sine


def make_phases(cos_ref, sin_ref, angular, reference):
    rows, cols = cos_ref.shape
    half = rows // 2
    reach = (angular * reference) * (angular * reference)
    base_turn = angular * layer_thick * reference
    step_x = 2.0 * math.pi / (rows * cell_width)
    step_y = 2.0 * math.pi / (cols * cell_width)
    lane = lax.broadcasted_iota(jnp.int32, (8, cols), 1)
    wave_y = jnp.where(lane <= cols // 2, lane, lane - cols // 2).astype(f32) * step_y
    square_y = wave_y * wave_y
    tall = 64

    def body(block, carry):
        start = pl.multiple_of(block * tall, tall)
        row = lax.broadcasted_iota(jnp.int32, (tall, cols), 0) + start
        wave_x = row.astype(f32) * step_x
        cosine, sine = phase_block(
            reach, base_turn, wave_x * wave_x + jnp.concatenate([square_y] * (tall // 8), axis=0)
        )
        cos_ref[pl.ds(start, tall), :] = cosine
        sin_ref[pl.ds(start, tall), :] = sine
        cos_ref[pl.ds(half + start, tall), :] = cosine
        sin_ref[pl.ds(half + start, tall), :] = sine
        return carry

    lax.fori_loop(0, half // tall, body, 0)
    edge = (half * step_x) ** 2
    cosine, sine = phase_block(reach, base_turn, edge + square_y)
    top = lax.broadcasted_iota(jnp.int32, (8, cols), 0) == 0
    cos_ref[half : half + 8, :] = jnp.where(top, cosine, cos_ref[half : half + 8, :])
    sin_ref[half : half + 8, :] = jnp.where(top, sine, sin_ref[half : half + 8, :])


def dot(left, right):
    return jnp.dot(left, right, preferred_element_type=f32)


def march_out(fill_half, forward_x, scalars, half_ref, spectrum, ready=((), ())):
    angular, references = scalars
    spec_ref, cos_ref, sin_ref = spectrum
    for j in range(3):
        make_phases(cos_ref.at[j], sin_ref.at[j], angular, references[j])
    for wait in ready[0]:
        wait()
    for plane in range(4):
        fill_half(plane)
    for wait in ready[1]:
        wait()
    for plane in range(4):
        spec_ref[plane] = dot(forward_x[...], half_ref[plane])


def march_back(spectrum, inverse_x, shift_ref, out_ref, ready=()):
    spec_ref, cos_ref, sin_ref = spectrum
    for j in range(3):
        for field in range(2):
            real, imag = spec_ref[2 * field], spec_ref[2 * field + 1]
            cosine, sine = cos_ref[j], sin_ref[j]
            shift_ref[j, 2 * field] = (cosine * real - sine * imag).astype(bf16)
            shift_ref[j, 2 * field + 1] = (cosine * imag + sine * real).astype(bf16)
        if j == 0:
            for wait in ready:
                wait()
        for plane in range(4):
            out_ref[j, plane] = dot(inverse_x[...], shift_ref[j, plane]).astype(bf16)


def blend(returned_ref, slow_ref, bracket_ref, inverse_y, scalars, parts, put_wave, put_cross, starts):
    tall, cols = slow_ref.shape[1:]
    chunk = 16
    angular, (low, mid, high) = scalars
    slope_low = 1.0 / (mid - low)
    slope_high = 1.0 / (high - mid)
    def first_row(block):
        return pl.multiple_of(starts[block], tall)

    def fill(part_ref, block):
        left = returned_ref[:, :, pl.ds(first_row(block), tall), :].reshape(12 * tall, cols)
        part_ref[...] = dot(left, inverse_y[...]).reshape(12, tall, cols)

    def mix(part_ref, block):
        start = first_row(block)
        crossed = []
        for piece in range(tall // chunk):
            within = slice(piece * chunk, (piece + 1) * chunk)
            here = pl.ds(start + piece * chunk, chunk)
            slow = slow_ref[block, within].astype(f32)
            lower = bracket_ref[here, :] == 0
            weight = jnp.where(lower, (slow - low) * slope_low, (slow - mid) * slope_high)
            weight = jnp.minimum(jnp.maximum(weight, 0.0), 1.0)
            sine, cosine = sin_cos(slow * (angular * layer_thick))
            halves = []
            for plane in range(4):
                first, second, third = [part_ref[4 * j + plane, within] for j in range(3)]
                bottom = jnp.where(lower, first, second)
                top = jnp.where(lower, second, third)
                halves.append(bottom + weight * (top - bottom))
            fresh = []
            for field in range(2):
                real, imag = halves[2 * field], halves[2 * field + 1]
                fresh.append((cosine * real - sine * imag).astype(bf16))
                fresh.append((cosine * imag + sine * real).astype(bf16))
            if put_wave is not None:
                for plane in range(4):
                    put_wave(block, within, plane, fresh[plane])
            s_real, s_imag, r_real, r_imag = [value.astype(f32) for value in fresh]
            crossed.append(
                (
                    (s_real * r_real - s_imag * r_imag).astype(bf16),
                    (s_real * r_imag + s_imag * r_real).astype(bf16),
                )
            )
        for side in range(2):
            put_cross(block, side, jnp.concatenate([pair[side] for pair in crossed], axis=0))

    even, odd = parts
    fill(even, 0)
    for block in range(len(starts)):
        here, other = (even, odd) if block % 2 == 0 else (odd, even)
        if block + 1 < len(starts):
            fill(other, block + 1)
        mix(here, block)


def put_tiles(cross_ref, first, side, values):
    tile = cross_ref.shape[2]
    for part in range(values.shape[0] // tile):
        cross_ref[first + part, side] = values[part * tile : (part + 1) * tile]


PIECES = 4


def piece_starts(piece):
    rank = lax.axis_index("freq")
    core, place = rank % 2, (rank // 2) % PIECES
    return [
        [(side * PIECES + (place ^ step)) * piece for step in range(PIECES)]
        for side in (core, 1 - core)
    ]


def window_kernel(
    map_hbm, corner_hbm, slab_hbm, keep_ref, send_ref, map_ref, corner_ref, slab_ref, sems
):
    depths, piece, cols = keep_ref.shape[1:]
    slab_count = slab_hbm.shape[0]
    tall, wide = slab_hbm.shape[1:]
    copies = [
        pltpu.make_async_copy(map_hbm, map_ref, sems.at[0]),
        pltpu.make_async_copy(corner_hbm, corner_ref, sems.at[1]),
    ]
    for copy in copies:
        copy.start()
    if slab_count == 1:
        whole = pltpu.make_async_copy(slab_hbm.at[0], slab_ref.at[0], sems.at[2])
        whole.start()
    for copy in copies:
        copy.wait()
    if slab_count == 1:
        whole.wait()
    rank = lax.axis_index("freq")
    rows = 2 * PIECES * piece
    first_row = jnp.minimum((corner_ref[0] // 16) * 16, tall - rows - 16)
    first_col = jnp.minimum((corner_ref[1] // 128) * 128, wide - cols - 128)
    above = corner_ref[0] - first_row
    before = corner_ref[1] - first_col
    reach = piece + 16
    span = cols + 128
    for depth in range(depths):
        slab = map_ref[depth]
        mine = slab // slab_count == rank

        @pl.when(mine)
        def _():
            if slab_count == 1:
                here = slab_ref.at[0]
            else:
                here = slab_ref.at[0]
                copy = pltpu.make_async_copy(
                    slab_hbm.at[lax.rem(slab, slab_count)], here, sems.at[2]
                )
                copy.start()
                copy.wait()
            for target, starts in zip((keep_ref, send_ref), piece_starts(piece)):
                for step, start in enumerate(starts):
                    block = here[
                        pl.ds(pl.multiple_of(first_row + start, 16), reach),
                        pl.ds(pl.multiple_of(first_col, 128), span),
                    ].astype(f32)
                    block = pltpu.roll(block, lax.rem(span - before, span), 1)[:, :cols]
                    block = pltpu.roll(block, lax.rem(reach - above, reach), 0)[:piece]
                    target[step, depth] = block.astype(bf16)

        @pl.when(jnp.logical_not(mine))
        def _():
            for target in (keep_ref, send_ref):
                target[:, depth] = jnp.zeros((PIECES, piece, cols), bf16)


def fetch(pairs, sems):
    copies = [
        pltpu.make_async_copy(source, target, sems.at[index])
        for index, (source, target) in enumerate(pairs)
    ]
    for copy in copies:
        copy.start()
    return [copy.wait for copy in copies]


def out_kernel(
    bins_hbm,
    gaps_hbm,
    source_hbm,
    receiver_hbm,
    forward_x_hbm,
    forward_y_hbm,
    spec_ref,
    cos_ref,
    sin_ref,
    held_ref,
    bins_ref,
    gaps_ref,
    wave_ref,
    forward_x,
    forward_y,
    half_ref,
    sems,
):
    waits = fetch(
        [
            (bins_hbm, bins_ref),
            (gaps_hbm, gaps_ref),
            (forward_y_hbm, forward_y),
            (source_hbm.at[:, 0], wave_ref.at[0:2]),
            (receiver_hbm.at[:, 0], wave_ref.at[2:4]),
            (forward_x_hbm, forward_x),
        ],
        sems,
    )
    waits[0]()
    waits[1]()
    angular = angular_of(bins_ref)
    held_ref[0:1] = jnp.full((1, held_ref.shape[1]), angular, f32)
    for depth in range(gaps_ref.shape[0]):
        for j, reference in enumerate(references_of(gaps_ref, depth)):
            row = 1 + 3 * depth + j
            held_ref[row : row + 1] = jnp.full((1, held_ref.shape[1]), reference, f32)

    def fill_half(plane):
        half = dot(wave_ref[plane], forward_y[...])
        half_ref[plane] = (half if plane < 3 else -half).astype(bf16)

    march_out(
        fill_half,
        forward_x,
        (angular, references_of(gaps_ref, 0)),
        half_ref,
        (spec_ref, cos_ref, sin_ref),
        ready=(waits[2:5], waits[5:]),
    )


def back_kernel(
    spec_ref,
    cos_ref,
    sin_ref,
    inverse_x_hbm,
    bracket_hbm,
    inverse_y_hbm,
    out_ref,
    bracket_ref,
    inverse_y,
    inverse_x,
    shift_ref,
    sems,
):
    waits = fetch(
        [
            (inverse_x_hbm, inverse_x),
            (bracket_hbm.at[0], bracket_ref),
            (inverse_y_hbm, inverse_y),
        ],
        sems,
    )
    march_back((spec_ref, cos_ref, sin_ref), inverse_x, shift_ref, out_ref, waits[:1])
    for wait in waits[1:]:
        wait()


def mix_kernel(*refs, depth, far, last):
    held_ref, returned_ref, slow_ref, bracket_ref, inverse_y = refs[:5]
    rest = refs[5:]
    if far:
        near_cross, rest = rest[0], rest[1:]
    if not last:
        wave_ref, rest = rest[0], rest[1:]
    cross_ref, even, odd = rest
    piece = slow_ref.shape[2]
    tile = cross_ref.shape[2]
    tiles = piece // tile
    near_starts, far_starts = piece_starts(piece)
    starts = far_starts if far else near_starts
    if far:
        for step, start in enumerate(near_starts):
            cross_ref[pl.ds(start // tile, tiles)] = near_cross[step * tiles : (step + 1) * tiles]

    def put_wave(block, within, plane, values):
        wave_ref[plane, block * piece + within.start : block * piece + within.stop] = values

    def put_cross(block, side, values):
        put_tiles(cross_ref, starts[block] // tile if far else block * tiles, side, values)

    blend(
        returned_ref,
        slow_ref.at[:, depth],
        bracket_ref,
        inverse_y,
        scalars_of(held_ref, depth),
        (even, odd),
        None if last else put_wave,
        put_cross,
        starts,
    )


def march_kernel(
    held_ref,
    near_wave,
    far_wave,
    bracket_hbm,
    forward_x_hbm,
    forward_y_hbm,
    inverse_x_hbm,
    out_ref,
    bracket_ref,
    forward_x,
    forward_y,
    inverse_x,
    sems,
    half_ref,
    shift_ref,
    *spectrum,
    depth,
):
    waits = fetch(
        [
            (forward_y_hbm, forward_y),
            (forward_x_hbm, forward_x),
            (inverse_x_hbm, inverse_x),
            (bracket_hbm.at[depth], bracket_ref),
        ],
        sems,
    )
    piece = near_wave.shape[1] // PIECES

    def fill_half(plane):
        for starts, wave_ref in zip(piece_starts(piece), (near_wave, far_wave)):
            half = dot(wave_ref[plane], forward_y[...]).astype(bf16)
            for step, start in enumerate(starts):
                here = pl.ds(pl.multiple_of(start, piece), piece)
                half_ref[plane, here, :] = half[step * piece : (step + 1) * piece]

    march_out(
        fill_half,
        forward_x,
        scalars_of(held_ref, depth),
        half_ref,
        spectrum,
        ready=(waits[:1], waits[1:2]),
    )
    march_back(spectrum, inverse_x, shift_ref, out_ref, waits[2:3])
    waits[3]()


IMAGE_ROWS = 8


def lag_kernel(lag_ref, weight_ref):
    bins, pair, lags = lag_ref.shape
    height = bins * pair * IMAGE_ROWS
    table = jnp.broadcast_to(
        lag_ref[...].reshape(bins * pair, 1, lags), (bins * pair, IMAGE_ROWS, lags)
    ).reshape(height, lags)
    place = lax.broadcasted_iota(jnp.int32, (height, lags), 0) % IMAGE_ROWS
    for row in range(IMAGE_ROWS):
        weight_ref[:, row * lags : (row + 1) * lags] = jnp.where(place == row, table, 0.0).astype(
            bf16
        )


def image_kernel(*refs, scale, depth, aliased):
    cross_ref, weight_ref = refs[:2]
    out_hbm, made_ref, sems = refs[2 + aliased :]
    bins, pair, tile, cols = cross_ref.shape
    lags = made_ref.shape[2]
    copies = []
    for group in range(tile // IMAGE_ROWS):
        rows = cross_ref[:, :, group * IMAGE_ROWS : (group + 1) * IMAGE_ROWS, :].astype(f32)
        left = rows.reshape(bins * pair * IMAGE_ROWS, cols).T.astype(bf16)
        for row in range(IMAGE_ROWS):
            place = group * IMAGE_ROWS + row
            made_ref[place] = dot(left, weight_ref[:, row * lags : (row + 1) * lags]) * scale
            copies.append(
                pltpu.make_async_copy(
                    made_ref.at[place], out_hbm.at[depth, place], sems.at[place]
                )
            )
            copies[-1].start()
    for copy in copies:
        copy.wait()


def pin(value):
    return pltpu.with_memory_space_constraint(value, pltpu.HBM)


def shards(
    source_field,
    receiver_field,
    slowness_slabs,
    slab_map,
    reference_gaps,
    reference_index,
    frequency_bins,
    shot_corner,
    *,
    ranks,
):
    rows, cols = source_field.shape[2:]
    depths = slab_map.shape[0]
    slab_count = slowness_slabs.shape[0]
    half = rows // 2
    piece = half // PIECES
    tile = rows // ranks
    bins = frequency_bins.shape[0]
    slab_shape = slowness_slabs.shape[1:]
    forward_x, inverse_x = real_table(rows)
    forward_x = forward_x.T
    forward_y, inverse_y = real_table(cols)
    inverse_y = inverse_y.T

    hbm = pl.BlockSpec(memory_space=pltpu.HBM)
    vmem = pl.BlockSpec(memory_space=VMEM)
    dma = pltpu.SemaphoreType.DMA

    keep, send = pl.pallas_call(
        window_kernel,
        in_specs=[hbm] * 3,
        out_specs=[vmem] * 2,
        out_shape=[jax.ShapeDtypeStruct((PIECES, depths, piece, cols), bf16)] * 2,
        scratch_shapes=[
            SMEM(slab_map.shape, jnp.int32),
            SMEM(shot_corner.shape, jnp.int32),
            VMEM((1,) + slab_shape, bf16),
            dma((3,)),
        ],
        compiler_params=pltpu.CompilerParams(vmem_limit_bytes=16 << 20),
        name="window",
    )(pin(slab_map), pin(shot_corner), pin(slowness_slabs))

    def swap(value, bit):
        return lax.ppermute(value, "freq", [(i, i ^ bit) for i in range(ranks)])

    held = keep + swap(send, 1)
    early_bins, held = lax.optimization_barrier((frequency_bins, held))
    spectrum_shapes = [
        jax.ShapeDtypeStruct((4, rows, cols), f32),
        jax.ShapeDtypeStruct((3, rows, cols), f32),
        jax.ShapeDtypeStruct((3, rows, cols), f32),
    ]
    returned_shape = jax.ShapeDtypeStruct((3, 4, rows, cols), bf16)
    flops = 2 * 4 * (1 + 3) * rows * rows * cols
    *spectrum, held_scalars = pl.pallas_call(
        out_kernel,
        in_specs=[hbm] * 6,
        out_specs=[vmem] * 4,
        out_shape=spectrum_shapes
        + [jax.ShapeDtypeStruct((8 * pl.cdiv(1 + 3 * depths, 8), cols), f32)],
        scratch_shapes=[
            SMEM(frequency_bins.shape, jnp.int32),
            SMEM(reference_gaps.shape, f32),
            VMEM((4, rows, cols), bf16),
            VMEM((rows, rows), bf16),
            VMEM((cols, cols), bf16),
            VMEM((4, rows, cols), bf16),
            dma((6,)),
        ],
        compiler_params=pltpu.CompilerParams(vmem_limit_bytes=20 << 20),
        cost_estimate=pl.CostEstimate(flops=flops // 2, bytes_accessed=4 << 20, transcendentals=0),
        name="out",
    )(
        *[
            pin(value)
            for value in (
                early_bins,
                reference_gaps,
                source_field,
                receiver_field,
                forward_x,
                forward_y,
            )
        ]
    )
    own = held[0] + sum(swap(held[step], 2 * step) for step in range(1, PIECES))
    own, spectrum = lax.optimization_barrier((own, spectrum))
    returned, bracket, kept_inverse = pl.pallas_call(
        back_kernel,
        in_specs=[vmem] * 3 + [hbm] * 3,
        out_specs=[vmem] * 3,
        out_shape=[
            returned_shape,
            jax.ShapeDtypeStruct((rows, cols), jnp.int32),
            jax.ShapeDtypeStruct((cols, cols), bf16),
        ],
        scratch_shapes=[
            VMEM((rows, rows), bf16),
            VMEM((3, 4, rows, cols), bf16),
            dma((3,)),
        ],
        compiler_params=pltpu.CompilerParams(vmem_limit_bytes=24 << 20),
        cost_estimate=pl.CostEstimate(flops=flops, bytes_accessed=4 << 20, transcendentals=0),
        name="back",
    )(*spectrum, pin(inverse_x), pin(reference_index), pin(inverse_y))
    bit = 2 * PIECES
    while bit < ranks:
        own = own + swap(own, bit)
        bit *= 2
    own, returned = lax.optimization_barrier((own, returned))
    near_slow = jnp.stack([own] + [swap(own, 2 * step) for step in range(1, PIECES)])
    far_slow = swap(near_slow, 1)

    blend_scratch = [VMEM((12, piece, cols), f32)] * 2
    wave_shape = jax.ShapeDtypeStruct((4, half, cols), bf16)

    def mix(depth, far, *operands):
        last = depth == depths - 1
        tiles = ranks if far else ranks // 2
        return pl.pallas_call(
            functools.partial(mix_kernel, depth=depth, far=far, last=last),
            in_specs=[vmem] * len(operands),
            out_specs=[vmem] * (2 - last),
            out_shape=[wave_shape] * (1 - last)
            + [jax.ShapeDtypeStruct((tiles, 2, tile, cols), bf16)],
            scratch_shapes=blend_scratch,
            compiler_params=pltpu.CompilerParams(vmem_limit_bytes=16 << 20),
            cost_estimate=pl.CostEstimate(
                flops=flops // 4, bytes_accessed=1 << 20, transcendentals=0
            ),
            name="far" if far else "near",
        )(*operands)

    *near_wave, near_cross = mix(0, False, held_scalars, returned, near_slow, bracket, kept_inverse)
    *far_wave, cross = mix(
        0, True, held_scalars, returned, far_slow, bracket, kept_inverse, near_cross
    )
    crosses = [cross]
    for depth in range(1, depths):
        returned, bracket = pl.pallas_call(
            functools.partial(march_kernel, depth=depth),
            in_specs=[vmem] * 3 + [hbm] * 4,
            out_specs=[vmem] * 2,
            out_shape=[returned_shape, jax.ShapeDtypeStruct((rows, cols), jnp.int32)],
            scratch_shapes=[
                VMEM((rows, rows), bf16),
                VMEM((cols, cols), bf16),
                VMEM((rows, rows), bf16),
                dma((4,)),
                VMEM((4, rows, cols), bf16),
                VMEM((3, 4, rows, cols), bf16),
                *[VMEM(shape.shape, f32) for shape in spectrum_shapes],
            ],
            compiler_params=pltpu.CompilerParams(vmem_limit_bytes=28 << 20),
            cost_estimate=pl.CostEstimate(
                flops=3 * flops // 2, bytes_accessed=8 << 20, transcendentals=0
            ),
            name="march",
        )(
            held_scalars,
            *near_wave,
            *far_wave,
            pin(reference_index),
            pin(forward_x),
            pin(forward_y),
            pin(inverse_x),
        )
        *near_wave, near_cross = mix(
            depth, False, held_scalars, returned, near_slow, bracket, kept_inverse
        )
        *far_wave, cross = mix(
            depth, True, held_scalars, returned, far_slow, bracket, kept_inverse, near_cross
        )
        crosses.append(cross)

    offsets = jnp.arange(LAGS, dtype=jnp.int32) - LAGS // 2
    cycles = jnp.mod(frequency_bins[:, None] * offsets[None, :], period_bins).astype(f32)
    angles = cycles * (2.0 * math.pi / period_bins)
    lag_weights = jnp.stack([jnp.cos(angles), jnp.sin(angles)], axis=1).astype(bf16)

    scale = bins ** (-0.5)
    arrivals = [
        lax.all_to_all(cross, "freq", split_axis=0, concat_axis=0, tiled=True) for cross in crosses
    ]
    if tile % (2 * IMAGE_ROWS):
        summed = jnp.einsum(
            "dwcab,wcl->dabl", jnp.stack(arrivals), lag_weights, preferred_element_type=f32
        )
        return summed * scale
    height = bins * 2 * IMAGE_ROWS
    weights = pl.pallas_call(
        lag_kernel,
        in_specs=[vmem],
        out_specs=vmem,
        out_shape=jax.ShapeDtypeStruct((height, IMAGE_ROWS * LAGS), bf16),
        compiler_params=pltpu.CompilerParams(vmem_limit_bytes=16 << 20),
        name="lag",
    )(lag_weights.astype(f32))
    image = None
    for depth, arrived in enumerate(arrivals):
        aliased = image is not None
        image = pl.pallas_call(
            functools.partial(image_kernel, scale=scale, depth=depth, aliased=aliased),
            in_specs=[vmem, vmem] + [hbm] * aliased,
            out_specs=hbm,
            out_shape=jax.ShapeDtypeStruct((depths, tile, cols, LAGS), f32),
            scratch_shapes=[VMEM((tile, cols, LAGS), f32), dma((tile,))],
            input_output_aliases={2: 0} if aliased else {},
            compiler_params=pltpu.CompilerParams(vmem_limit_bytes=28 << 20),
            name="image",
        )(arrived, weights, *([image] if aliased else []))
    return image


def solution(mesh):
    placed = (
        P("grp", "freq", None, None),
        P("grp", "freq", None, None),
        P(("grp", "freq"), None, None),
        P("grp"),
        P("grp", None),
        P("grp", None, None),
        P(),
        P("grp"),
    )
    return jax.shard_map(
        functools.partial(shards, ranks=mesh.shape["freq"]),
        mesh=mesh,
        in_specs=placed,
        out_specs=P("grp", "freq", None, None),
        check_vma=False,
    )
```

```python
import functools
import math

import jax
import jax.numpy as jnp
import numpy as np
from jax import lax
from jax.experimental import pallas as pl
from jax.experimental.pallas import tpu as pltpu
from jax.sharding import PartitionSpec as P

LAGS = 256

cell_width = 0.0125
layer_thick = 0.0125
bin_hertz = 0.5
period_bins = 500
slow_base = 0.3

VMEM = pltpu.VMEM
SMEM = pltpu.SMEM
f32 = jnp.float32
bf16 = jnp.bfloat16


def real_table(length):
    half = length // 2
    steps = np.arange(length, dtype=np.int64)
    wave = np.concatenate([np.arange(half), [half], np.arange(1, half)])
    phases = np.mod(steps[:, None] * wave[None, :], length).astype(np.float32)
    angles = phases * np.float32(2.0 * math.pi / length)
    scale = np.float32(1.0 / math.sqrt(length))
    is_cos = np.arange(length) <= half
    table = np.where(is_cos[None, :], np.cos(angles), np.sin(angles)) * scale
    twice = np.where((wave == 0) | (wave == half), 1.0, 2.0)
    forward = jnp.asarray(table.astype(np.float32)).astype(bf16)
    inverse = (forward.astype(f32) * jnp.asarray(twice[None, :], f32)).astype(bf16)
    return forward, inverse


def sin_cos(angle):
    turns = jnp.floor(angle * (2.0 / math.pi) + 0.5)
    rest = angle - turns * 1.5707397460937500
    rest = rest - turns * 5.6580702948965924e-05
    quadrant = turns.astype(jnp.int32)
    square = rest * rest
    sine = rest + rest * square * (
        -1.6666654611e-1 + square * (8.3321608736e-3 - square * 1.9515295891e-4)
    )
    cosine = (
        1.0
        - 0.5 * square
        + square
        * square
        * (4.166664568298827e-2 + square * (-1.388731625493765e-3 + square * 2.443315711809948e-5))
    )
    odd = (quadrant & 1) == 1
    out_sin = jnp.where(odd, cosine, sine)
    out_cos = jnp.where(odd, sine, cosine)
    out_sin = jnp.where((quadrant & 2) == 2, -out_sin, out_sin)
    out_cos = jnp.where(((quadrant + 1) & 2) == 2, -out_cos, out_cos)
    return out_sin, out_cos


def references_of(gaps_ref, depth):
    first = slow_base + gaps_ref[depth, 0]
    second = first + gaps_ref[depth, 1]
    third = second + gaps_ref[depth, 2]
    return first, second, third


def scalars_of(held_ref, depth):
    rows = [held_ref[row : row + 1] for row in (0, *range(1 + 3 * depth, 4 + 3 * depth))]
    return rows[0], tuple(rows[1:])


def angular_of(bins_ref):
    return bins_ref[lax.axis_index("freq")].astype(f32) * (2.0 * math.pi * bin_hertz)


def phase_block(reach, base_turn, squares):
    radicand = reach - squares
    root = jnp.sqrt(jnp.abs(radicand)) * layer_thick
    travelling = radicand > 0.0
    fading = jnp.where(travelling, 1.0, jnp.exp(-root))
    sine, cosine = sin_cos(jnp.where(travelling, root, 0.0) - base_turn)
    return fading * cosine, fading * sine


def make_phases(cos_ref, sin_ref, angular, reference):
    rows, cols = cos_ref.shape
    half = rows // 2
    reach = (angular * reference) * (angular * reference)
    base_turn = angular * layer_thick * reference
    step_x = 2.0 * math.pi / (rows * cell_width)
    step_y = 2.0 * math.pi / (cols * cell_width)
    lane = lax.broadcasted_iota(jnp.int32, (8, cols), 1)
    wave_y = jnp.where(lane <= cols // 2, lane, lane - cols // 2).astype(f32) * step_y
    square_y = wave_y * wave_y
    tall = 64

    def body(block, carry):
        start = pl.multiple_of(block * tall, tall)
        row = lax.broadcasted_iota(jnp.int32, (tall, cols), 0) + start
        wave_x = row.astype(f32) * step_x
        cosine, sine = phase_block(
            reach, base_turn, wave_x * wave_x + jnp.concatenate([square_y] * (tall // 8), axis=0)
        )
        cos_ref[pl.ds(start, tall), :] = cosine
        sin_ref[pl.ds(start, tall), :] = sine
        cos_ref[pl.ds(half + start, tall), :] = cosine
        sin_ref[pl.ds(half + start, tall), :] = sine
        return carry

    lax.fori_loop(0, half // tall, body, 0)
    edge = (half * step_x) ** 2
    cosine, sine = phase_block(reach, base_turn, edge + square_y)
    top = lax.broadcasted_iota(jnp.int32, (8, cols), 0) == 0
    cos_ref[half : half + 8, :] = jnp.where(top, cosine, cos_ref[half : half + 8, :])
    sin_ref[half : half + 8, :] = jnp.where(top, sine, sin_ref[half : half + 8, :])


def dot(left, right):
    return jnp.dot(left, right, preferred_element_type=f32)


def march_out(fill_half, forward_x, scalars, half_ref, spectrum, ready=((), ())):
    angular, references = scalars
    spec_ref, cos_ref, sin_ref = spectrum
    for j in range(3):
        make_phases(cos_ref.at[j], sin_ref.at[j], angular, references[j])
    for wait in ready[0]:
        wait()
    for plane in range(4):
        fill_half(plane)
    for wait in ready[1]:
        wait()
    for plane in range(4):
        spec_ref[plane] = dot(forward_x[...], half_ref[plane])


def march_back(spectrum, inverse_x, shift_ref, out_ref, ready=()):
    spec_ref, cos_ref, sin_ref = spectrum
    for j in range(3):
        for field in range(2):
            real, imag = spec_ref[2 * field], spec_ref[2 * field + 1]
            cosine, sine = cos_ref[j], sin_ref[j]
            shift_ref[j, 2 * field] = (cosine * real - sine * imag).astype(bf16)
            shift_ref[j, 2 * field + 1] = (cosine * imag + sine * real).astype(bf16)
        if j == 0:
            for wait in ready:
                wait()
        for plane in range(4):
            out_ref[j, plane] = dot(inverse_x[...], shift_ref[j, plane]).astype(bf16)


def blend(returned_ref, slow_ref, bracket_ref, inverse_y, scalars, parts, put_wave, put_cross, starts):
    tall, cols = slow_ref.shape[1:]
    chunk = 16
    angular, (low, mid, high) = scalars
    slope_low = 1.0 / (mid - low)
    slope_high = 1.0 / (high - mid)
    def first_row(block):
        return pl.multiple_of(starts[block], tall)

    def fill(part_ref, block):
        left = returned_ref[:, :, pl.ds(first_row(block), tall), :].reshape(12 * tall, cols)
        part_ref[...] = dot(left, inverse_y[...]).reshape(12, tall, cols)

    def mix(part_ref, block):
        start = first_row(block)
        crossed = []
        for piece in range(tall // chunk):
            within = slice(piece * chunk, (piece + 1) * chunk)
            here = pl.ds(start + piece * chunk, chunk)
            slow = slow_ref[block, within].astype(f32)
            lower = bracket_ref[here, :] == 0
            weight = jnp.where(lower, (slow - low) * slope_low, (slow - mid) * slope_high)
            weight = jnp.minimum(jnp.maximum(weight, 0.0), 1.0)
            sine, cosine = sin_cos(slow * (angular * layer_thick))
            halves = []
            for plane in range(4):
                first, second, third = [part_ref[4 * j + plane, within] for j in range(3)]
                bottom = jnp.where(lower, first, second)
                top = jnp.where(lower, second, third)
                halves.append(bottom + weight * (top - bottom))
            fresh = []
            for field in range(2):
                real, imag = halves[2 * field], halves[2 * field + 1]
                fresh.append((cosine * real - sine * imag).astype(bf16))
                fresh.append((cosine * imag + sine * real).astype(bf16))
            if put_wave is not None:
                for plane in range(4):
                    put_wave(block, within, plane, fresh[plane])
            s_real, s_imag, r_real, r_imag = [value.astype(f32) for value in fresh]
            crossed.append(
                (
                    (s_real * r_real - s_imag * r_imag).astype(bf16),
                    (s_real * r_imag + s_imag * r_real).astype(bf16),
                )
            )
        for side in range(2):
            put_cross(block, side, jnp.concatenate([pair[side] for pair in crossed], axis=0))

    even, odd = parts
    fill(even, 0)
    for block in range(len(starts)):
        here, other = (even, odd) if block % 2 == 0 else (odd, even)
        if block + 1 < len(starts):
            fill(other, block + 1)
        mix(here, block)


PIECES = 4


def piece_starts(piece):
    rank = lax.axis_index("freq")
    core, place = rank % 2, (rank // 2) % PIECES
    return [
        [(side * PIECES + (place ^ step)) * piece for step in range(PIECES)]
        for side in (core, 1 - core)
    ]


def window_kernel(
    map_hbm, corner_hbm, slab_hbm, keep_ref, send_ref, map_ref, corner_ref, slab_ref, sems
):
    depths, piece, cols = keep_ref.shape[1:]
    slab_count = slab_hbm.shape[0]
    tall, wide = slab_hbm.shape[1:]
    copies = [
        pltpu.make_async_copy(map_hbm, map_ref, sems.at[0]),
        pltpu.make_async_copy(corner_hbm, corner_ref, sems.at[1]),
    ]
    for copy in copies:
        copy.start()
    if slab_count == 1:
        whole = pltpu.make_async_copy(slab_hbm.at[0], slab_ref.at[0], sems.at[2])
        whole.start()
    for copy in copies:
        copy.wait()
    if slab_count == 1:
        whole.wait()
    rank = lax.axis_index("freq")
    rows = 2 * PIECES * piece
    first_row = jnp.minimum((corner_ref[0] // 16) * 16, tall - rows - 16)
    first_col = jnp.minimum((corner_ref[1] // 128) * 128, wide - cols - 128)
    above = corner_ref[0] - first_row
    before = corner_ref[1] - first_col
    reach = piece + 16
    span = cols + 128
    for depth in range(depths):
        slab = map_ref[depth]
        mine = slab // slab_count == rank

        @pl.when(mine)
        def _():
            if slab_count == 1:
                here = slab_ref.at[0]
            else:
                here = slab_ref.at[0]
                copy = pltpu.make_async_copy(
                    slab_hbm.at[lax.rem(slab, slab_count)], here, sems.at[2]
                )
                copy.start()
                copy.wait()
            for target, starts in zip((keep_ref, send_ref), piece_starts(piece)):
                for step, start in enumerate(starts):
                    block = here[
                        pl.ds(pl.multiple_of(first_row + start, 16), reach),
                        pl.ds(pl.multiple_of(first_col, 128), span),
                    ].astype(f32)
                    block = pltpu.roll(block, lax.rem(span - before, span), 1)[:, :cols]
                    block = pltpu.roll(block, lax.rem(reach - above, reach), 0)[:piece]
                    target[step, depth] = block.astype(bf16)

        @pl.when(jnp.logical_not(mine))
        def _():
            for target in (keep_ref, send_ref):
                target[:, depth] = jnp.zeros((PIECES, piece, cols), bf16)


def fetch(pairs, sems):
    copies = [
        pltpu.make_async_copy(source, target, sems.at[index])
        for index, (source, target) in enumerate(pairs)
    ]
    for copy in copies:
        copy.start()
    return [copy.wait for copy in copies]


def out_kernel(
    bins_hbm,
    gaps_hbm,
    source_hbm,
    receiver_hbm,
    forward_x_hbm,
    forward_y_hbm,
    spec_ref,
    cos_ref,
    sin_ref,
    held_ref,
    bins_ref,
    gaps_ref,
    wave_ref,
    forward_x,
    forward_y,
    half_ref,
    sems,
):
    waits = fetch(
        [
            (bins_hbm, bins_ref),
            (gaps_hbm, gaps_ref),
            (forward_y_hbm, forward_y),
            (source_hbm.at[:, 0], wave_ref.at[0:2]),
            (receiver_hbm.at[:, 0], wave_ref.at[2:4]),
            (forward_x_hbm, forward_x),
        ],
        sems,
    )
    waits[0]()
    waits[1]()
    angular = angular_of(bins_ref)
    held_ref[0:1] = jnp.full((1, held_ref.shape[1]), angular, f32)
    for depth in range(gaps_ref.shape[0]):
        for j, reference in enumerate(references_of(gaps_ref, depth)):
            row = 1 + 3 * depth + j
            held_ref[row : row + 1] = jnp.full((1, held_ref.shape[1]), reference, f32)

    def fill_half(plane):
        half = dot(wave_ref[plane], forward_y[...])
        half_ref[plane] = (half if plane < 3 else -half).astype(bf16)

    march_out(
        fill_half,
        forward_x,
        (angular, references_of(gaps_ref, 0)),
        half_ref,
        (spec_ref, cos_ref, sin_ref),
        ready=(waits[2:5], waits[5:]),
    )


def back_kernel(
    spec_ref,
    cos_ref,
    sin_ref,
    inverse_x_hbm,
    bracket_hbm,
    inverse_y_hbm,
    out_ref,
    bracket_ref,
    inverse_y,
    inverse_x,
    shift_ref,
    sems,
):
    waits = fetch(
        [
            (inverse_x_hbm, inverse_x),
            (bracket_hbm.at[0], bracket_ref),
            (inverse_y_hbm, inverse_y),
        ],
        sems,
    )
    march_back((spec_ref, cos_ref, sin_ref), inverse_x, shift_ref, out_ref, waits[:1])
    for wait in waits[1:]:
        wait()


def place_of(rank):
    here = lax.axis_index("freq")
    return (rank ^ here) % 2, (rank // 2) ^ (here // 2)


def mix_kernel(*refs, depth, far, last, paired):
    held_ref, returned_ref, slow_ref, bracket_ref, inverse_y = refs[:5]
    rest = refs[5:]
    if far:
        near_cross, rest = rest[0], rest[1:]
    if not last:
        wave_ref, rest = rest[0], rest[1:]
    cross_ref, even, odd = rest
    piece = slow_ref.shape[2]
    tile = cross_ref.shape[-2]
    tiles = piece // tile
    near_starts, far_starts = piece_starts(piece)
    starts = far_starts if far else near_starts
    if far:
        for step, start in enumerate(near_starts):
            if paired:
                for part in range(tiles):
                    cross_ref[place_of(start // tile + part)] = near_cross[step * tiles + part]
                continue
            cross_ref[pl.ds(start // tile, tiles)] = near_cross[step * tiles : (step + 1) * tiles]

    def put_wave(block, within, plane, values):
        wave_ref[plane, block * piece + within.start : block * piece + within.stop] = values

    def put_cross(block, side, values):
        for part in range(tiles):
            rank = starts[block] // tile + part if far else block * tiles + part
            place = place_of(rank) if far and paired else (rank,)
            cross_ref[*place, side] = values[part * tile : (part + 1) * tile]

    blend(
        returned_ref,
        slow_ref.at[:, depth],
        bracket_ref,
        inverse_y,
        scalars_of(held_ref, depth),
        (even, odd),
        None if last else put_wave,
        put_cross,
        starts,
    )


def march_kernel(
    held_ref,
    near_wave,
    far_wave,
    bracket_hbm,
    forward_x_hbm,
    forward_y_hbm,
    inverse_x_hbm,
    out_ref,
    bracket_ref,
    forward_x,
    forward_y,
    inverse_x,
    sems,
    half_ref,
    shift_ref,
    *spectrum,
    depth,
):
    waits = fetch(
        [
            (forward_y_hbm, forward_y),
            (forward_x_hbm, forward_x),
            (inverse_x_hbm, inverse_x),
            (bracket_hbm.at[depth], bracket_ref),
        ],
        sems,
    )
    piece = near_wave.shape[1] // PIECES

    def fill_half(plane):
        for starts, wave_ref in zip(piece_starts(piece), (near_wave, far_wave)):
            half = dot(wave_ref[plane], forward_y[...]).astype(bf16)
            for step, start in enumerate(starts):
                here = pl.ds(pl.multiple_of(start, piece), piece)
                half_ref[plane, here, :] = half[step * piece : (step + 1) * piece]

    march_out(
        fill_half,
        forward_x,
        scalars_of(held_ref, depth),
        half_ref,
        spectrum,
        ready=(waits[:1], waits[1:2]),
    )
    march_back(spectrum, inverse_x, shift_ref, out_ref, waits[2:3])
    waits[3]()


IMAGE_ROWS = 8


def lag_kernel(lag_ref, *weight_refs):
    bins, pair, lags = lag_ref.shape
    height = bins * pair * IMAGE_ROWS
    here = lax.axis_index("freq")
    for weight_ref, mask in zip(weight_refs, (0, here)):
        table = jnp.concatenate(
            [
                jnp.broadcast_to(lag_ref[spot ^ mask][:, None], (pair, IMAGE_ROWS, lags)).reshape(
                    pair * IMAGE_ROWS, lags
                )
                for spot in range(bins)
            ],
            axis=0,
        )
        place = lax.broadcasted_iota(jnp.int32, (height, lags), 0) % IMAGE_ROWS
        for row in range(IMAGE_ROWS):
            weight_ref[:, row * lags : (row + 1) * lags] = jnp.where(
                place == row, table, 0.0
            ).astype(bf16)


def image_kernel(*refs, scale, depth, aliased, count):
    cross_refs, weight_ref = refs[:count], refs[count]
    out_hbm, made_ref, sems = refs[count + 1 + aliased :]
    tile, cols, lags = made_ref.shape
    copies = []
    for group in range(tile // IMAGE_ROWS):
        rows = slice(group * IMAGE_ROWS, (group + 1) * IMAGE_ROWS)
        left = jnp.concatenate(
            [ref[..., rows, :].astype(f32).reshape(-1, cols) for ref in cross_refs], axis=0
        )
        left = left.T.astype(bf16)
        for row in range(IMAGE_ROWS):
            place = group * IMAGE_ROWS + row
            made_ref[place] = dot(left, weight_ref[:, row * lags : (row + 1) * lags]) * scale
            copies.append(
                pltpu.make_async_copy(
                    made_ref.at[place], out_hbm.at[depth, place], sems.at[place]
                )
            )
            copies[-1].start()
    for copy in copies:
        copy.wait()


def pin(value):
    return pltpu.with_memory_space_constraint(value, pltpu.HBM)


def shards(
    source_field,
    receiver_field,
    slowness_slabs,
    slab_map,
    reference_gaps,
    reference_index,
    frequency_bins,
    shot_corner,
    *,
    ranks,
):
    rows, cols = source_field.shape[2:]
    depths = slab_map.shape[0]
    slab_count = slowness_slabs.shape[0]
    half = rows // 2
    piece = half // PIECES
    tile = rows // ranks
    bins = frequency_bins.shape[0]
    slab_shape = slowness_slabs.shape[1:]
    forward_x, inverse_x = real_table(rows)
    forward_x = forward_x.T
    forward_y, inverse_y = real_table(cols)
    inverse_y = inverse_y.T

    hbm = pl.BlockSpec(memory_space=pltpu.HBM)
    vmem = pl.BlockSpec(memory_space=VMEM)
    dma = pltpu.SemaphoreType.DMA

    keep, send = pl.pallas_call(
        window_kernel,
        in_specs=[hbm] * 3,
        out_specs=[vmem] * 2,
        out_shape=[jax.ShapeDtypeStruct((PIECES, depths, piece, cols), bf16)] * 2,
        scratch_shapes=[
            SMEM(slab_map.shape, jnp.int32),
            SMEM(shot_corner.shape, jnp.int32),
            VMEM((1,) + slab_shape, bf16),
            dma((3,)),
        ],
        compiler_params=pltpu.CompilerParams(vmem_limit_bytes=16 << 20),
        name="window",
    )(pin(slab_map), pin(shot_corner), pin(slowness_slabs))

    def swap(value, bit):
        return lax.ppermute(value, "freq", [(i, i ^ bit) for i in range(ranks)])

    held = keep + swap(send, 1)
    early_bins, held = lax.optimization_barrier((frequency_bins, held))
    spectrum_shapes = [
        jax.ShapeDtypeStruct((4, rows, cols), f32),
        jax.ShapeDtypeStruct((3, rows, cols), f32),
        jax.ShapeDtypeStruct((3, rows, cols), f32),
    ]
    returned_shape = jax.ShapeDtypeStruct((3, 4, rows, cols), bf16)
    flops = 2 * 4 * (1 + 3) * rows * rows * cols
    *spectrum, held_scalars = pl.pallas_call(
        out_kernel,
        in_specs=[hbm] * 6,
        out_specs=[vmem] * 4,
        out_shape=spectrum_shapes
        + [jax.ShapeDtypeStruct((8 * pl.cdiv(1 + 3 * depths, 8), cols), f32)],
        scratch_shapes=[
            SMEM(frequency_bins.shape, jnp.int32),
            SMEM(reference_gaps.shape, f32),
            VMEM((4, rows, cols), bf16),
            VMEM((rows, rows), bf16),
            VMEM((cols, cols), bf16),
            VMEM((4, rows, cols), bf16),
            dma((6,)),
        ],
        compiler_params=pltpu.CompilerParams(vmem_limit_bytes=20 << 20),
        cost_estimate=pl.CostEstimate(flops=flops // 2, bytes_accessed=4 << 20, transcendentals=0),
        name="out",
    )(
        *[
            pin(value)
            for value in (
                early_bins,
                reference_gaps,
                source_field,
                receiver_field,
                forward_x,
                forward_y,
            )
        ]
    )
    own = held[0] + sum(swap(held[step], 2 * step) for step in range(1, PIECES))
    own, spectrum = lax.optimization_barrier((own, spectrum))
    returned, bracket, kept_inverse = pl.pallas_call(
        back_kernel,
        in_specs=[vmem] * 3 + [hbm] * 3,
        out_specs=[vmem] * 3,
        out_shape=[
            returned_shape,
            jax.ShapeDtypeStruct((rows, cols), jnp.int32),
            jax.ShapeDtypeStruct((cols, cols), bf16),
        ],
        scratch_shapes=[
            VMEM((rows, rows), bf16),
            VMEM((3, 4, rows, cols), bf16),
            dma((3,)),
        ],
        compiler_params=pltpu.CompilerParams(vmem_limit_bytes=24 << 20),
        cost_estimate=pl.CostEstimate(flops=flops, bytes_accessed=4 << 20, transcendentals=0),
        name="back",
    )(*spectrum, pin(inverse_x), pin(reference_index), pin(inverse_y))
    bit = 2 * PIECES
    while bit < ranks:
        own = own + swap(own, bit)
        bit *= 2
    own, returned = lax.optimization_barrier((own, returned))
    near_slow = jnp.stack([own] + [swap(own, 2 * step) for step in range(1, PIECES)])
    far_slow = swap(near_slow, 1)

    blend_scratch = [VMEM((12, piece, cols), f32)] * 2
    paired = ranks <= 16 and depths > 1 and tile % (2 * IMAGE_ROWS) == 0
    wave_shape = jax.ShapeDtypeStruct((4, half, cols), bf16)

    def mix(depth, far, *operands):
        last = depth == depths - 1
        tiles = (ranks // 2,) if not far else (2, ranks // 2) if paired and last else (ranks,)
        return pl.pallas_call(
            functools.partial(
                mix_kernel, depth=depth, far=far, last=last, paired=paired and last
            ),
            in_specs=[vmem] * len(operands),
            out_specs=[vmem] * (2 - last),
            out_shape=[wave_shape] * (1 - last)
            + [jax.ShapeDtypeStruct(tiles + (2, tile, cols), bf16)],
            scratch_shapes=blend_scratch,
            compiler_params=pltpu.CompilerParams(vmem_limit_bytes=16 << 20),
            cost_estimate=pl.CostEstimate(
                flops=flops // 4, bytes_accessed=1 << 20, transcendentals=0
            ),
            name="far" if far else "near",
        )(*operands)

    *near_wave, near_cross = mix(0, False, held_scalars, returned, near_slow, bracket, kept_inverse)
    *far_wave, cross = mix(
        0, True, held_scalars, returned, far_slow, bracket, kept_inverse, near_cross
    )
    crosses = [cross]
    for depth in range(1, depths):
        returned, bracket = pl.pallas_call(
            functools.partial(march_kernel, depth=depth),
            in_specs=[vmem] * 3 + [hbm] * 4,
            out_specs=[vmem] * 2,
            out_shape=[returned_shape, jax.ShapeDtypeStruct((rows, cols), jnp.int32)],
            scratch_shapes=[
                VMEM((rows, rows), bf16),
                VMEM((cols, cols), bf16),
                VMEM((rows, rows), bf16),
                dma((4,)),
                VMEM((4, rows, cols), bf16),
                VMEM((3, 4, rows, cols), bf16),
                *[VMEM(shape.shape, f32) for shape in spectrum_shapes],
            ],
            compiler_params=pltpu.CompilerParams(vmem_limit_bytes=28 << 20),
            cost_estimate=pl.CostEstimate(
                flops=3 * flops // 2, bytes_accessed=8 << 20, transcendentals=0
            ),
            name="march",
        )(
            held_scalars,
            *near_wave,
            *far_wave,
            pin(reference_index),
            pin(forward_x),
            pin(forward_y),
            pin(inverse_x),
        )
        *near_wave, near_cross = mix(
            depth, False, held_scalars, returned, near_slow, bracket, kept_inverse
        )
        *far_wave, cross = mix(
            depth, True, held_scalars, returned, far_slow, bracket, kept_inverse, near_cross
        )
        crosses.append(cross)

    offsets = jnp.arange(LAGS, dtype=jnp.int32) - LAGS // 2
    cycles = jnp.mod(frequency_bins[:, None] * offsets[None, :], period_bins).astype(f32)
    angles = cycles * (2.0 * math.pi / period_bins)
    lag_weights = jnp.stack([jnp.cos(angles), jnp.sin(angles)], axis=1).astype(bf16)

    scale = bins ** (-0.5)
    def exchange(value):
        return lax.all_to_all(value, "freq", split_axis=0, concat_axis=0, tiled=True)

    if not paired:
        arrivals = [[exchange(cross)] for cross in crosses]
    else:
        arrivals = [[exchange(cross)] for cross in crosses[:-1]]
        by_core = crosses[-1]
        by_chip = jnp.stack([by_core[0], swap(by_core[1], 1)], axis=1)
        chips = ranks // 2
        got = {step: swap(by_chip[step], 2 * step) for step in range(chips - 1, 0, -1)}
        arrivals.append([by_chip[0]] + [got[step] for step in range(1, chips)])
    if tile % (2 * IMAGE_ROWS):
        summed = jnp.einsum(
            "dwcab,wcl->dabl",
            jnp.stack([arrived for (arrived,) in arrivals]),
            lag_weights,
            preferred_element_type=f32,
        )
        return summed * scale
    height = bins * 2 * IMAGE_ROWS
    weights = pl.pallas_call(
        lag_kernel,
        in_specs=[vmem],
        out_specs=[vmem] * (1 + paired),
        out_shape=[jax.ShapeDtypeStruct((height, IMAGE_ROWS * LAGS), bf16)] * (1 + paired),
        compiler_params=pltpu.CompilerParams(vmem_limit_bytes=16 << 20),
        name="lag",
    )(lag_weights.astype(f32))
    image = None
    for depth, arrived in enumerate(arrivals):
        aliased = image is not None
        count = len(arrived)
        image = pl.pallas_call(
            functools.partial(
                image_kernel, scale=scale, depth=depth, aliased=aliased, count=count
            ),
            in_specs=[vmem] * (count + 1) + [hbm] * aliased,
            out_specs=hbm,
            out_shape=jax.ShapeDtypeStruct((depths, tile, cols, LAGS), f32),
            scratch_shapes=[VMEM((tile, cols, LAGS), f32), dma((tile,))],
            input_output_aliases={count + 1: 0} if aliased else {},
            compiler_params=pltpu.CompilerParams(vmem_limit_bytes=28 << 20),
            name="image",
        )(*arrived, weights[count > 1], *([image] if aliased else []))
    return image


def solution(mesh):
    placed = (
        P("grp", "freq", None, None),
        P("grp", "freq", None, None),
        P(("grp", "freq"), None, None),
        P("grp"),
        P("grp", None),
        P("grp", None, None),
        P(),
        P("grp"),
    )
    return jax.shard_map(
        functools.partial(shards, ranks=mesh.shape["freq"]),
        mesh=mesh,
        in_specs=placed,
        out_specs=P("grp", "freq", None, None),
        check_vma=False,
    )
```

```python
import functools
import math

import jax
import jax.numpy as jnp
import numpy as np
from jax import lax
from jax.experimental import pallas as pl
from jax.experimental.pallas import tpu as pltpu
from jax.sharding import PartitionSpec as P

LAGS = 256

cell_width = 0.0125
layer_thick = 0.0125
bin_hertz = 0.5
period_bins = 500
slow_base = 0.3

VMEM = pltpu.VMEM
SMEM = pltpu.SMEM
f32 = jnp.float32
bf16 = jnp.bfloat16


def real_table(length):
    half = length // 2
    steps = np.arange(length, dtype=np.int64)
    wave = np.concatenate([np.arange(half), [half], np.arange(1, half)])
    phases = np.mod(steps[:, None] * wave[None, :], length).astype(np.float32)
    angles = phases * np.float32(2.0 * math.pi / length)
    scale = np.float32(1.0 / math.sqrt(length))
    is_cos = np.arange(length) <= half
    table = np.where(is_cos[None, :], np.cos(angles), np.sin(angles)) * scale
    twice = np.where((wave == 0) | (wave == half), 1.0, 2.0)
    forward = jnp.asarray(table.astype(np.float32)).astype(bf16)
    inverse = (forward.astype(f32) * jnp.asarray(twice[None, :], f32)).astype(bf16)
    return forward, inverse


def sin_cos(angle):
    turns = jnp.floor(angle * (2.0 / math.pi) + 0.5)
    rest = angle - turns * 1.5707397460937500
    rest = rest - turns * 5.6580702948965924e-05
    quadrant = turns.astype(jnp.int32)
    square = rest * rest
    sine = rest + rest * square * (
        -1.6666654611e-1 + square * (8.3321608736e-3 - square * 1.9515295891e-4)
    )
    cosine = (
        1.0
        - 0.5 * square
        + square
        * square
        * (4.166664568298827e-2 + square * (-1.388731625493765e-3 + square * 2.443315711809948e-5))
    )
    odd = (quadrant & 1) == 1
    out_sin = jnp.where(odd, cosine, sine)
    out_cos = jnp.where(odd, sine, cosine)
    out_sin = jnp.where((quadrant & 2) == 2, -out_sin, out_sin)
    out_cos = jnp.where(((quadrant + 1) & 2) == 2, -out_cos, out_cos)
    return out_sin, out_cos


def references_of(gaps_ref, depth):
    first = slow_base + gaps_ref[depth, 0]
    second = first + gaps_ref[depth, 1]
    third = second + gaps_ref[depth, 2]
    return first, second, third


def scalars_of(held_ref, depth):
    rows = [held_ref[row : row + 1] for row in (0, *range(1 + 3 * depth, 4 + 3 * depth))]
    return rows[0], tuple(rows[1:])


def angular_of(bins_ref):
    return bins_ref[lax.axis_index("freq")].astype(f32) * (2.0 * math.pi * bin_hertz)


def phase_block(reach, base_turn, squares):
    radicand = reach - squares
    root = jnp.sqrt(jnp.abs(radicand)) * layer_thick
    travelling = radicand > 0.0
    fading = jnp.where(travelling, 1.0, jnp.exp(-root))
    sine, cosine = sin_cos(jnp.where(travelling, root, 0.0) - base_turn)
    return fading * cosine, fading * sine


def make_phases(cos_ref, sin_ref, angular, reference):
    rows, cols = cos_ref.shape
    half = rows // 2
    reach = (angular * reference) * (angular * reference)
    base_turn = angular * layer_thick * reference
    step_x = 2.0 * math.pi / (rows * cell_width)
    step_y = 2.0 * math.pi / (cols * cell_width)
    lane = lax.broadcasted_iota(jnp.int32, (8, cols), 1)
    wave_y = jnp.where(lane <= cols // 2, lane, lane - cols // 2).astype(f32) * step_y
    square_y = wave_y * wave_y
    tall = 64

    def body(block, carry):
        start = pl.multiple_of(block * tall, tall)
        row = lax.broadcasted_iota(jnp.int32, (tall, cols), 0) + start
        wave_x = row.astype(f32) * step_x
        cosine, sine = phase_block(
            reach, base_turn, wave_x * wave_x + jnp.concatenate([square_y] * (tall // 8), axis=0)
        )
        cos_ref[pl.ds(start, tall), :] = cosine
        sin_ref[pl.ds(start, tall), :] = sine
        cos_ref[pl.ds(half + start, tall), :] = cosine
        sin_ref[pl.ds(half + start, tall), :] = sine
        return carry

    lax.fori_loop(0, half // tall, body, 0)
    edge = (half * step_x) ** 2
    cosine, sine = phase_block(reach, base_turn, edge + square_y)
    top = lax.broadcasted_iota(jnp.int32, (8, cols), 0) == 0
    cos_ref[half : half + 8, :] = jnp.where(top, cosine, cos_ref[half : half + 8, :])
    sin_ref[half : half + 8, :] = jnp.where(top, sine, sin_ref[half : half + 8, :])


def dot(left, right):
    return jnp.dot(left, right, preferred_element_type=f32)


def march_out(fill_half, forward_x, scalars, half_ref, spectrum, ready=((), ())):
    angular, references = scalars
    spec_ref, cos_ref, sin_ref = spectrum
    for j in range(3):
        make_phases(cos_ref.at[j], sin_ref.at[j], angular, references[j])
    for wait in ready[0]:
        wait()
    for plane in range(4):
        fill_half(plane)
    for wait in ready[1]:
        wait()
    for plane in range(4):
        spec_ref[plane] = dot(forward_x[...], half_ref[plane])


def march_back(spectrum, inverse_x, shift_ref, out_ref, ready=()):
    spec_ref, cos_ref, sin_ref = spectrum
    for j in range(3):
        for field in range(2):
            real, imag = spec_ref[2 * field], spec_ref[2 * field + 1]
            cosine, sine = cos_ref[j], sin_ref[j]
            shift_ref[j, 2 * field] = (cosine * real - sine * imag).astype(bf16)
            shift_ref[j, 2 * field + 1] = (cosine * imag + sine * real).astype(bf16)
        if j == 0:
            for wait in ready:
                wait()
        for plane in range(4):
            out_ref[j, plane] = dot(inverse_x[...], shift_ref[j, plane]).astype(bf16)


def blend(returned_ref, slow_ref, bracket_ref, inverse_y, scalars, parts, put_wave, put_cross, starts):
    tall, cols = slow_ref.shape[1:]
    chunk = 16
    angular, (low, mid, high) = scalars
    slope_low = 1.0 / (mid - low)
    slope_high = 1.0 / (high - mid)
    def first_row(block):
        return pl.multiple_of(starts[block], tall)

    def fill(part_ref, block):
        left = returned_ref[:, :, pl.ds(first_row(block), tall), :].reshape(12 * tall, cols)
        part_ref[...] = dot(left, inverse_y[...]).reshape(12, tall, cols)

    def mix(part_ref, block):
        start = first_row(block)
        crossed = []
        for piece in range(tall // chunk):
            within = slice(piece * chunk, (piece + 1) * chunk)
            here = pl.ds(pl.multiple_of(start + piece * chunk, chunk), chunk)
            slow = slow_ref[block, within].astype(f32)
            lower = bracket_ref[here, :] == 0
            weight = jnp.where(lower, (slow - low) * slope_low, (slow - mid) * slope_high)
            weight = jnp.minimum(jnp.maximum(weight, 0.0), 1.0)
            sine, cosine = sin_cos(slow * (angular * layer_thick))
            halves = []
            for plane in range(4):
                if inverse_y is None:
                    first, second, third = [returned_ref[4 * j + plane, here] for j in range(3)]
                else:
                    first, second, third = [part_ref[4 * j + plane, within] for j in range(3)]
                bottom = jnp.where(lower, first, second)
                top = jnp.where(lower, second, third)
                halves.append(bottom + weight * (top - bottom))
            fresh = []
            for field in range(2):
                real, imag = halves[2 * field], halves[2 * field + 1]
                fresh.append((cosine * real - sine * imag).astype(bf16))
                fresh.append((cosine * imag + sine * real).astype(bf16))
            if put_wave is not None:
                for plane in range(4):
                    put_wave(block, within, plane, fresh[plane])
            s_real, s_imag, r_real, r_imag = [value.astype(f32) for value in fresh]
            crossed.append(
                (
                    (s_real * r_real - s_imag * r_imag).astype(bf16),
                    (s_real * r_imag + s_imag * r_real).astype(bf16),
                )
            )
        for side in range(2):
            put_cross(block, side, jnp.concatenate([pair[side] for pair in crossed], axis=0))

    if inverse_y is None:
        for block in range(len(starts)):
            mix(None, block)
        return
    even, odd = parts
    fill(even, 0)
    for block in range(len(starts)):
        here, other = (even, odd) if block % 2 == 0 else (odd, even)
        if block + 1 < len(starts):
            fill(other, block + 1)
        mix(here, block)


PIECES = 4


def piece_starts(piece):
    rank = lax.axis_index("freq")
    core, place = rank % 2, (rank // 2) % PIECES
    return [
        [(side * PIECES + (place ^ step)) * piece for step in range(PIECES)]
        for side in (core, 1 - core)
    ]


def window_kernel(
    map_hbm, corner_hbm, slab_hbm, keep_ref, send_ref, map_ref, corner_ref, slab_ref, sems
):
    depths, piece, cols = keep_ref.shape[1:]
    slab_count = slab_hbm.shape[0]
    tall, wide = slab_hbm.shape[1:]
    copies = [
        pltpu.make_async_copy(map_hbm, map_ref, sems.at[0]),
        pltpu.make_async_copy(corner_hbm, corner_ref, sems.at[1]),
    ]
    for copy in copies:
        copy.start()
    if slab_count == 1:
        whole = pltpu.make_async_copy(slab_hbm.at[0], slab_ref.at[0], sems.at[2])
        whole.start()
    for copy in copies:
        copy.wait()
    if slab_count == 1:
        whole.wait()
    rank = lax.axis_index("freq")
    rows = 2 * PIECES * piece
    first_row = jnp.minimum((corner_ref[0] // 16) * 16, tall - rows - 16)
    first_col = jnp.minimum((corner_ref[1] // 128) * 128, wide - cols - 128)
    above = corner_ref[0] - first_row
    before = corner_ref[1] - first_col
    reach = piece + 16
    span = cols + 128
    for depth in range(depths):
        slab = map_ref[depth]
        mine = slab // slab_count == rank

        @pl.when(mine)
        def _():
            if slab_count == 1:
                here = slab_ref.at[0]
            else:
                here = slab_ref.at[0]
                copy = pltpu.make_async_copy(
                    slab_hbm.at[lax.rem(slab, slab_count)], here, sems.at[2]
                )
                copy.start()
                copy.wait()
            for target, starts in zip((keep_ref, send_ref), piece_starts(piece)):
                for step, start in enumerate(starts):
                    block = here[
                        pl.ds(pl.multiple_of(first_row + start, 16), reach),
                        pl.ds(pl.multiple_of(first_col, 128), span),
                    ].astype(f32)
                    block = pltpu.roll(block, lax.rem(span - before, span), 1)[:, :cols]
                    block = pltpu.roll(block, lax.rem(reach - above, reach), 0)[:piece]
                    target[step, depth] = block.astype(bf16)

        @pl.when(jnp.logical_not(mine))
        def _():
            for target in (keep_ref, send_ref):
                target[:, depth] = jnp.zeros((PIECES, piece, cols), bf16)


def fetch(pairs, sems):
    copies = [
        pltpu.make_async_copy(source, target, sems.at[index])
        for index, (source, target) in enumerate(pairs)
    ]
    for copy in copies:
        copy.start()
    return [copy.wait for copy in copies]


def out_kernel(
    bins_hbm,
    gaps_hbm,
    source_hbm,
    receiver_hbm,
    forward_x_hbm,
    forward_y_hbm,
    spec_ref,
    cos_ref,
    sin_ref,
    held_ref,
    bins_ref,
    gaps_ref,
    wave_ref,
    forward_x,
    forward_y,
    half_ref,
    sems,
):
    waits = fetch(
        [
            (bins_hbm, bins_ref),
            (gaps_hbm, gaps_ref),
            (forward_y_hbm, forward_y),
            (source_hbm.at[:, 0], wave_ref.at[0:2]),
            (receiver_hbm.at[:, 0], wave_ref.at[2:4]),
            (forward_x_hbm, forward_x),
        ],
        sems,
    )
    waits[0]()
    waits[1]()
    angular = angular_of(bins_ref)
    held_ref[0:1] = jnp.full((1, held_ref.shape[1]), angular, f32)
    for depth in range(gaps_ref.shape[0]):
        for j, reference in enumerate(references_of(gaps_ref, depth)):
            row = 1 + 3 * depth + j
            held_ref[row : row + 1] = jnp.full((1, held_ref.shape[1]), reference, f32)

    def fill_half(plane):
        half = dot(wave_ref[plane], forward_y[...])
        half_ref[plane] = (half if plane < 3 else -half).astype(bf16)

    march_out(
        fill_half,
        forward_x,
        (angular, references_of(gaps_ref, 0)),
        half_ref,
        (spec_ref, cos_ref, sin_ref),
        ready=(waits[2:5], waits[5:]),
    )


def back_kernel(
    spec_ref,
    cos_ref,
    sin_ref,
    inverse_x_hbm,
    bracket_hbm,
    inverse_y_hbm,
    out_ref,
    bracket_ref,
    inverse_y,
    inverse_x,
    shift_ref,
    sems,
):
    waits = fetch(
        [
            (inverse_x_hbm, inverse_x),
            (bracket_hbm.at[0], bracket_ref),
            (inverse_y_hbm, inverse_y),
        ],
        sems,
    )
    march_back((spec_ref, cos_ref, sin_ref), inverse_x, shift_ref, out_ref, waits[:1])
    for wait in waits[1:]:
        wait()


def unfold_kernel(returned_ref, inverse_y, part_ref):
    rows, cols = returned_ref.shape[2:]
    for j in range(3):
        for plane in range(4):
            part_ref[4 * j + plane] = dot(returned_ref[j, plane], inverse_y[...])


def place_of(rank):
    here = lax.axis_index("freq")
    return (rank ^ here) % 2, (rank // 2) ^ (here // 2)


def mix_kernel(*refs, depth, far, last, paired):
    held_ref, returned_ref, slow_ref, bracket_ref = refs[:4]
    inverse_y, rest = (None, refs[4:]) if depth == 0 else (refs[4], refs[5:])
    if far:
        near_cross, rest = rest[0], rest[1:]
    if not last:
        wave_ref, rest = rest[0], rest[1:]
    cross_ref, *parts = rest
    piece = slow_ref.shape[2]
    tile = cross_ref.shape[-2]
    tiles = piece // tile
    near_starts, far_starts = piece_starts(piece)
    starts = far_starts if far else near_starts
    if far:
        for step, start in enumerate(near_starts):
            if paired:
                for part in range(tiles):
                    cross_ref[place_of(start // tile + part)] = near_cross[step * tiles + part]
                continue
            cross_ref[pl.ds(start // tile, tiles)] = near_cross[step * tiles : (step + 1) * tiles]

    def put_wave(block, within, plane, values):
        wave_ref[plane, block * piece + within.start : block * piece + within.stop] = values

    def put_cross(block, side, values):
        for part in range(tiles):
            rank = starts[block] // tile + part if far else block * tiles + part
            place = place_of(rank) if far and paired else (rank,)
            cross_ref[*place, side] = values[part * tile : (part + 1) * tile]

    blend(
        returned_ref,
        slow_ref.at[:, depth],
        bracket_ref,
        inverse_y,
        scalars_of(held_ref, depth),
        parts,
        None if last else put_wave,
        put_cross,
        starts,
    )


def march_kernel(
    held_ref,
    near_wave,
    far_wave,
    bracket_hbm,
    forward_x_hbm,
    forward_y_hbm,
    inverse_x_hbm,
    out_ref,
    bracket_ref,
    forward_x,
    forward_y,
    inverse_x,
    sems,
    half_ref,
    shift_ref,
    *spectrum,
    depth,
):
    waits = fetch(
        [
            (forward_y_hbm, forward_y),
            (forward_x_hbm, forward_x),
            (inverse_x_hbm, inverse_x),
            (bracket_hbm.at[depth], bracket_ref),
        ],
        sems,
    )
    piece = near_wave.shape[1] // PIECES

    def fill_half(plane):
        for starts, wave_ref in zip(piece_starts(piece), (near_wave, far_wave)):
            half = dot(wave_ref[plane], forward_y[...]).astype(bf16)
            for step, start in enumerate(starts):
                here = pl.ds(pl.multiple_of(start, piece), piece)
                half_ref[plane, here, :] = half[step * piece : (step + 1) * piece]

    march_out(
        fill_half,
        forward_x,
        scalars_of(held_ref, depth),
        half_ref,
        spectrum,
        ready=(waits[:1], waits[1:2]),
    )
    march_back(spectrum, inverse_x, shift_ref, out_ref, waits[2:3])
    waits[3]()


IMAGE_ROWS = 8
PAIR_ORDER = (4, 5, 6, 7, 2, 3, 1)


def lag_kernel(lag_ref, *weight_refs):
    bins, pair, lags = lag_ref.shape
    height = bins * pair * IMAGE_ROWS
    here = lax.axis_index("freq")
    steps = (0, *PAIR_ORDER)
    by_pair = [2 * steps[spot // 2] + spot % 2 for spot in range(bins)] if weight_refs[1:] else None
    for weight_ref, spots, mask in zip(weight_refs, (range(bins), by_pair), (0, here)):
        table = jnp.concatenate(
            [
                jnp.broadcast_to(lag_ref[spot ^ mask][:, None], (pair, IMAGE_ROWS, lags)).reshape(
                    pair * IMAGE_ROWS, lags
                )
                for spot in spots
            ],
            axis=0,
        )
        place = lax.broadcasted_iota(jnp.int32, (height, lags), 0) % IMAGE_ROWS
        for row in range(IMAGE_ROWS):
            weight_ref[:, row * lags : (row + 1) * lags] = jnp.where(
                place == row, table, 0.0
            ).astype(bf16)


def image_kernel(*refs, scale, depth, aliased, count):
    cross_refs, weight_ref = refs[:count], refs[count]
    out_hbm, made_ref, sems = refs[count + 1 + aliased :]
    tile, cols, lags = made_ref.shape
    copies = []
    for group in range(tile // IMAGE_ROWS):
        rows = slice(group * IMAGE_ROWS, (group + 1) * IMAGE_ROWS)
        left = jnp.concatenate(
            [ref[..., rows, :].astype(f32).reshape(-1, cols) for ref in cross_refs], axis=0
        )
        left = left.T.astype(bf16)
        for row in range(IMAGE_ROWS):
            place = group * IMAGE_ROWS + row
            made_ref[place] = dot(left, weight_ref[:, row * lags : (row + 1) * lags]) * scale
            copies.append(
                pltpu.make_async_copy(
                    made_ref.at[place], out_hbm.at[depth, place], sems.at[place]
                )
            )
            copies[-1].start()
    for copy in copies:
        copy.wait()


def pin(value):
    return pltpu.with_memory_space_constraint(value, pltpu.HBM)


def shards(
    source_field,
    receiver_field,
    slowness_slabs,
    slab_map,
    reference_gaps,
    reference_index,
    frequency_bins,
    shot_corner,
    *,
    ranks,
):
    rows, cols = source_field.shape[2:]
    depths = slab_map.shape[0]
    slab_count = slowness_slabs.shape[0]
    half = rows // 2
    piece = half // PIECES
    tile = rows // ranks
    bins = frequency_bins.shape[0]
    slab_shape = slowness_slabs.shape[1:]
    forward_x, inverse_x = real_table(rows)
    forward_x = forward_x.T
    forward_y, inverse_y = real_table(cols)
    inverse_y = inverse_y.T

    hbm = pl.BlockSpec(memory_space=pltpu.HBM)
    vmem = pl.BlockSpec(memory_space=VMEM)
    dma = pltpu.SemaphoreType.DMA

    keep, send = pl.pallas_call(
        window_kernel,
        in_specs=[hbm] * 3,
        out_specs=[vmem] * 2,
        out_shape=[jax.ShapeDtypeStruct((PIECES, depths, piece, cols), bf16)] * 2,
        scratch_shapes=[
            SMEM(slab_map.shape, jnp.int32),
            SMEM(shot_corner.shape, jnp.int32),
            VMEM((1,) + slab_shape, bf16),
            dma((3,)),
        ],
        compiler_params=pltpu.CompilerParams(vmem_limit_bytes=16 << 20),
        name="window",
    )(pin(slab_map), pin(shot_corner), pin(slowness_slabs))

    def swap(value, bit):
        return lax.ppermute(value, "freq", [(i, i ^ bit) for i in range(ranks)])

    held = keep + swap(send, 1)
    early_bins, held = lax.optimization_barrier((frequency_bins, held))
    spectrum_shapes = [
        jax.ShapeDtypeStruct((4, rows, cols), f32),
        jax.ShapeDtypeStruct((3, rows, cols), f32),
        jax.ShapeDtypeStruct((3, rows, cols), f32),
    ]
    returned_shape = jax.ShapeDtypeStruct((3, 4, rows, cols), bf16)
    flops = 2 * 4 * (1 + 3) * rows * rows * cols
    *spectrum, held_scalars = pl.pallas_call(
        out_kernel,
        in_specs=[hbm] * 6,
        out_specs=[vmem] * 4,
        out_shape=spectrum_shapes
        + [jax.ShapeDtypeStruct((8 * pl.cdiv(1 + 3 * depths, 8), cols), f32)],
        scratch_shapes=[
            SMEM(frequency_bins.shape, jnp.int32),
            SMEM(reference_gaps.shape, f32),
            VMEM((4, rows, cols), bf16),
            VMEM((rows, rows), bf16),
            VMEM((cols, cols), bf16),
            VMEM((4, rows, cols), bf16),
            dma((6,)),
        ],
        compiler_params=pltpu.CompilerParams(vmem_limit_bytes=20 << 20),
        cost_estimate=pl.CostEstimate(flops=flops // 2, bytes_accessed=4 << 20, transcendentals=0),
        name="out",
    )(
        *[
            pin(value)
            for value in (
                early_bins,
                reference_gaps,
                source_field,
                receiver_field,
                forward_x,
                forward_y,
            )
        ]
    )
    own = held[0] + sum(swap(held[step], 2 * step) for step in range(1, PIECES))
    own, spectrum = lax.optimization_barrier((own, spectrum))
    returned, bracket, kept_inverse = pl.pallas_call(
        back_kernel,
        in_specs=[vmem] * 3 + [hbm] * 3,
        out_specs=[vmem] * 3,
        out_shape=[
            returned_shape,
            jax.ShapeDtypeStruct((rows, cols), jnp.int32),
            jax.ShapeDtypeStruct((cols, cols), bf16),
        ],
        scratch_shapes=[
            VMEM((rows, rows), bf16),
            VMEM((3, 4, rows, cols), bf16),
            dma((3,)),
        ],
        compiler_params=pltpu.CompilerParams(vmem_limit_bytes=24 << 20),
        cost_estimate=pl.CostEstimate(flops=flops, bytes_accessed=4 << 20, transcendentals=0),
        name="back",
    )(*spectrum, pin(inverse_x), pin(reference_index), pin(inverse_y))
    bit = 2 * PIECES
    while bit < ranks:
        own = own + swap(own, bit)
        bit *= 2
    own, returned = lax.optimization_barrier((own, returned))
    pieces = [own] + [swap(own, 2 * step) for step in range(1, PIECES)]
    part = pl.pallas_call(
        unfold_kernel,
        in_specs=[vmem] * 2,
        out_specs=vmem,
        out_shape=jax.ShapeDtypeStruct((12, rows, cols), f32),
        compiler_params=pltpu.CompilerParams(vmem_limit_bytes=16 << 20),
        cost_estimate=pl.CostEstimate(flops=flops // 2, bytes_accessed=1 << 20, transcendentals=0),
        name="unfold",
    )(returned, kept_inverse)
    pieces, part = lax.optimization_barrier((pieces, part))
    near_slow = jnp.stack(pieces)
    far_slow = swap(near_slow, 1)

    blend_scratch = [VMEM((12, piece, cols), f32)] * 2
    paired = ranks == 2 * (1 + len(PAIR_ORDER)) and depths > 1 and tile % (2 * IMAGE_ROWS) == 0
    wave_shape = jax.ShapeDtypeStruct((4, half, cols), bf16)

    def mix(depth, far, *operands):
        last = depth == depths - 1
        tiles = (ranks // 2,) if not far else (2, ranks // 2) if paired and last else (ranks,)
        return pl.pallas_call(
            functools.partial(
                mix_kernel, depth=depth, far=far, last=last, paired=paired and last
            ),
            in_specs=[vmem] * len(operands),
            out_specs=[vmem] * (2 - last),
            out_shape=[wave_shape] * (1 - last)
            + [jax.ShapeDtypeStruct(tiles + (2, tile, cols), bf16)],
            scratch_shapes=blend_scratch if depth else [],
            compiler_params=pltpu.CompilerParams(vmem_limit_bytes=16 << 20),
            cost_estimate=pl.CostEstimate(
                flops=flops // 4, bytes_accessed=1 << 20, transcendentals=0
            ),
            name="far" if far else "near",
        )(*operands)

    *near_wave, near_cross = mix(0, False, held_scalars, part, near_slow, bracket)
    *far_wave, cross = mix(
        0, True, held_scalars, part, far_slow, bracket, near_cross
    )
    crosses = [cross]
    for depth in range(1, depths):
        returned, bracket = pl.pallas_call(
            functools.partial(march_kernel, depth=depth),
            in_specs=[vmem] * 3 + [hbm] * 4,
            out_specs=[vmem] * 2,
            out_shape=[returned_shape, jax.ShapeDtypeStruct((rows, cols), jnp.int32)],
            scratch_shapes=[
                VMEM((rows, rows), bf16),
                VMEM((cols, cols), bf16),
                VMEM((rows, rows), bf16),
                dma((4,)),
                VMEM((4, rows, cols), bf16),
                VMEM((3, 4, rows, cols), bf16),
                *[VMEM(shape.shape, f32) for shape in spectrum_shapes],
            ],
            compiler_params=pltpu.CompilerParams(vmem_limit_bytes=28 << 20),
            cost_estimate=pl.CostEstimate(
                flops=3 * flops // 2, bytes_accessed=8 << 20, transcendentals=0
            ),
            name="march",
        )(
            held_scalars,
            *near_wave,
            *far_wave,
            pin(reference_index),
            pin(forward_x),
            pin(forward_y),
            pin(inverse_x),
        )
        *near_wave, near_cross = mix(
            depth, False, held_scalars, returned, near_slow, bracket, kept_inverse
        )
        *far_wave, cross = mix(
            depth, True, held_scalars, returned, far_slow, bracket, kept_inverse, near_cross
        )
        crosses.append(cross)

    offsets = jnp.arange(LAGS, dtype=jnp.int32) - LAGS // 2
    cycles = jnp.mod(frequency_bins[:, None] * offsets[None, :], period_bins).astype(f32)
    angles = cycles * (2.0 * math.pi / period_bins)
    lag_weights = jnp.stack([jnp.cos(angles), jnp.sin(angles)], axis=1).astype(bf16)

    scale = bins ** (-0.5)
    def exchange(value):
        return lax.all_to_all(value, "freq", split_axis=0, concat_axis=0, tiled=True)

    if not paired:
        arrivals = [[exchange(cross)] for cross in crosses]
    else:
        arrivals = [[exchange(cross)] for cross in crosses[:-1]]
        by_core = crosses[-1]
        by_chip = jnp.stack([by_core[0], swap(by_core[1], 1)], axis=1)
        arrivals.append([by_chip[0]] + [swap(by_chip[step], 2 * step) for step in PAIR_ORDER])
    if tile % (2 * IMAGE_ROWS):
        summed = jnp.einsum(
            "dwcab,wcl->dabl",
            jnp.stack([arrived for (arrived,) in arrivals]),
            lag_weights,
            preferred_element_type=f32,
        )
        return summed * scale
    height = bins * 2 * IMAGE_ROWS
    weights = pl.pallas_call(
        lag_kernel,
        in_specs=[vmem],
        out_specs=[vmem] * (1 + paired),
        out_shape=[jax.ShapeDtypeStruct((height, IMAGE_ROWS * LAGS), bf16)] * (1 + paired),
        compiler_params=pltpu.CompilerParams(vmem_limit_bytes=16 << 20),
        name="lag",
    )(lag_weights.astype(f32))
    image = None
    for depth, arrived in enumerate(arrivals):
        aliased = image is not None
        count = len(arrived)
        image = pl.pallas_call(
            functools.partial(
                image_kernel, scale=scale, depth=depth, aliased=aliased, count=count
            ),
            in_specs=[vmem] * (count + 1) + [hbm] * aliased,
            out_specs=hbm,
            out_shape=jax.ShapeDtypeStruct((depths, tile, cols, LAGS), f32),
            scratch_shapes=[VMEM((tile, cols, LAGS), f32), dma((tile,))],
            input_output_aliases={count + 1: 0} if aliased else {},
            compiler_params=pltpu.CompilerParams(vmem_limit_bytes=28 << 20),
            name="image",
        )(*arrived, weights[count > 1], *([image] if aliased else []))
    return image


def solution(mesh):
    placed = (
        P("grp", "freq", None, None),
        P("grp", "freq", None, None),
        P(("grp", "freq"), None, None),
        P("grp"),
        P("grp", None),
        P("grp", None, None),
        P(),
        P("grp"),
    )
    return jax.shard_map(
        functools.partial(shards, ranks=mesh.shape["freq"]),
        mesh=mesh,
        in_specs=placed,
        out_specs=P("grp", "freq", None, None),
        check_vma=False,
    )
```

```python
import functools
import math

import jax
import jax.numpy as jnp
import numpy as np
from jax import lax
from jax.experimental import pallas as pl
from jax.experimental.pallas import tpu as pltpu
from jax.sharding import PartitionSpec as P

LAGS = 256

cell_width = 0.0125
layer_thick = 0.0125
bin_hertz = 0.5
period_bins = 500
slow_base = 0.3

VMEM = pltpu.VMEM
SMEM = pltpu.SMEM
f32 = jnp.float32
bf16 = jnp.bfloat16


def real_table(length):
    half = length // 2
    steps = np.arange(length, dtype=np.int64)
    wave = np.concatenate([np.arange(half), [half], np.arange(1, half)])
    phases = np.mod(steps[:, None] * wave[None, :], length).astype(np.float32)
    angles = phases * np.float32(2.0 * math.pi / length)
    scale = np.float32(1.0 / math.sqrt(length))
    is_cos = np.arange(length) <= half
    table = np.where(is_cos[None, :], np.cos(angles), np.sin(angles)) * scale
    twice = np.where((wave == 0) | (wave == half), 1.0, 2.0)
    forward = jnp.asarray(table.astype(np.float32)).astype(bf16)
    inverse = (forward.astype(f32) * jnp.asarray(twice[None, :], f32)).astype(bf16)
    return forward, inverse


def sin_cos(angle):
    turns = jnp.floor(angle * (2.0 / math.pi) + 0.5)
    rest = angle - turns * 1.5707397460937500
    rest = rest - turns * 5.6580702948965924e-05
    quadrant = turns.astype(jnp.int32)
    square = rest * rest
    sine = rest + rest * square * (
        -1.6666654611e-1 + square * (8.3321608736e-3 - square * 1.9515295891e-4)
    )
    cosine = (
        1.0
        - 0.5 * square
        + square
        * square
        * (4.166664568298827e-2 + square * (-1.388731625493765e-3 + square * 2.443315711809948e-5))
    )
    odd = (quadrant & 1) == 1
    out_sin = jnp.where(odd, cosine, sine)
    out_cos = jnp.where(odd, sine, cosine)
    out_sin = jnp.where((quadrant & 2) == 2, -out_sin, out_sin)
    out_cos = jnp.where(((quadrant + 1) & 2) == 2, -out_cos, out_cos)
    return out_sin, out_cos


def references_of(gaps_ref, depth):
    first = slow_base + gaps_ref[depth, 0]
    second = first + gaps_ref[depth, 1]
    third = second + gaps_ref[depth, 2]
    return first, second, third


def scalars_of(held_ref, depth):
    rows = [held_ref[row : row + 1] for row in (0, *range(1 + 3 * depth, 4 + 3 * depth))]
    return rows[0], tuple(rows[1:])


def angular_of(bins_ref):
    return bins_ref[lax.axis_index("freq")].astype(f32) * (2.0 * math.pi * bin_hertz)


def phase_block(reach, base_turn, squares):
    radicand = reach - squares
    root = jnp.sqrt(jnp.abs(radicand)) * layer_thick
    travelling = radicand > 0.0
    fading = jnp.where(travelling, 1.0, jnp.exp(-root))
    sine, cosine = sin_cos(jnp.where(travelling, root, 0.0) - base_turn)
    return fading * cosine, fading * sine


def make_phases(cos_ref, sin_ref, angular, reference):
    rows, cols = cos_ref.shape
    half = rows // 2
    reach = (angular * reference) * (angular * reference)
    base_turn = angular * layer_thick * reference
    step_x = 2.0 * math.pi / (rows * cell_width)
    step_y = 2.0 * math.pi / (cols * cell_width)
    lane = lax.broadcasted_iota(jnp.int32, (8, cols), 1)
    wave_y = jnp.where(lane <= cols // 2, lane, lane - cols // 2).astype(f32) * step_y
    square_y = wave_y * wave_y
    tall = 64

    def body(block, carry):
        start = pl.multiple_of(block * tall, tall)
        row = lax.broadcasted_iota(jnp.int32, (tall, cols), 0) + start
        wave_x = row.astype(f32) * step_x
        cosine, sine = phase_block(
            reach, base_turn, wave_x * wave_x + jnp.concatenate([square_y] * (tall // 8), axis=0)
        )
        cos_ref[pl.ds(start, tall), :] = cosine
        sin_ref[pl.ds(start, tall), :] = sine
        cos_ref[pl.ds(half + start, tall), :] = cosine
        sin_ref[pl.ds(half + start, tall), :] = sine
        return carry

    lax.fori_loop(0, half // tall, body, 0)
    edge = (half * step_x) ** 2
    cosine, sine = phase_block(reach, base_turn, edge + square_y)
    top = lax.broadcasted_iota(jnp.int32, (8, cols), 0) == 0
    cos_ref[half : half + 8, :] = jnp.where(top, cosine, cos_ref[half : half + 8, :])
    sin_ref[half : half + 8, :] = jnp.where(top, sine, sin_ref[half : half + 8, :])


def dot(left, right):
    return jnp.dot(left, right, preferred_element_type=f32)


def march_out(fill_half, forward_x, scalars, half_ref, spectrum, ready=((), ())):
    angular, references = scalars
    spec_ref, cos_ref, sin_ref = spectrum
    for j in range(3):
        make_phases(cos_ref.at[j], sin_ref.at[j], angular, references[j])
    for wait in ready[0]:
        wait()
    for plane in range(4):
        fill_half(plane)
    for wait in ready[1]:
        wait()
    for plane in range(4):
        spec_ref[plane] = dot(forward_x[...], half_ref[plane])


def march_back(spectrum, inverse_x, shift_ref, out_ref, ready=()):
    spec_ref, cos_ref, sin_ref = spectrum
    for j in range(3):
        for field in range(2):
            real, imag = spec_ref[2 * field], spec_ref[2 * field + 1]
            cosine, sine = cos_ref[j], sin_ref[j]
            shift_ref[j, 2 * field] = (cosine * real - sine * imag).astype(bf16)
            shift_ref[j, 2 * field + 1] = (cosine * imag + sine * real).astype(bf16)
        if j == 0:
            for wait in ready:
                wait()
        for plane in range(4):
            out_ref[j, plane] = dot(inverse_x[...], shift_ref[j, plane]).astype(bf16)


def blend(returned_ref, slow_ref, bracket_ref, inverse_y, scalars, parts, put_wave, put_cross, starts):
    tall, cols = slow_ref.shape[1:]
    chunk = 16
    angular, (low, mid, high) = scalars
    slope_low = 1.0 / (mid - low)
    slope_high = 1.0 / (high - mid)
    def first_row(block):
        return pl.multiple_of(starts[block], tall)

    def fill(part_ref, block):
        left = returned_ref[:, :, pl.ds(first_row(block), tall), :].reshape(12 * tall, cols)
        part_ref[...] = dot(left, inverse_y[...]).reshape(12, tall, cols)

    def mix(part_ref, block):
        start = first_row(block)
        crossed = []
        for piece in range(tall // chunk):
            within = slice(piece * chunk, (piece + 1) * chunk)
            here = pl.ds(pl.multiple_of(start + piece * chunk, chunk), chunk)
            slow = slow_ref[block, within].astype(f32)
            lower = bracket_ref[here, :] == 0
            weight = jnp.where(lower, (slow - low) * slope_low, (slow - mid) * slope_high)
            weight = jnp.minimum(jnp.maximum(weight, 0.0), 1.0)
            sine, cosine = sin_cos(slow * (angular * layer_thick))
            halves = []
            for plane in range(4):
                if inverse_y is None:
                    first, second, third = [returned_ref[4 * j + plane, here] for j in range(3)]
                else:
                    first, second, third = [part_ref[4 * j + plane, within] for j in range(3)]
                bottom = jnp.where(lower, first, second)
                top = jnp.where(lower, second, third)
                halves.append(bottom + weight * (top - bottom))
            fresh = []
            for field in range(2):
                real, imag = halves[2 * field], halves[2 * field + 1]
                fresh.append((cosine * real - sine * imag).astype(bf16))
                fresh.append((cosine * imag + sine * real).astype(bf16))
            if put_wave is not None:
                for plane in range(4):
                    put_wave(block, within, plane, fresh[plane])
            s_real, s_imag, r_real, r_imag = [value.astype(f32) for value in fresh]
            crossed.append(
                (
                    (s_real * r_real - s_imag * r_imag).astype(bf16),
                    (s_real * r_imag + s_imag * r_real).astype(bf16),
                )
            )
        for side in range(2):
            put_cross(block, side, jnp.concatenate([pair[side] for pair in crossed], axis=0))

    if inverse_y is None:
        for block in range(len(starts)):
            mix(None, block)
        return
    even, odd = parts
    fill(even, 0)
    for block in range(len(starts)):
        here, other = (even, odd) if block % 2 == 0 else (odd, even)
        if block + 1 < len(starts):
            fill(other, block + 1)
        mix(here, block)


PIECES = 4


def piece_starts(piece):
    rank = lax.axis_index("freq")
    core, place = rank % 2, (rank // 2) % PIECES
    return [
        [(side * PIECES + (place ^ step)) * piece for step in range(PIECES)]
        for side in (core, 1 - core)
    ]


def window_kernel(
    map_hbm, corner_hbm, slab_hbm, keep_ref, send_ref, map_ref, corner_ref, slab_ref, sems
):
    depths, piece, cols = keep_ref.shape[1:]
    slab_count = slab_hbm.shape[0]
    tall, wide = slab_hbm.shape[1:]
    copies = [
        pltpu.make_async_copy(map_hbm, map_ref, sems.at[0]),
        pltpu.make_async_copy(corner_hbm, corner_ref, sems.at[1]),
    ]
    for copy in copies:
        copy.start()
    if slab_count == 1:
        whole = pltpu.make_async_copy(slab_hbm.at[0], slab_ref.at[0], sems.at[2])
        whole.start()
    for copy in copies:
        copy.wait()
    if slab_count == 1:
        whole.wait()
    rank = lax.axis_index("freq")
    rows = 2 * PIECES * piece
    first_row = jnp.minimum((corner_ref[0] // 16) * 16, tall - rows - 16)
    first_col = jnp.minimum((corner_ref[1] // 128) * 128, wide - cols - 128)
    above = corner_ref[0] - first_row
    before = corner_ref[1] - first_col
    reach = piece + 16
    span = cols + 128
    for depth in range(depths):
        slab = map_ref[depth]
        mine = slab // slab_count == rank

        @pl.when(mine)
        def _():
            if slab_count == 1:
                here = slab_ref.at[0]
            else:
                here = slab_ref.at[0]
                copy = pltpu.make_async_copy(
                    slab_hbm.at[lax.rem(slab, slab_count)], here, sems.at[2]
                )
                copy.start()
                copy.wait()
            for target, starts in zip((keep_ref, send_ref), piece_starts(piece)):
                for step, start in enumerate(starts):
                    block = here[
                        pl.ds(pl.multiple_of(first_row + start, 16), reach),
                        pl.ds(pl.multiple_of(first_col, 128), span),
                    ].astype(f32)
                    block = pltpu.roll(block, lax.rem(span - before, span), 1)[:, :cols]
                    block = pltpu.roll(block, lax.rem(reach - above, reach), 0)[:piece]
                    target[step, depth] = block.astype(bf16)

        @pl.when(jnp.logical_not(mine))
        def _():
            for target in (keep_ref, send_ref):
                target[:, depth] = jnp.zeros((PIECES, piece, cols), bf16)


def fetch(pairs, sems):
    copies = [
        pltpu.make_async_copy(source, target, sems.at[index])
        for index, (source, target) in enumerate(pairs)
    ]
    for copy in copies:
        copy.start()
    return [copy.wait for copy in copies]


def out_kernel(
    bins_hbm,
    gaps_hbm,
    source_hbm,
    receiver_hbm,
    forward_x_hbm,
    forward_y_hbm,
    spec_ref,
    cos_ref,
    sin_ref,
    held_ref,
    bins_ref,
    gaps_ref,
    wave_ref,
    forward_x,
    forward_y,
    half_ref,
    sems,
):
    waits = fetch(
        [
            (bins_hbm, bins_ref),
            (gaps_hbm, gaps_ref),
            (forward_y_hbm, forward_y),
            (source_hbm.at[:, 0], wave_ref.at[0:2]),
            (receiver_hbm.at[:, 0], wave_ref.at[2:4]),
            (forward_x_hbm, forward_x),
        ],
        sems,
    )
    waits[0]()
    waits[1]()
    angular = angular_of(bins_ref)
    held_ref[0:1] = jnp.full((1, held_ref.shape[1]), angular, f32)
    for depth in range(gaps_ref.shape[0]):
        for j, reference in enumerate(references_of(gaps_ref, depth)):
            row = 1 + 3 * depth + j
            held_ref[row : row + 1] = jnp.full((1, held_ref.shape[1]), reference, f32)

    def fill_half(plane):
        half = dot(wave_ref[plane], forward_y[...])
        half_ref[plane] = (half if plane < 3 else -half).astype(bf16)

    march_out(
        fill_half,
        forward_x,
        (angular, references_of(gaps_ref, 0)),
        half_ref,
        (spec_ref, cos_ref, sin_ref),
        ready=(waits[2:5], waits[5:]),
    )


def back_kernel(
    spec_ref,
    cos_ref,
    sin_ref,
    inverse_x_hbm,
    bracket_hbm,
    inverse_y_hbm,
    out_ref,
    bracket_ref,
    inverse_y,
    inverse_x,
    shift_ref,
    sems,
):
    waits = fetch(
        [
            (inverse_x_hbm, inverse_x),
            (bracket_hbm.at[0], bracket_ref),
            (inverse_y_hbm, inverse_y),
        ],
        sems,
    )
    march_back((spec_ref, cos_ref, sin_ref), inverse_x, shift_ref, out_ref, waits[:1])
    for wait in waits[1:]:
        wait()


def unfold_kernel(returned_ref, inverse_y, part_ref):
    rows, cols = returned_ref.shape[2:]
    for j in range(3):
        for plane in range(4):
            part_ref[4 * j + plane] = dot(returned_ref[j, plane], inverse_y[...])


def place_of(rank):
    here = lax.axis_index("freq")
    return (rank ^ here) % 2, (rank // 2) ^ (here // 2)


def mix_kernel(*refs, depth, far, last, paired):
    held_ref, returned_ref, slow_ref, bracket_ref = refs[:4]
    inverse_y, rest = (None, refs[4:]) if depth == 0 else (refs[4], refs[5:])
    if far:
        near_cross, rest = rest[0], rest[1:]
    if not last:
        wave_ref, rest = rest[0], rest[1:]
    cross_ref, *parts = rest
    piece = slow_ref.shape[2]
    tile = cross_ref.shape[-2]
    tiles = piece // tile
    near_starts, far_starts = piece_starts(piece)
    starts = far_starts if far else near_starts
    if far:
        for step, start in enumerate(near_starts):
            if paired:
                for part in range(tiles):
                    cross_ref[place_of(start // tile + part)] = near_cross[step * tiles + part]
                continue
            cross_ref[pl.ds(start // tile, tiles)] = near_cross[step * tiles : (step + 1) * tiles]

    def put_wave(block, within, plane, values):
        wave_ref[plane, block * piece + within.start : block * piece + within.stop] = values

    def put_cross(block, side, values):
        for part in range(tiles):
            rank = starts[block] // tile + part if far else block * tiles + part
            place = place_of(rank) if far and paired else (rank,)
            cross_ref[*place, side] = values[part * tile : (part + 1) * tile]

    blend(
        returned_ref,
        slow_ref.at[:, depth],
        bracket_ref,
        inverse_y,
        scalars_of(held_ref, depth),
        parts,
        None if last else put_wave,
        put_cross,
        starts,
    )


def march_kernel(
    held_ref,
    near_wave,
    far_wave,
    bracket_hbm,
    forward_x_hbm,
    forward_y_hbm,
    inverse_x_hbm,
    out_ref,
    bracket_ref,
    forward_x,
    forward_y,
    inverse_x,
    sems,
    half_ref,
    shift_ref,
    *spectrum,
    depth,
):
    waits = fetch(
        [
            (forward_y_hbm, forward_y),
            (forward_x_hbm, forward_x),
            (inverse_x_hbm, inverse_x),
            (bracket_hbm.at[depth], bracket_ref),
        ],
        sems,
    )
    piece = near_wave.shape[1] // PIECES

    def fill_half(plane):
        for starts, wave_ref in zip(piece_starts(piece), (near_wave, far_wave)):
            half = dot(wave_ref[plane], forward_y[...]).astype(bf16)
            for step, start in enumerate(starts):
                here = pl.ds(pl.multiple_of(start, piece), piece)
                half_ref[plane, here, :] = half[step * piece : (step + 1) * piece]

    march_out(
        fill_half,
        forward_x,
        scalars_of(held_ref, depth),
        half_ref,
        spectrum,
        ready=(waits[:1], waits[1:2]),
    )
    march_back(spectrum, inverse_x, shift_ref, out_ref, waits[2:3])
    waits[3]()


IMAGE_ROWS = 8
PAIR_ORDER = (2, 4, 5, 6, 7, 3, 1)


def lag_kernel(lag_ref, *weight_refs):
    bins, pair, lags = lag_ref.shape
    height = bins * pair * IMAGE_ROWS
    here = lax.axis_index("freq")
    steps = (0, *PAIR_ORDER)
    by_pair = [2 * steps[spot // 2] + spot % 2 for spot in range(bins)] if weight_refs[1:] else None
    for weight_ref, spots, mask in zip(weight_refs, (range(bins), by_pair), (0, here)):
        table = jnp.concatenate(
            [
                jnp.broadcast_to(lag_ref[spot ^ mask][:, None], (pair, IMAGE_ROWS, lags)).reshape(
                    pair * IMAGE_ROWS, lags
                )
                for spot in spots
            ],
            axis=0,
        )
        place = lax.broadcasted_iota(jnp.int32, (height, lags), 0) % IMAGE_ROWS
        for row in range(IMAGE_ROWS):
            weight_ref[:, row * lags : (row + 1) * lags] = jnp.where(
                place == row, table, 0.0
            ).astype(bf16)


def image_kernel(*refs, scale, depth, aliased, count):
    cross_refs, weight_ref = refs[:count], refs[count]
    out_hbm, made_ref, sems = refs[count + 1 + aliased :]
    tile, cols, lags = made_ref.shape
    copies = []
    for group in range(tile // IMAGE_ROWS):
        rows = slice(group * IMAGE_ROWS, (group + 1) * IMAGE_ROWS)
        left = jnp.concatenate(
            [ref[..., rows, :].astype(f32).reshape(-1, cols) for ref in cross_refs], axis=0
        )
        left = left.T.astype(bf16)
        for row in range(IMAGE_ROWS):
            place = group * IMAGE_ROWS + row
            made_ref[place] = dot(left, weight_ref[:, row * lags : (row + 1) * lags]) * scale
            copies.append(
                pltpu.make_async_copy(
                    made_ref.at[place], out_hbm.at[depth, place], sems.at[place]
                )
            )
            copies[-1].start()
    for copy in copies:
        copy.wait()


def pin(value):
    return pltpu.with_memory_space_constraint(value, pltpu.HBM)


def shards(
    source_field,
    receiver_field,
    slowness_slabs,
    slab_map,
    reference_gaps,
    reference_index,
    frequency_bins,
    shot_corner,
    *,
    ranks,
):
    rows, cols = source_field.shape[2:]
    depths = slab_map.shape[0]
    slab_count = slowness_slabs.shape[0]
    half = rows // 2
    piece = half // PIECES
    tile = rows // ranks
    bins = frequency_bins.shape[0]
    slab_shape = slowness_slabs.shape[1:]
    forward_x, inverse_x = real_table(rows)
    forward_x = forward_x.T
    forward_y, inverse_y = real_table(cols)
    inverse_y = inverse_y.T

    hbm = pl.BlockSpec(memory_space=pltpu.HBM)
    vmem = pl.BlockSpec(memory_space=VMEM)
    dma = pltpu.SemaphoreType.DMA

    keep, send = pl.pallas_call(
        window_kernel,
        in_specs=[hbm] * 3,
        out_specs=[vmem] * 2,
        out_shape=[jax.ShapeDtypeStruct((PIECES, depths, piece, cols), bf16)] * 2,
        scratch_shapes=[
            SMEM(slab_map.shape, jnp.int32),
            SMEM(shot_corner.shape, jnp.int32),
            VMEM((1,) + slab_shape, bf16),
            dma((3,)),
        ],
        compiler_params=pltpu.CompilerParams(vmem_limit_bytes=16 << 20),
        name="window",
    )(pin(slab_map), pin(shot_corner), pin(slowness_slabs))

    def swap(value, bit):
        return lax.ppermute(value, "freq", [(i, i ^ bit) for i in range(ranks)])

    held = keep + swap(send, 1)
    early_bins, held = lax.optimization_barrier((frequency_bins, held))
    spectrum_shapes = [
        jax.ShapeDtypeStruct((4, rows, cols), f32),
        jax.ShapeDtypeStruct((3, rows, cols), f32),
        jax.ShapeDtypeStruct((3, rows, cols), f32),
    ]
    returned_shape = jax.ShapeDtypeStruct((3, 4, rows, cols), bf16)
    flops = 2 * 4 * (1 + 3) * rows * rows * cols
    *spectrum, held_scalars = pl.pallas_call(
        out_kernel,
        in_specs=[hbm] * 6,
        out_specs=[vmem] * 4,
        out_shape=spectrum_shapes
        + [jax.ShapeDtypeStruct((8 * pl.cdiv(1 + 3 * depths, 8), cols), f32)],
        scratch_shapes=[
            SMEM(frequency_bins.shape, jnp.int32),
            SMEM(reference_gaps.shape, f32),
            VMEM((4, rows, cols), bf16),
            VMEM((rows, rows), bf16),
            VMEM((cols, cols), bf16),
            VMEM((4, rows, cols), bf16),
            dma((6,)),
        ],
        compiler_params=pltpu.CompilerParams(vmem_limit_bytes=20 << 20),
        cost_estimate=pl.CostEstimate(flops=flops // 2, bytes_accessed=4 << 20, transcendentals=0),
        name="out",
    )(
        *[
            pin(value)
            for value in (
                early_bins,
                reference_gaps,
                source_field,
                receiver_field,
                forward_x,
                forward_y,
            )
        ]
    )
    own = held[0] + sum(swap(held[step], 2 * step) for step in range(1, PIECES))
    own, spectrum = lax.optimization_barrier((own, spectrum))
    returned, bracket, kept_inverse = pl.pallas_call(
        back_kernel,
        in_specs=[vmem] * 3 + [hbm] * 3,
        out_specs=[vmem] * 3,
        out_shape=[
            returned_shape,
            jax.ShapeDtypeStruct((rows, cols), jnp.int32),
            jax.ShapeDtypeStruct((cols, cols), bf16),
        ],
        scratch_shapes=[
            VMEM((rows, rows), bf16),
            VMEM((3, 4, rows, cols), bf16),
            dma((3,)),
        ],
        compiler_params=pltpu.CompilerParams(vmem_limit_bytes=24 << 20),
        cost_estimate=pl.CostEstimate(flops=flops, bytes_accessed=4 << 20, transcendentals=0),
        name="back",
    )(*spectrum, pin(inverse_x), pin(reference_index), pin(inverse_y))
    bit = 2 * PIECES
    while bit < ranks:
        own = own + swap(own, bit)
        bit *= 2
    own, returned = lax.optimization_barrier((own, returned))
    pieces = [own] + [swap(own, 2 * step) for step in range(1, PIECES)]
    part = pl.pallas_call(
        unfold_kernel,
        in_specs=[vmem] * 2,
        out_specs=vmem,
        out_shape=jax.ShapeDtypeStruct((12, rows, cols), f32),
        compiler_params=pltpu.CompilerParams(vmem_limit_bytes=16 << 20),
        cost_estimate=pl.CostEstimate(flops=flops // 2, bytes_accessed=1 << 20, transcendentals=0),
        name="unfold",
    )(returned, kept_inverse)
    pieces, part = lax.optimization_barrier((pieces, part))
    near_slow = jnp.stack(pieces)
    offsets = jnp.arange(LAGS, dtype=jnp.int32) - LAGS // 2
    cycles = jnp.mod(frequency_bins[:, None] * offsets[None, :], period_bins).astype(f32)
    angles = cycles * (2.0 * math.pi / period_bins)
    lag_weights = jnp.stack([jnp.cos(angles), jnp.sin(angles)], axis=1).astype(bf16)

    far_slow, lag_weights = lax.optimization_barrier((swap(near_slow, 1), lag_weights))

    blend_scratch = [VMEM((12, piece, cols), f32)] * 2
    paired = ranks == 2 * (1 + len(PAIR_ORDER)) and depths > 1 and tile % (2 * IMAGE_ROWS) == 0
    wave_shape = jax.ShapeDtypeStruct((4, half, cols), bf16)

    def mix(depth, far, *operands):
        last = depth == depths - 1
        tiles = (ranks // 2,) if not far else (2, ranks // 2) if paired and last else (ranks,)
        return pl.pallas_call(
            functools.partial(
                mix_kernel, depth=depth, far=far, last=last, paired=paired and last
            ),
            in_specs=[vmem] * len(operands),
            out_specs=[vmem] * (2 - last),
            out_shape=[wave_shape] * (1 - last)
            + [jax.ShapeDtypeStruct(tiles + (2, tile, cols), bf16)],
            scratch_shapes=blend_scratch if depth else [],
            compiler_params=pltpu.CompilerParams(vmem_limit_bytes=16 << 20),
            cost_estimate=pl.CostEstimate(
                flops=flops // 4, bytes_accessed=1 << 20, transcendentals=0
            ),
            name="far" if far else "near",
        )(*operands)

    *near_wave, near_cross = mix(0, False, held_scalars, part, near_slow, bracket)
    *far_wave, cross = mix(
        0, True, held_scalars, part, far_slow, bracket, near_cross
    )
    crosses = [cross]
    for depth in range(1, depths):
        returned, bracket = pl.pallas_call(
            functools.partial(march_kernel, depth=depth),
            in_specs=[vmem] * 3 + [hbm] * 4,
            out_specs=[vmem] * 2,
            out_shape=[returned_shape, jax.ShapeDtypeStruct((rows, cols), jnp.int32)],
            scratch_shapes=[
                VMEM((rows, rows), bf16),
                VMEM((cols, cols), bf16),
                VMEM((rows, rows), bf16),
                dma((4,)),
                VMEM((4, rows, cols), bf16),
                VMEM((3, 4, rows, cols), bf16),
                *[VMEM(shape.shape, f32) for shape in spectrum_shapes],
            ],
            compiler_params=pltpu.CompilerParams(vmem_limit_bytes=28 << 20),
            cost_estimate=pl.CostEstimate(
                flops=3 * flops // 2, bytes_accessed=8 << 20, transcendentals=0
            ),
            name="march",
        )(
            held_scalars,
            *near_wave,
            *far_wave,
            pin(reference_index),
            pin(forward_x),
            pin(forward_y),
            pin(inverse_x),
        )
        *near_wave, near_cross = mix(
            depth, False, held_scalars, returned, near_slow, bracket, kept_inverse
        )
        *far_wave, cross = mix(
            depth, True, held_scalars, returned, far_slow, bracket, kept_inverse, near_cross
        )
        crosses.append(cross)

    scale = bins ** (-0.5)
    def exchange(value):
        return lax.all_to_all(value, "freq", split_axis=0, concat_axis=0, tiled=True)

    if not paired:
        arrivals = [[exchange(cross)] for cross in crosses]
    else:
        arrivals = [[exchange(cross)] for cross in crosses[:-1]]
        by_core = crosses[-1]
        by_chip = jnp.stack([by_core[0], swap(by_core[1], 1)], axis=1)
        arrivals.append([by_chip[0]] + [swap(by_chip[step], 2 * step) for step in PAIR_ORDER])
    if tile % (2 * IMAGE_ROWS):
        summed = jnp.einsum(
            "dwcab,wcl->dabl",
            jnp.stack([arrived for (arrived,) in arrivals]),
            lag_weights,
            preferred_element_type=f32,
        )
        return summed * scale
    height = bins * 2 * IMAGE_ROWS
    weights = pl.pallas_call(
        lag_kernel,
        in_specs=[vmem],
        out_specs=[vmem] * (1 + paired),
        out_shape=[jax.ShapeDtypeStruct((height, IMAGE_ROWS * LAGS), bf16)] * (1 + paired),
        compiler_params=pltpu.CompilerParams(vmem_limit_bytes=16 << 20),
        name="lag",
    )(lag_weights.astype(f32))
    image = None
    for depth, arrived in enumerate(arrivals):
        aliased = image is not None
        count = len(arrived)
        image = pl.pallas_call(
            functools.partial(
                image_kernel, scale=scale, depth=depth, aliased=aliased, count=count
            ),
            in_specs=[vmem] * (count + 1) + [hbm] * aliased,
            out_specs=hbm,
            out_shape=jax.ShapeDtypeStruct((depths, tile, cols, LAGS), f32),
            scratch_shapes=[VMEM((tile, cols, LAGS), f32), dma((tile,))],
            input_output_aliases={count + 1: 0} if aliased else {},
            compiler_params=pltpu.CompilerParams(vmem_limit_bytes=28 << 20),
            name="image",
        )(*arrived, weights[count > 1], *([image] if aliased else []))
    return image


def solution(mesh):
    placed = (
        P("grp", "freq", None, None),
        P("grp", "freq", None, None),
        P(("grp", "freq"), None, None),
        P("grp"),
        P("grp", None),
        P("grp", None, None),
        P(),
        P("grp"),
    )
    return jax.shard_map(
        functools.partial(shards, ranks=mesh.shape["freq"]),
        mesh=mesh,
        in_specs=placed,
        out_specs=P("grp", "freq", None, None),
        check_vma=False,
    )
```

```python
import functools
import math

import jax
import jax.numpy as jnp
import numpy as np
from jax import lax
from jax.experimental import pallas as pl
from jax.experimental.pallas import tpu as pltpu
from jax.sharding import PartitionSpec as P

LAGS = 256

cell_width = 0.0125
layer_thick = 0.0125
bin_hertz = 0.5
period_bins = 500
slow_base = 0.3

VMEM = pltpu.VMEM
SMEM = pltpu.SMEM
f32 = jnp.float32
bf16 = jnp.bfloat16


def real_table(length):
    half = length // 2
    steps = np.arange(length, dtype=np.int64)
    wave = np.concatenate([np.arange(half), [half], np.arange(1, half)])
    phases = np.mod(steps[:, None] * wave[None, :], length).astype(np.float32)
    angles = phases * np.float32(2.0 * math.pi / length)
    scale = np.float32(1.0 / math.sqrt(length))
    is_cos = np.arange(length) <= half
    table = np.where(is_cos[None, :], np.cos(angles), np.sin(angles)) * scale
    twice = np.where((wave == 0) | (wave == half), 1.0, 2.0)
    forward = jnp.asarray(table.astype(np.float32)).astype(bf16)
    inverse = (forward.astype(f32) * jnp.asarray(twice[None, :], f32)).astype(bf16)
    return forward, inverse


def sin_cos(angle):
    turns = jnp.floor(angle * (2.0 / math.pi) + 0.5)
    rest = angle - turns * 1.5707397460937500
    rest = rest - turns * 5.6580702948965924e-05
    quadrant = turns.astype(jnp.int32)
    square = rest * rest
    sine = rest + rest * square * (
        -1.6666654611e-1 + square * (8.3321608736e-3 - square * 1.9515295891e-4)
    )
    cosine = (
        1.0
        - 0.5 * square
        + square
        * square
        * (4.166664568298827e-2 + square * (-1.388731625493765e-3 + square * 2.443315711809948e-5))
    )
    odd = (quadrant & 1) == 1
    out_sin = jnp.where(odd, cosine, sine)
    out_cos = jnp.where(odd, sine, cosine)
    out_sin = jnp.where((quadrant & 2) == 2, -out_sin, out_sin)
    out_cos = jnp.where(((quadrant + 1) & 2) == 2, -out_cos, out_cos)
    return out_sin, out_cos


def references_of(gaps_ref, depth):
    first = slow_base + gaps_ref[depth, 0]
    second = first + gaps_ref[depth, 1]
    third = second + gaps_ref[depth, 2]
    return first, second, third


def scalars_of(held_ref, depth):
    rows = [held_ref[row : row + 1] for row in (0, *range(1 + 3 * depth, 4 + 3 * depth))]
    return rows[0], tuple(rows[1:])


def angular_of(bins_ref):
    return bins_ref[lax.axis_index("freq")].astype(f32) * (2.0 * math.pi * bin_hertz)


def phase_block(reach, base_turn, squares):
    radicand = reach - squares
    root = jnp.sqrt(jnp.abs(radicand)) * layer_thick
    travelling = radicand > 0.0
    fading = jnp.where(travelling, 1.0, jnp.exp(-root))
    sine, cosine = sin_cos(jnp.where(travelling, root, 0.0) - base_turn)
    return fading * cosine, fading * sine


def make_phases(cos_ref, sin_ref, angular, reference):
    rows, cols = cos_ref.shape
    half = rows // 2
    reach = (angular * reference) * (angular * reference)
    base_turn = angular * layer_thick * reference
    step_x = 2.0 * math.pi / (rows * cell_width)
    step_y = 2.0 * math.pi / (cols * cell_width)
    lane = lax.broadcasted_iota(jnp.int32, (8, cols), 1)
    wave_y = jnp.where(lane <= cols // 2, lane, lane - cols // 2).astype(f32) * step_y
    square_y = wave_y * wave_y
    tall = 64

    def body(block, carry):
        start = pl.multiple_of(block * tall, tall)
        row = lax.broadcasted_iota(jnp.int32, (tall, cols), 0) + start
        wave_x = row.astype(f32) * step_x
        cosine, sine = phase_block(
            reach, base_turn, wave_x * wave_x + jnp.concatenate([square_y] * (tall // 8), axis=0)
        )
        cos_ref[pl.ds(start, tall), :] = cosine
        sin_ref[pl.ds(start, tall), :] = sine
        cos_ref[pl.ds(half + start, tall), :] = cosine
        sin_ref[pl.ds(half + start, tall), :] = sine
        return carry

    lax.fori_loop(0, half // tall, body, 0)
    edge = (half * step_x) ** 2
    cosine, sine = phase_block(reach, base_turn, edge + square_y)
    top = lax.broadcasted_iota(jnp.int32, (8, cols), 0) == 0
    cos_ref[half : half + 8, :] = jnp.where(top, cosine, cos_ref[half : half + 8, :])
    sin_ref[half : half + 8, :] = jnp.where(top, sine, sin_ref[half : half + 8, :])


def dot(left, right):
    return jnp.dot(left, right, preferred_element_type=f32)


def march_out(fill_half, forward_x, scalars, half_ref, spectrum, ready=((), ())):
    angular, references = scalars
    spec_ref, cos_ref, sin_ref = spectrum
    for j in range(3):
        make_phases(cos_ref.at[j], sin_ref.at[j], angular, references[j])
    for wait in ready[0]:
        wait()
    for plane in range(4):
        fill_half(plane)
    for wait in ready[1]:
        wait()
    for plane in range(4):
        spec_ref[plane] = dot(forward_x[...], half_ref[plane])


def march_back(spectrum, inverse_x, shift_ref, out_ref, ready=()):
    spec_ref, cos_ref, sin_ref = spectrum
    for j in range(3):
        for field in range(2):
            real, imag = spec_ref[2 * field], spec_ref[2 * field + 1]
            cosine, sine = cos_ref[j], sin_ref[j]
            shift_ref[j, 2 * field] = (cosine * real - sine * imag).astype(bf16)
            shift_ref[j, 2 * field + 1] = (cosine * imag + sine * real).astype(bf16)
        if j == 0:
            for wait in ready:
                wait()
        for plane in range(4):
            out_ref[j, plane] = dot(inverse_x[...], shift_ref[j, plane]).astype(bf16)


def blend(returned_ref, slow_ref, bracket_ref, inverse_y, scalars, parts, put_wave, put_cross, starts):
    tall, cols = slow_ref.shape[1:]
    chunk = 16
    angular, (low, mid, high) = scalars
    slope_low = 1.0 / (mid - low)
    slope_high = 1.0 / (high - mid)
    def first_row(block):
        return pl.multiple_of(starts[block], tall)

    def fill(part_ref, block):
        left = returned_ref[:, :, pl.ds(first_row(block), tall), :].reshape(12 * tall, cols)
        part_ref[...] = dot(left, inverse_y[...]).reshape(12, tall, cols)

    def mix(part_ref, block):
        start = first_row(block)
        crossed = []
        for piece in range(tall // chunk):
            within = slice(piece * chunk, (piece + 1) * chunk)
            here = pl.ds(pl.multiple_of(start + piece * chunk, chunk), chunk)
            slow = slow_ref[block, within].astype(f32)
            lower = bracket_ref[here, :] == 0
            weight = jnp.where(lower, (slow - low) * slope_low, (slow - mid) * slope_high)
            weight = jnp.minimum(jnp.maximum(weight, 0.0), 1.0)
            sine, cosine = sin_cos(slow * (angular * layer_thick))
            halves = []
            for plane in range(4):
                if inverse_y is None:
                    first, second, third = [returned_ref[4 * j + plane, here] for j in range(3)]
                else:
                    first, second, third = [part_ref[4 * j + plane, within] for j in range(3)]
                bottom = jnp.where(lower, first, second)
                top = jnp.where(lower, second, third)
                halves.append(bottom + weight * (top - bottom))
            fresh = []
            for field in range(2):
                real, imag = halves[2 * field], halves[2 * field + 1]
                fresh.append((cosine * real - sine * imag).astype(bf16))
                fresh.append((cosine * imag + sine * real).astype(bf16))
            if put_wave is not None:
                for plane in range(4):
                    put_wave(block, within, plane, fresh[plane])
            s_real, s_imag, r_real, r_imag = [value.astype(f32) for value in fresh]
            crossed.append(
                (
                    (s_real * r_real - s_imag * r_imag).astype(bf16),
                    (s_real * r_imag + s_imag * r_real).astype(bf16),
                )
            )
        for side in range(2):
            put_cross(block, side, jnp.concatenate([pair[side] for pair in crossed], axis=0))

    if inverse_y is None:
        for block in range(len(starts)):
            mix(None, block)
        return
    even, odd = parts
    fill(even, 0)
    for block in range(len(starts)):
        here, other = (even, odd) if block % 2 == 0 else (odd, even)
        if block + 1 < len(starts):
            fill(other, block + 1)
        mix(here, block)


PIECES = 4


def piece_starts(piece):
    rank = lax.axis_index("freq")
    core, place = rank % 2, (rank // 2) % PIECES
    return [
        [(side * PIECES + (place ^ step)) * piece for step in range(PIECES)]
        for side in (core, 1 - core)
    ]


def window_kernel(
    map_hbm, corner_hbm, slab_hbm, keep_ref, send_ref, map_ref, corner_ref, slab_ref, sems
):
    depths, piece, cols = keep_ref.shape[1:]
    slab_count = slab_hbm.shape[0]
    tall, wide = slab_hbm.shape[1:]
    copies = [
        pltpu.make_async_copy(map_hbm, map_ref, sems.at[0]),
        pltpu.make_async_copy(corner_hbm, corner_ref, sems.at[1]),
    ]
    for copy in copies:
        copy.start()
    if slab_count == 1:
        whole = pltpu.make_async_copy(slab_hbm.at[0], slab_ref.at[0], sems.at[2])
        whole.start()
    for copy in copies:
        copy.wait()
    if slab_count == 1:
        whole.wait()
    rank = lax.axis_index("freq")
    rows = 2 * PIECES * piece
    first_row = jnp.minimum((corner_ref[0] // 16) * 16, tall - rows - 16)
    first_col = jnp.minimum((corner_ref[1] // 128) * 128, wide - cols - 128)
    above = corner_ref[0] - first_row
    before = corner_ref[1] - first_col
    reach = piece + 16
    span = cols + 128
    for depth in range(depths):
        slab = map_ref[depth]
        mine = slab // slab_count == rank

        @pl.when(mine)
        def _():
            if slab_count == 1:
                here = slab_ref.at[0]
            else:
                here = slab_ref.at[0]
                copy = pltpu.make_async_copy(
                    slab_hbm.at[lax.rem(slab, slab_count)], here, sems.at[2]
                )
                copy.start()
                copy.wait()
            for target, starts in zip((keep_ref, send_ref), piece_starts(piece)):
                for step, start in enumerate(starts):
                    block = here[
                        pl.ds(pl.multiple_of(first_row + start, 16), reach),
                        pl.ds(pl.multiple_of(first_col, 128), span),
                    ].astype(f32)
                    block = pltpu.roll(block, lax.rem(span - before, span), 1)[:, :cols]
                    block = pltpu.roll(block, lax.rem(reach - above, reach), 0)[:piece]
                    target[step, depth] = block.astype(bf16)

        @pl.when(jnp.logical_not(mine))
        def _():
            for target in (keep_ref, send_ref):
                target[:, depth] = jnp.zeros((PIECES, piece, cols), bf16)


def fetch(pairs, sems):
    copies = [
        pltpu.make_async_copy(source, target, sems.at[index])
        for index, (source, target) in enumerate(pairs)
    ]
    for copy in copies:
        copy.start()
    return [copy.wait for copy in copies]


def out_kernel(
    bins_hbm,
    gaps_hbm,
    source_hbm,
    receiver_hbm,
    forward_x_hbm,
    forward_y_hbm,
    spec_ref,
    cos_ref,
    sin_ref,
    held_ref,
    bins_ref,
    gaps_ref,
    wave_ref,
    forward_x,
    forward_y,
    half_ref,
    sems,
):
    waits = fetch(
        [
            (bins_hbm, bins_ref),
            (gaps_hbm, gaps_ref),
            (forward_y_hbm, forward_y),
            (source_hbm.at[:, 0], wave_ref.at[0:2]),
            (receiver_hbm.at[:, 0], wave_ref.at[2:4]),
            (forward_x_hbm, forward_x),
        ],
        sems,
    )
    waits[0]()
    waits[1]()
    angular = angular_of(bins_ref)
    held_ref[0:1] = jnp.full((1, held_ref.shape[1]), angular, f32)
    for depth in range(gaps_ref.shape[0]):
        for j, reference in enumerate(references_of(gaps_ref, depth)):
            row = 1 + 3 * depth + j
            held_ref[row : row + 1] = jnp.full((1, held_ref.shape[1]), reference, f32)

    def fill_half(plane):
        half = dot(wave_ref[plane], forward_y[...])
        half_ref[plane] = (half if plane < 3 else -half).astype(bf16)

    march_out(
        fill_half,
        forward_x,
        (angular, references_of(gaps_ref, 0)),
        half_ref,
        (spec_ref, cos_ref, sin_ref),
        ready=(waits[2:5], waits[5:]),
    )


def back_kernel(
    spec_ref,
    cos_ref,
    sin_ref,
    inverse_x_hbm,
    bracket_hbm,
    inverse_y_hbm,
    out_ref,
    bracket_ref,
    inverse_y,
    inverse_x,
    shift_ref,
    sems,
):
    waits = fetch(
        [
            (inverse_x_hbm, inverse_x),
            (bracket_hbm.at[0], bracket_ref),
            (inverse_y_hbm, inverse_y),
        ],
        sems,
    )
    march_back((spec_ref, cos_ref, sin_ref), inverse_x, shift_ref, out_ref, waits[:1])
    for wait in waits[1:]:
        wait()


def unfold_kernel(returned_ref, inverse_y, part_ref):
    rows, cols = returned_ref.shape[2:]
    for j in range(3):
        for plane in range(4):
            part_ref[4 * j + plane] = dot(returned_ref[j, plane], inverse_y[...])


def place_of(rank):
    here = lax.axis_index("freq")
    return (rank ^ here) % 2, (rank // 2) ^ (here // 2)


def mix_kernel(*refs, depth, far, last, paired):
    held_ref, returned_ref, slow_ref, bracket_ref = refs[:4]
    inverse_y, rest = (None, refs[4:]) if depth == 0 else (refs[4], refs[5:])
    if far:
        near_cross, rest = rest[0], rest[1:]
    if not last:
        wave_ref, rest = rest[0], rest[1:]
    cross_ref, *parts = rest
    piece = slow_ref.shape[2]
    tile = cross_ref.shape[-2]
    tiles = piece // tile
    near_starts, far_starts = piece_starts(piece)
    starts = far_starts if far else near_starts
    if far:
        for step, start in enumerate(near_starts):
            if paired:
                for part in range(tiles):
                    cross_ref[place_of(start // tile + part)] = near_cross[step * tiles + part]
                continue
            cross_ref[pl.ds(start // tile, tiles)] = near_cross[step * tiles : (step + 1) * tiles]

    def put_wave(block, within, plane, values):
        wave_ref[plane, block * piece + within.start : block * piece + within.stop] = values

    def put_cross(block, side, values):
        for part in range(tiles):
            rank = starts[block] // tile + part if far else block * tiles + part
            place = place_of(rank) if far and paired else (rank,)
            cross_ref[*place, side] = values[part * tile : (part + 1) * tile]

    blend(
        returned_ref,
        slow_ref.at[:, depth],
        bracket_ref,
        inverse_y,
        scalars_of(held_ref, depth),
        parts,
        None if last else put_wave,
        put_cross,
        starts,
    )


def pair_mix_kernel(
    held_ref, returned_ref, near_slow, far_slow, bracket_ref, inverse_y, cross_ref, even, odd, *, depth
):
    piece = near_slow.shape[2]
    tile = cross_ref.shape[-2]
    for slow_ref, starts in zip((near_slow, far_slow), piece_starts(piece)):

        def put_cross(block, side, values, starts=starts):
            for part in range(piece // tile):
                place = place_of(starts[block] // tile + part)
                cross_ref[*place, side] = values[part * tile : (part + 1) * tile]

        blend(
            returned_ref,
            slow_ref.at[:, depth],
            bracket_ref,
            inverse_y,
            scalars_of(held_ref, depth),
            (even, odd),
            None,
            put_cross,
            starts,
        )


def march_kernel(
    held_ref,
    near_wave,
    far_wave,
    bracket_hbm,
    forward_x_hbm,
    forward_y_hbm,
    inverse_x_hbm,
    out_ref,
    bracket_ref,
    forward_x,
    forward_y,
    inverse_x,
    sems,
    half_ref,
    shift_ref,
    *spectrum,
    depth,
):
    waits = fetch(
        [
            (forward_y_hbm, forward_y),
            (forward_x_hbm, forward_x),
            (inverse_x_hbm, inverse_x),
            (bracket_hbm.at[depth], bracket_ref),
        ],
        sems,
    )
    piece = near_wave.shape[1] // PIECES

    def fill_half(plane):
        for starts, wave_ref in zip(piece_starts(piece), (near_wave, far_wave)):
            half = dot(wave_ref[plane], forward_y[...]).astype(bf16)
            for step, start in enumerate(starts):
                here = pl.ds(pl.multiple_of(start, piece), piece)
                half_ref[plane, here, :] = half[step * piece : (step + 1) * piece]

    march_out(
        fill_half,
        forward_x,
        scalars_of(held_ref, depth),
        half_ref,
        spectrum,
        ready=(waits[:1], waits[1:2]),
    )
    march_back(spectrum, inverse_x, shift_ref, out_ref, waits[2:3])
    waits[3]()


IMAGE_ROWS = 8
PAIR_ORDER = (3, 4, 5, 6, 7, 2, 1)


def lag_kernel(lag_ref, *weight_refs):
    bins, pair, lags = lag_ref.shape
    height = bins * pair * IMAGE_ROWS
    here = lax.axis_index("freq")
    steps = (0, *PAIR_ORDER)
    by_pair = [2 * steps[spot // 2] + spot % 2 for spot in range(bins)] if weight_refs[1:] else None
    for weight_ref, spots, mask in zip(weight_refs, (range(bins), by_pair), (0, here)):
        table = jnp.concatenate(
            [
                jnp.broadcast_to(lag_ref[spot ^ mask][:, None], (pair, IMAGE_ROWS, lags)).reshape(
                    pair * IMAGE_ROWS, lags
                )
                for spot in spots
            ],
            axis=0,
        )
        place = lax.broadcasted_iota(jnp.int32, (height, lags), 0) % IMAGE_ROWS
        for row in range(IMAGE_ROWS):
            weight_ref[:, row * lags : (row + 1) * lags] = jnp.where(
                place == row, table, 0.0
            ).astype(bf16)


def image_kernel(*refs, scale, depth, aliased, count):
    cross_refs, weight_ref = refs[:count], refs[count]
    out_hbm, made_ref, sems = refs[count + 1 + aliased :]
    tile, cols, lags = made_ref.shape
    copies = []
    for group in range(tile // IMAGE_ROWS):
        rows = slice(group * IMAGE_ROWS, (group + 1) * IMAGE_ROWS)
        left = jnp.concatenate(
            [ref[..., rows, :].astype(f32).reshape(-1, cols) for ref in cross_refs], axis=0
        )
        left = left.T.astype(bf16)
        for row in range(IMAGE_ROWS):
            place = group * IMAGE_ROWS + row
            made_ref[place] = dot(left, weight_ref[:, row * lags : (row + 1) * lags]) * scale
            copies.append(
                pltpu.make_async_copy(
                    made_ref.at[place], out_hbm.at[depth, place], sems.at[place]
                )
            )
            copies[-1].start()
    for copy in copies:
        copy.wait()


def pin(value):
    return pltpu.with_memory_space_constraint(value, pltpu.HBM)


def shards(
    source_field,
    receiver_field,
    slowness_slabs,
    slab_map,
    reference_gaps,
    reference_index,
    frequency_bins,
    shot_corner,
    *,
    ranks,
):
    rows, cols = source_field.shape[2:]
    depths = slab_map.shape[0]
    slab_count = slowness_slabs.shape[0]
    half = rows // 2
    piece = half // PIECES
    tile = rows // ranks
    bins = frequency_bins.shape[0]
    slab_shape = slowness_slabs.shape[1:]
    forward_x, inverse_x = real_table(rows)
    forward_x = forward_x.T
    forward_y, inverse_y = real_table(cols)
    inverse_y = inverse_y.T

    hbm = pl.BlockSpec(memory_space=pltpu.HBM)
    vmem = pl.BlockSpec(memory_space=VMEM)
    dma = pltpu.SemaphoreType.DMA

    keep, send = pl.pallas_call(
        window_kernel,
        in_specs=[hbm] * 3,
        out_specs=[vmem] * 2,
        out_shape=[jax.ShapeDtypeStruct((PIECES, depths, piece, cols), bf16)] * 2,
        scratch_shapes=[
            SMEM(slab_map.shape, jnp.int32),
            SMEM(shot_corner.shape, jnp.int32),
            VMEM((1,) + slab_shape, bf16),
            dma((3,)),
        ],
        compiler_params=pltpu.CompilerParams(vmem_limit_bytes=16 << 20),
        name="window",
    )(pin(slab_map), pin(shot_corner), pin(slowness_slabs))

    def swap(value, bit):
        return lax.ppermute(value, "freq", [(i, i ^ bit) for i in range(ranks)])

    held = keep + swap(send, 1)
    early_bins, held = lax.optimization_barrier((frequency_bins, held))
    spectrum_shapes = [
        jax.ShapeDtypeStruct((4, rows, cols), f32),
        jax.ShapeDtypeStruct((3, rows, cols), f32),
        jax.ShapeDtypeStruct((3, rows, cols), f32),
    ]
    returned_shape = jax.ShapeDtypeStruct((3, 4, rows, cols), bf16)
    flops = 2 * 4 * (1 + 3) * rows * rows * cols
    *spectrum, held_scalars = pl.pallas_call(
        out_kernel,
        in_specs=[hbm] * 6,
        out_specs=[vmem] * 4,
        out_shape=spectrum_shapes
        + [jax.ShapeDtypeStruct((8 * pl.cdiv(1 + 3 * depths, 8), cols), f32)],
        scratch_shapes=[
            SMEM(frequency_bins.shape, jnp.int32),
            SMEM(reference_gaps.shape, f32),
            VMEM((4, rows, cols), bf16),
            VMEM((rows, rows), bf16),
            VMEM((cols, cols), bf16),
            VMEM((4, rows, cols), bf16),
            dma((6,)),
        ],
        compiler_params=pltpu.CompilerParams(vmem_limit_bytes=20 << 20),
        cost_estimate=pl.CostEstimate(flops=flops // 2, bytes_accessed=4 << 20, transcendentals=0),
        name="out",
    )(
        *[
            pin(value)
            for value in (
                early_bins,
                reference_gaps,
                source_field,
                receiver_field,
                forward_x,
                forward_y,
            )
        ]
    )
    own = held[0] + sum(swap(held[step], 2 * step) for step in range(1, PIECES))
    own, spectrum = lax.optimization_barrier((own, spectrum))
    returned, bracket, kept_inverse = pl.pallas_call(
        back_kernel,
        in_specs=[vmem] * 3 + [hbm] * 3,
        out_specs=[vmem] * 3,
        out_shape=[
            returned_shape,
            jax.ShapeDtypeStruct((rows, cols), jnp.int32),
            jax.ShapeDtypeStruct((cols, cols), bf16),
        ],
        scratch_shapes=[
            VMEM((rows, rows), bf16),
            VMEM((3, 4, rows, cols), bf16),
            dma((3,)),
        ],
        compiler_params=pltpu.CompilerParams(vmem_limit_bytes=24 << 20),
        cost_estimate=pl.CostEstimate(flops=flops, bytes_accessed=4 << 20, transcendentals=0),
        name="back",
    )(*spectrum, pin(inverse_x), pin(reference_index), pin(inverse_y))
    bit = 2 * PIECES
    while bit < ranks:
        own = own + swap(own, bit)
        bit *= 2
    own, returned = lax.optimization_barrier((own, returned))
    pieces = [own] + [swap(own, 2 * step) for step in range(1, PIECES)]
    part = pl.pallas_call(
        unfold_kernel,
        in_specs=[vmem] * 2,
        out_specs=vmem,
        out_shape=jax.ShapeDtypeStruct((12, rows, cols), f32),
        compiler_params=pltpu.CompilerParams(vmem_limit_bytes=16 << 20),
        cost_estimate=pl.CostEstimate(flops=flops // 2, bytes_accessed=1 << 20, transcendentals=0),
        name="unfold",
    )(returned, kept_inverse)
    pieces, part = lax.optimization_barrier((pieces, part))
    near_slow = jnp.stack(pieces)
    offsets = jnp.arange(LAGS, dtype=jnp.int32) - LAGS // 2
    cycles = jnp.mod(frequency_bins[:, None] * offsets[None, :], period_bins).astype(f32)
    angles = cycles * (2.0 * math.pi / period_bins)
    lag_weights = jnp.stack([jnp.cos(angles), jnp.sin(angles)], axis=1).astype(bf16)

    far_slow, lag_weights = lax.optimization_barrier((swap(near_slow, 1), lag_weights))

    blend_scratch = [VMEM((12, piece, cols), f32)] * 2
    paired = ranks == 2 * (1 + len(PAIR_ORDER)) and depths > 1 and tile % (2 * IMAGE_ROWS) == 0
    wave_shape = jax.ShapeDtypeStruct((4, half, cols), bf16)

    def mix(depth, far, *operands):
        last = depth == depths - 1
        tiles = (ranks // 2,) if not far else (2, ranks // 2) if paired and last else (ranks,)
        return pl.pallas_call(
            functools.partial(
                mix_kernel, depth=depth, far=far, last=last, paired=paired and last
            ),
            in_specs=[vmem] * len(operands),
            out_specs=[vmem] * (2 - last),
            out_shape=[wave_shape] * (1 - last)
            + [jax.ShapeDtypeStruct(tiles + (2, tile, cols), bf16)],
            scratch_shapes=blend_scratch if depth else [],
            compiler_params=pltpu.CompilerParams(vmem_limit_bytes=16 << 20),
            cost_estimate=pl.CostEstimate(
                flops=flops // 4, bytes_accessed=1 << 20, transcendentals=0
            ),
            name="far" if far else "near",
        )(*operands)

    *near_wave, near_cross = mix(0, False, held_scalars, part, near_slow, bracket)
    *far_wave, cross = mix(
        0, True, held_scalars, part, far_slow, bracket, near_cross
    )
    crosses = [cross]
    for depth in range(1, depths):
        returned, bracket = pl.pallas_call(
            functools.partial(march_kernel, depth=depth),
            in_specs=[vmem] * 3 + [hbm] * 4,
            out_specs=[vmem] * 2,
            out_shape=[returned_shape, jax.ShapeDtypeStruct((rows, cols), jnp.int32)],
            scratch_shapes=[
                VMEM((rows, rows), bf16),
                VMEM((cols, cols), bf16),
                VMEM((rows, rows), bf16),
                dma((4,)),
                VMEM((4, rows, cols), bf16),
                VMEM((3, 4, rows, cols), bf16),
                *[VMEM(shape.shape, f32) for shape in spectrum_shapes],
            ],
            compiler_params=pltpu.CompilerParams(vmem_limit_bytes=28 << 20),
            cost_estimate=pl.CostEstimate(
                flops=3 * flops // 2, bytes_accessed=8 << 20, transcendentals=0
            ),
            name="march",
        )(
            held_scalars,
            *near_wave,
            *far_wave,
            pin(reference_index),
            pin(forward_x),
            pin(forward_y),
            pin(inverse_x),
        )
        if paired and depth == depths - 1:
            cross = pl.pallas_call(
                functools.partial(pair_mix_kernel, depth=depth),
                in_specs=[vmem] * 6,
                out_specs=vmem,
                out_shape=jax.ShapeDtypeStruct((2, ranks // 2, 2, tile, cols), bf16),
                scratch_shapes=blend_scratch,
                compiler_params=pltpu.CompilerParams(vmem_limit_bytes=16 << 20),
                cost_estimate=pl.CostEstimate(
                    flops=flops // 2, bytes_accessed=1 << 20, transcendentals=0
                ),
                name="mix",
            )(held_scalars, returned, near_slow, far_slow, bracket, kept_inverse)
        else:
            *near_wave, near_cross = mix(
                depth, False, held_scalars, returned, near_slow, bracket, kept_inverse
            )
            *far_wave, cross = mix(
                depth, True, held_scalars, returned, far_slow, bracket, kept_inverse, near_cross
            )
        crosses.append(cross)

    scale = bins ** (-0.5)
    def exchange(value):
        return lax.all_to_all(value, "freq", split_axis=0, concat_axis=0, tiled=True)

    if not paired:
        arrivals = [[exchange(cross)] for cross in crosses]
    else:
        arrivals = [[exchange(cross)] for cross in crosses[:-1]]
        by_core = crosses[-1]
        by_chip = jnp.stack([by_core[0], swap(by_core[1], 1)], axis=1)
        arrivals.append([by_chip[0]] + [swap(by_chip[step], 2 * step) for step in PAIR_ORDER])
    if tile % (2 * IMAGE_ROWS):
        summed = jnp.einsum(
            "dwcab,wcl->dabl",
            jnp.stack([arrived for (arrived,) in arrivals]),
            lag_weights,
            preferred_element_type=f32,
        )
        return summed * scale
    height = bins * 2 * IMAGE_ROWS
    weights = pl.pallas_call(
        lag_kernel,
        in_specs=[vmem],
        out_specs=[vmem] * (1 + paired),
        out_shape=[jax.ShapeDtypeStruct((height, IMAGE_ROWS * LAGS), bf16)] * (1 + paired),
        compiler_params=pltpu.CompilerParams(vmem_limit_bytes=16 << 20),
        name="lag",
    )(lag_weights.astype(f32))
    image = None
    for depth, arrived in enumerate(arrivals):
        aliased = image is not None
        count = len(arrived)
        image = pl.pallas_call(
            functools.partial(
                image_kernel, scale=scale, depth=depth, aliased=aliased, count=count
            ),
            in_specs=[vmem] * (count + 1) + [hbm] * aliased,
            out_specs=hbm,
            out_shape=jax.ShapeDtypeStruct((depths, tile, cols, LAGS), f32),
            scratch_shapes=[VMEM((tile, cols, LAGS), f32), dma((tile,))],
            input_output_aliases={count + 1: 0} if aliased else {},
            compiler_params=pltpu.CompilerParams(vmem_limit_bytes=28 << 20),
            name="image",
        )(*arrived, weights[count > 1], *([image] if aliased else []))
    return image


def solution(mesh):
    placed = (
        P("grp", "freq", None, None),
        P("grp", "freq", None, None),
        P(("grp", "freq"), None, None),
        P("grp"),
        P("grp", None),
        P("grp", None, None),
        P(),
        P("grp"),
    )
    return jax.shard_map(
        functools.partial(shards, ranks=mesh.shape["freq"]),
        mesh=mesh,
        in_specs=placed,
        out_specs=P("grp", "freq", None, None),
        check_vma=False,
    )
```

```python
import functools
import math

import jax
import jax.numpy as jnp
import numpy as np
from jax import lax
from jax.experimental import pallas as pl
from jax.experimental.pallas import tpu as pltpu
from jax.sharding import PartitionSpec as P

LAGS = 256

cell_width = 0.0125
layer_thick = 0.0125
bin_hertz = 0.5
period_bins = 500
slow_base = 0.3

VMEM = pltpu.VMEM
SMEM = pltpu.SMEM
f32 = jnp.float32
bf16 = jnp.bfloat16


def real_table(length):
    half = length // 2
    steps = np.arange(length, dtype=np.int64)
    wave = np.concatenate([np.arange(half), [half], np.arange(1, half)])
    phases = np.mod(steps[:, None] * wave[None, :], length).astype(np.float32)
    angles = phases * np.float32(2.0 * math.pi / length)
    scale = np.float32(1.0 / math.sqrt(length))
    is_cos = np.arange(length) <= half
    table = np.where(is_cos[None, :], np.cos(angles), np.sin(angles)) * scale
    twice = np.where((wave == 0) | (wave == half), 1.0, 2.0)
    forward = jnp.asarray(table.astype(np.float32)).astype(bf16)
    inverse = (forward.astype(f32) * jnp.asarray(twice[None, :], f32)).astype(bf16)
    return forward, inverse


def sin_cos(angle):
    turns = jnp.floor(angle * (2.0 / math.pi) + 0.5)
    rest = angle - turns * 1.5707397460937500
    rest = rest - turns * 5.6580702948965924e-05
    quadrant = turns.astype(jnp.int32)
    square = rest * rest
    sine = rest + rest * square * (
        -1.6666654611e-1 + square * (8.3321608736e-3 - square * 1.9515295891e-4)
    )
    cosine = (
        1.0
        - 0.5 * square
        + square
        * square
        * (4.166664568298827e-2 + square * (-1.388731625493765e-3 + square * 2.443315711809948e-5))
    )
    odd = (quadrant & 1) == 1
    out_sin = jnp.where(odd, cosine, sine)
    out_cos = jnp.where(odd, sine, cosine)
    out_sin = jnp.where((quadrant & 2) == 2, -out_sin, out_sin)
    out_cos = jnp.where(((quadrant + 1) & 2) == 2, -out_cos, out_cos)
    return out_sin, out_cos


def references_of(gaps_ref, depth):
    first = slow_base + gaps_ref[depth, 0]
    second = first + gaps_ref[depth, 1]
    third = second + gaps_ref[depth, 2]
    return first, second, third


def scalars_of(held_ref, depth):
    rows = [held_ref[row : row + 1] for row in (0, *range(1 + 3 * depth, 4 + 3 * depth))]
    return rows[0], tuple(rows[1:])


def angular_of(bins_ref):
    return bins_ref[lax.axis_index("freq")].astype(f32) * (2.0 * math.pi * bin_hertz)


def phase_block(reach, base_turn, squares):
    radicand = reach - squares
    root = jnp.sqrt(jnp.abs(radicand)) * layer_thick
    travelling = radicand > 0.0
    fading = jnp.where(travelling, 1.0, jnp.exp(-root))
    sine, cosine = sin_cos(jnp.where(travelling, root, 0.0) - base_turn)
    return fading * cosine, fading * sine


def make_phases(cos_ref, sin_ref, angular, reference):
    rows, cols = cos_ref.shape
    half = rows // 2
    reach = (angular * reference) * (angular * reference)
    base_turn = angular * layer_thick * reference
    step_x = 2.0 * math.pi / (rows * cell_width)
    step_y = 2.0 * math.pi / (cols * cell_width)
    lane = lax.broadcasted_iota(jnp.int32, (8, cols), 1)
    wave_y = jnp.where(lane <= cols // 2, lane, lane - cols // 2).astype(f32) * step_y
    square_y = wave_y * wave_y
    tall = 64

    def body(block, carry):
        start = pl.multiple_of(block * tall, tall)
        row = lax.broadcasted_iota(jnp.int32, (tall, cols), 0) + start
        wave_x = row.astype(f32) * step_x
        cosine, sine = phase_block(
            reach, base_turn, wave_x * wave_x + jnp.concatenate([square_y] * (tall // 8), axis=0)
        )
        cos_ref[pl.ds(start, tall), :] = cosine
        sin_ref[pl.ds(start, tall), :] = sine
        cos_ref[pl.ds(half + start, tall), :] = cosine
        sin_ref[pl.ds(half + start, tall), :] = sine
        return carry

    lax.fori_loop(0, half // tall, body, 0)
    edge = (half * step_x) ** 2
    cosine, sine = phase_block(reach, base_turn, edge + square_y)
    top = lax.broadcasted_iota(jnp.int32, (8, cols), 0) == 0
    cos_ref[half : half + 8, :] = jnp.where(top, cosine, cos_ref[half : half + 8, :])
    sin_ref[half : half + 8, :] = jnp.where(top, sine, sin_ref[half : half + 8, :])


def dot(left, right):
    return jnp.dot(left, right, preferred_element_type=f32)


def march_out(fill_half, forward_x, scalars, half_ref, spectrum, ready=((), ())):
    angular, references = scalars
    spec_ref, cos_ref, sin_ref = spectrum
    for j in range(3):
        make_phases(cos_ref.at[j], sin_ref.at[j], angular, references[j])
    for wait in ready[0]:
        wait()
    for plane in range(4):
        fill_half(plane)
    for wait in ready[1]:
        wait()
    for plane in range(4):
        spec_ref[plane] = dot(forward_x[...], half_ref[plane])


def march_back(spectrum, inverse_x, shift_ref, out_ref, ready=()):
    spec_ref, cos_ref, sin_ref = spectrum
    for j in range(3):
        for field in range(2):
            real, imag = spec_ref[2 * field], spec_ref[2 * field + 1]
            cosine, sine = cos_ref[j], sin_ref[j]
            shift_ref[j, 2 * field] = (cosine * real - sine * imag).astype(bf16)
            shift_ref[j, 2 * field + 1] = (cosine * imag + sine * real).astype(bf16)
        if j == 0:
            for wait in ready:
                wait()
        for plane in range(4):
            out_ref[j, plane] = dot(inverse_x[...], shift_ref[j, plane]).astype(bf16)


def blend(returned_ref, slow_ref, bracket_ref, inverse_y, scalars, parts, put_wave, put_cross, starts):
    tall, cols = slow_ref.shape[1:]
    chunk = 16
    angular, (low, mid, high) = scalars
    slope_low = 1.0 / (mid - low)
    slope_high = 1.0 / (high - mid)
    def first_row(block):
        return pl.multiple_of(starts[block], tall)

    def fill(part_ref, block):
        left = returned_ref[:, :, pl.ds(first_row(block), tall), :].reshape(12 * tall, cols)
        part_ref[...] = dot(left, inverse_y[...]).reshape(12, tall, cols)

    def mix(part_ref, block):
        start = first_row(block)
        crossed = []
        for piece in range(tall // chunk):
            within = slice(piece * chunk, (piece + 1) * chunk)
            here = pl.ds(pl.multiple_of(start + piece * chunk, chunk), chunk)
            slow = slow_ref[block, within].astype(f32)
            lower = bracket_ref[here, :] == 0
            weight = jnp.where(lower, (slow - low) * slope_low, (slow - mid) * slope_high)
            weight = jnp.minimum(jnp.maximum(weight, 0.0), 1.0)
            sine, cosine = sin_cos(slow * (angular * layer_thick))
            halves = []
            for plane in range(4):
                if inverse_y is None:
                    first, second, third = [returned_ref[4 * j + plane, here] for j in range(3)]
                else:
                    first, second, third = [part_ref[4 * j + plane, within] for j in range(3)]
                bottom = jnp.where(lower, first, second)
                top = jnp.where(lower, second, third)
                halves.append(bottom + weight * (top - bottom))
            fresh = []
            for field in range(2):
                real, imag = halves[2 * field], halves[2 * field + 1]
                fresh.append((cosine * real - sine * imag).astype(bf16))
                fresh.append((cosine * imag + sine * real).astype(bf16))
            if put_wave is not None:
                for plane in range(4):
                    put_wave(block, within, plane, fresh[plane])
            s_real, s_imag, r_real, r_imag = [value.astype(f32) for value in fresh]
            crossed.append(
                (
                    (s_real * r_real - s_imag * r_imag).astype(bf16),
                    (s_real * r_imag + s_imag * r_real).astype(bf16),
                )
            )
        for side in range(2):
            put_cross(block, side, jnp.concatenate([pair[side] for pair in crossed], axis=0))

    if inverse_y is None:
        for block in range(len(starts)):
            mix(None, block)
        return
    even, odd = parts
    fill(even, 0)
    for block in range(len(starts)):
        here, other = (even, odd) if block % 2 == 0 else (odd, even)
        if block + 1 < len(starts):
            fill(other, block + 1)
        mix(here, block)


PIECES = 4


def piece_starts(piece):
    rank = lax.axis_index("freq")
    core, place = rank % 2, (rank // 2) % PIECES
    return [
        [(side * PIECES + (place ^ step)) * piece for step in range(PIECES)]
        for side in (core, 1 - core)
    ]


def window_kernel(
    map_hbm, corner_hbm, slab_hbm, keep_ref, send_ref, map_ref, corner_ref, slab_ref, sems
):
    depths, piece, cols = keep_ref.shape[1:]
    slab_count = slab_hbm.shape[0]
    tall, wide = slab_hbm.shape[1:]
    copies = [
        pltpu.make_async_copy(map_hbm, map_ref, sems.at[0]),
        pltpu.make_async_copy(corner_hbm, corner_ref, sems.at[1]),
    ]
    for copy in copies:
        copy.start()
    if slab_count == 1:
        whole = pltpu.make_async_copy(slab_hbm.at[0], slab_ref.at[0], sems.at[2])
        whole.start()
    for copy in copies:
        copy.wait()
    if slab_count == 1:
        whole.wait()
    rank = lax.axis_index("freq")
    rows = 2 * PIECES * piece
    first_row = jnp.minimum((corner_ref[0] // 16) * 16, tall - rows - 16)
    first_col = jnp.minimum((corner_ref[1] // 128) * 128, wide - cols - 128)
    above = corner_ref[0] - first_row
    before = corner_ref[1] - first_col
    reach = piece + 16
    span = cols + 128
    for depth in range(depths):
        slab = map_ref[depth]
        mine = slab // slab_count == rank

        @pl.when(mine)
        def _():
            if slab_count == 1:
                here = slab_ref.at[0]
            else:
                here = slab_ref.at[0]
                copy = pltpu.make_async_copy(
                    slab_hbm.at[lax.rem(slab, slab_count)], here, sems.at[2]
                )
                copy.start()
                copy.wait()
            for target, starts in zip((keep_ref, send_ref), piece_starts(piece)):
                for step, start in enumerate(starts):
                    block = here[
                        pl.ds(pl.multiple_of(first_row + start, 16), reach),
                        pl.ds(pl.multiple_of(first_col, 128), span),
                    ].astype(f32)
                    block = pltpu.roll(block, lax.rem(span - before, span), 1)[:, :cols]
                    block = pltpu.roll(block, lax.rem(reach - above, reach), 0)[:piece]
                    target[step, depth] = block.astype(bf16)

        @pl.when(jnp.logical_not(mine))
        def _():
            for target in (keep_ref, send_ref):
                target[:, depth] = jnp.zeros((PIECES, piece, cols), bf16)


def fetch(pairs, sems):
    copies = [
        pltpu.make_async_copy(source, target, sems.at[index])
        for index, (source, target) in enumerate(pairs)
    ]
    for copy in copies:
        copy.start()
    return [copy.wait for copy in copies]


def out_kernel(
    bins_hbm,
    gaps_hbm,
    source_hbm,
    receiver_hbm,
    forward_x_hbm,
    forward_y_hbm,
    spec_ref,
    cos_ref,
    sin_ref,
    held_ref,
    bins_ref,
    gaps_ref,
    wave_ref,
    forward_x,
    forward_y,
    half_ref,
    sems,
):
    waits = fetch(
        [
            (bins_hbm, bins_ref),
            (gaps_hbm, gaps_ref),
            (forward_y_hbm, forward_y),
            (source_hbm.at[:, 0], wave_ref.at[0:2]),
            (receiver_hbm.at[:, 0], wave_ref.at[2:4]),
            (forward_x_hbm, forward_x),
        ],
        sems,
    )
    waits[0]()
    waits[1]()
    angular = angular_of(bins_ref)
    held_ref[0:1] = jnp.full((1, held_ref.shape[1]), angular, f32)
    for depth in range(gaps_ref.shape[0]):
        for j, reference in enumerate(references_of(gaps_ref, depth)):
            row = 1 + 3 * depth + j
            held_ref[row : row + 1] = jnp.full((1, held_ref.shape[1]), reference, f32)

    def fill_half(plane):
        half = dot(wave_ref[plane], forward_y[...])
        half_ref[plane] = (half if plane < 3 else -half).astype(bf16)

    march_out(
        fill_half,
        forward_x,
        (angular, references_of(gaps_ref, 0)),
        half_ref,
        (spec_ref, cos_ref, sin_ref),
        ready=(waits[2:5], waits[5:]),
    )


def back_kernel(
    spec_ref,
    cos_ref,
    sin_ref,
    inverse_x_hbm,
    bracket_hbm,
    inverse_y_hbm,
    out_ref,
    bracket_ref,
    inverse_y,
    inverse_x,
    shift_ref,
    sems,
):
    waits = fetch(
        [
            (inverse_x_hbm, inverse_x),
            (bracket_hbm.at[0], bracket_ref),
            (inverse_y_hbm, inverse_y),
        ],
        sems,
    )
    march_back((spec_ref, cos_ref, sin_ref), inverse_x, shift_ref, out_ref, waits[:1])
    for wait in waits[1:]:
        wait()


def unfold_kernel(returned_ref, inverse_y, part_ref):
    rows, cols = returned_ref.shape[2:]
    for j in range(3):
        for plane in range(4):
            part_ref[4 * j + plane] = dot(returned_ref[j, plane], inverse_y[...])


def place_of(rank):
    here = lax.axis_index("freq")
    return (rank ^ here) % 2, (rank // 2) ^ (here // 2)


def mix_kernel(*refs, depth, far, last, paired):
    held_ref, returned_ref, slow_ref, bracket_ref = refs[:4]
    inverse_y, rest = (None, refs[4:]) if depth == 0 else (refs[4], refs[5:])
    if far:
        near_cross, rest = rest[0], rest[1:]
    if not last:
        wave_ref, rest = rest[0], rest[1:]
    cross_ref, *parts = rest
    piece = slow_ref.shape[2]
    tile = cross_ref.shape[-2]
    tiles = piece // tile
    near_starts, far_starts = piece_starts(piece)
    starts = far_starts if far else near_starts
    if far:
        for step, start in enumerate(near_starts):
            if paired:
                for part in range(tiles):
                    cross_ref[place_of(start // tile + part)] = near_cross[step * tiles + part]
                continue
            cross_ref[pl.ds(start // tile, tiles)] = near_cross[step * tiles : (step + 1) * tiles]

    def put_wave(block, within, plane, values):
        wave_ref[plane, block * piece + within.start : block * piece + within.stop] = values

    def put_cross(block, side, values):
        for part in range(tiles):
            rank = starts[block] // tile + part if far else block * tiles + part
            place = place_of(rank) if far and paired else (rank,)
            cross_ref[*place, side] = values[part * tile : (part + 1) * tile]

    blend(
        returned_ref,
        slow_ref.at[:, depth],
        bracket_ref,
        inverse_y,
        scalars_of(held_ref, depth),
        parts,
        None if last else put_wave,
        put_cross,
        starts,
    )


def pair_mix_kernel(
    held_ref, returned_ref, near_slow, far_slow, bracket_ref, inverse_y, cross_ref, even, odd, *, depth
):
    piece = near_slow.shape[2]
    tile = cross_ref.shape[-2]
    for slow_ref, starts in zip((near_slow, far_slow), piece_starts(piece)):

        def put_cross(block, side, values, starts=starts):
            for part in range(piece // tile):
                place = place_of(starts[block] // tile + part)
                cross_ref[*place, side] = values[part * tile : (part + 1) * tile]

        blend(
            returned_ref,
            slow_ref.at[:, depth],
            bracket_ref,
            inverse_y,
            scalars_of(held_ref, depth),
            (even, odd),
            None,
            put_cross,
            starts,
        )


def march_kernel(
    held_ref,
    near_wave,
    far_wave,
    bracket_hbm,
    forward_x_hbm,
    forward_y_hbm,
    inverse_x_hbm,
    out_ref,
    bracket_ref,
    forward_x,
    forward_y,
    inverse_x,
    sems,
    half_ref,
    shift_ref,
    *spectrum,
    depth,
):
    waits = fetch(
        [
            (forward_y_hbm, forward_y),
            (forward_x_hbm, forward_x),
            (inverse_x_hbm, inverse_x),
            (bracket_hbm.at[depth], bracket_ref),
        ],
        sems,
    )
    piece = near_wave.shape[1] // PIECES

    def fill_half(plane):
        for starts, wave_ref in zip(piece_starts(piece), (near_wave, far_wave)):
            half = dot(wave_ref[plane], forward_y[...]).astype(bf16)
            for step, start in enumerate(starts):
                here = pl.ds(pl.multiple_of(start, piece), piece)
                half_ref[plane, here, :] = half[step * piece : (step + 1) * piece]

    march_out(
        fill_half,
        forward_x,
        scalars_of(held_ref, depth),
        half_ref,
        spectrum,
        ready=(waits[:1], waits[1:2]),
    )
    march_back(spectrum, inverse_x, shift_ref, out_ref, waits[2:3])
    waits[3]()


IMAGE_ROWS = 8
PAIR_ORDER = (2, 4, 5, 6, 7, 3, 1)


def lag_kernel(lag_ref, *weight_refs):
    bins, pair, lags = lag_ref.shape
    height = bins * pair * IMAGE_ROWS
    here = lax.axis_index("freq")
    steps = (0, *PAIR_ORDER)
    by_pair = [2 * steps[spot // 2] + spot % 2 for spot in range(bins)] if weight_refs[1:] else None
    for weight_ref, spots, mask in zip(weight_refs, (range(bins), by_pair), (0, here)):
        table = jnp.concatenate(
            [
                jnp.broadcast_to(lag_ref[spot ^ mask][:, None], (pair, IMAGE_ROWS, lags)).reshape(
                    pair * IMAGE_ROWS, lags
                )
                for spot in spots
            ],
            axis=0,
        )
        place = lax.broadcasted_iota(jnp.int32, (height, lags), 0) % IMAGE_ROWS
        for row in range(IMAGE_ROWS):
            weight_ref[:, row * lags : (row + 1) * lags] = jnp.where(
                place == row, table, 0.0
            ).astype(bf16)


def image_kernel(*refs, scale, depth, aliased, count):
    cross_refs, weight_ref = refs[:count], refs[count]
    out_hbm, made_ref, sems = refs[count + 1 + aliased :]
    tile, cols, lags = made_ref.shape
    copies = []
    for group in range(tile // IMAGE_ROWS):
        rows = slice(group * IMAGE_ROWS, (group + 1) * IMAGE_ROWS)
        left = jnp.concatenate(
            [ref[..., rows, :].astype(f32).reshape(-1, cols) for ref in cross_refs], axis=0
        )
        left = left.T.astype(bf16)
        for row in range(IMAGE_ROWS):
            place = group * IMAGE_ROWS + row
            made_ref[place] = dot(left, weight_ref[:, row * lags : (row + 1) * lags]) * scale
            copies.append(
                pltpu.make_async_copy(
                    made_ref.at[place], out_hbm.at[depth, place], sems.at[place]
                )
            )
            copies[-1].start()
    for copy in copies:
        copy.wait()


def pin(value):
    return pltpu.with_memory_space_constraint(value, pltpu.HBM)


def shards(
    source_field,
    receiver_field,
    slowness_slabs,
    slab_map,
    reference_gaps,
    reference_index,
    frequency_bins,
    shot_corner,
    *,
    ranks,
):
    rows, cols = source_field.shape[2:]
    depths = slab_map.shape[0]
    slab_count = slowness_slabs.shape[0]
    half = rows // 2
    piece = half // PIECES
    tile = rows // ranks
    bins = frequency_bins.shape[0]
    slab_shape = slowness_slabs.shape[1:]
    forward_x, inverse_x = real_table(rows)
    forward_x = forward_x.T
    forward_y, inverse_y = real_table(cols)
    inverse_y = inverse_y.T

    hbm = pl.BlockSpec(memory_space=pltpu.HBM)
    vmem = pl.BlockSpec(memory_space=VMEM)
    dma = pltpu.SemaphoreType.DMA

    keep, send = pl.pallas_call(
        window_kernel,
        in_specs=[hbm] * 3,
        out_specs=[vmem] * 2,
        out_shape=[jax.ShapeDtypeStruct((PIECES, depths, piece, cols), bf16)] * 2,
        scratch_shapes=[
            SMEM(slab_map.shape, jnp.int32),
            SMEM(shot_corner.shape, jnp.int32),
            VMEM((1,) + slab_shape, bf16),
            dma((3,)),
        ],
        compiler_params=pltpu.CompilerParams(vmem_limit_bytes=16 << 20),
        name="window",
    )(pin(slab_map), pin(shot_corner), pin(slowness_slabs))

    def swap(value, bit):
        return lax.ppermute(value, "freq", [(i, i ^ bit) for i in range(ranks)])

    held = keep + swap(send, 1)
    early_bins, held = lax.optimization_barrier((frequency_bins, held))
    spectrum_shapes = [
        jax.ShapeDtypeStruct((4, rows, cols), f32),
        jax.ShapeDtypeStruct((3, rows, cols), f32),
        jax.ShapeDtypeStruct((3, rows, cols), f32),
    ]
    returned_shape = jax.ShapeDtypeStruct((3, 4, rows, cols), bf16)
    flops = 2 * 4 * (1 + 3) * rows * rows * cols
    *spectrum, held_scalars = pl.pallas_call(
        out_kernel,
        in_specs=[hbm] * 6,
        out_specs=[vmem] * 4,
        out_shape=spectrum_shapes
        + [jax.ShapeDtypeStruct((8 * pl.cdiv(1 + 3 * depths, 8), cols), f32)],
        scratch_shapes=[
            SMEM(frequency_bins.shape, jnp.int32),
            SMEM(reference_gaps.shape, f32),
            VMEM((4, rows, cols), bf16),
            VMEM((rows, rows), bf16),
            VMEM((cols, cols), bf16),
            VMEM((4, rows, cols), bf16),
            dma((6,)),
        ],
        compiler_params=pltpu.CompilerParams(vmem_limit_bytes=20 << 20),
        cost_estimate=pl.CostEstimate(flops=flops // 2, bytes_accessed=4 << 20, transcendentals=0),
        name="out",
    )(
        *[
            pin(value)
            for value in (
                early_bins,
                reference_gaps,
                source_field,
                receiver_field,
                forward_x,
                forward_y,
            )
        ]
    )
    own = held[0] + sum(swap(held[step], 2 * step) for step in range(1, PIECES))
    own, spectrum = lax.optimization_barrier((own, spectrum))
    returned, bracket, kept_inverse = pl.pallas_call(
        back_kernel,
        in_specs=[vmem] * 3 + [hbm] * 3,
        out_specs=[vmem] * 3,
        out_shape=[
            returned_shape,
            jax.ShapeDtypeStruct((rows, cols), jnp.int32),
            jax.ShapeDtypeStruct((cols, cols), bf16),
        ],
        scratch_shapes=[
            VMEM((rows, rows), bf16),
            VMEM((3, 4, rows, cols), bf16),
            dma((3,)),
        ],
        compiler_params=pltpu.CompilerParams(vmem_limit_bytes=24 << 20),
        cost_estimate=pl.CostEstimate(flops=flops, bytes_accessed=4 << 20, transcendentals=0),
        name="back",
    )(*spectrum, pin(inverse_x), pin(reference_index), pin(inverse_y))
    bit = 2 * PIECES
    while bit < ranks:
        own = own + swap(own, bit)
        bit *= 2
    own, returned = lax.optimization_barrier((own, returned))
    pieces = [own] + [swap(own, 2 * step) for step in range(1, PIECES)]
    part = pl.pallas_call(
        unfold_kernel,
        in_specs=[vmem] * 2,
        out_specs=vmem,
        out_shape=jax.ShapeDtypeStruct((12, rows, cols), f32),
        compiler_params=pltpu.CompilerParams(vmem_limit_bytes=16 << 20),
        cost_estimate=pl.CostEstimate(flops=flops // 2, bytes_accessed=1 << 20, transcendentals=0),
        name="unfold",
    )(returned, kept_inverse)
    pieces, part = lax.optimization_barrier((pieces, part))
    near_slow = jnp.stack(pieces)
    offsets = jnp.arange(LAGS, dtype=jnp.int32) - LAGS // 2
    cycles = jnp.mod(frequency_bins[:, None] * offsets[None, :], period_bins).astype(f32)
    angles = cycles * (2.0 * math.pi / period_bins)
    lag_weights = jnp.stack([jnp.cos(angles), jnp.sin(angles)], axis=1).astype(bf16)

    far_slow, lag_weights = lax.optimization_barrier((swap(near_slow, 1), lag_weights))

    blend_scratch = [VMEM((12, piece, cols), f32)] * 2
    paired = ranks == 2 * (1 + len(PAIR_ORDER)) and depths > 1 and tile % (2 * IMAGE_ROWS) == 0
    wave_shape = jax.ShapeDtypeStruct((4, half, cols), bf16)

    def mix(depth, far, *operands):
        last = depth == depths - 1
        tiles = (ranks // 2,) if not far else (2, ranks // 2) if paired and last else (ranks,)
        return pl.pallas_call(
            functools.partial(
                mix_kernel, depth=depth, far=far, last=last, paired=paired and last
            ),
            in_specs=[vmem] * len(operands),
            out_specs=[vmem] * (2 - last),
            out_shape=[wave_shape] * (1 - last)
            + [jax.ShapeDtypeStruct(tiles + (2, tile, cols), bf16)],
            scratch_shapes=blend_scratch if depth else [],
            compiler_params=pltpu.CompilerParams(vmem_limit_bytes=16 << 20),
            cost_estimate=pl.CostEstimate(
                flops=flops // 4, bytes_accessed=1 << 20, transcendentals=0
            ),
            name="far" if far else "near",
        )(*operands)

    *near_wave, near_cross = mix(0, False, held_scalars, part, near_slow, bracket)
    *far_wave, cross = mix(
        0, True, held_scalars, part, far_slow, bracket, near_cross
    )
    crosses = [cross]
    for depth in range(1, depths):
        returned, bracket = pl.pallas_call(
            functools.partial(march_kernel, depth=depth),
            in_specs=[vmem] * 3 + [hbm] * 4,
            out_specs=[vmem] * 2,
            out_shape=[returned_shape, jax.ShapeDtypeStruct((rows, cols), jnp.int32)],
            scratch_shapes=[
                VMEM((rows, rows), bf16),
                VMEM((cols, cols), bf16),
                VMEM((rows, rows), bf16),
                dma((4,)),
                VMEM((4, rows, cols), bf16),
                VMEM((3, 4, rows, cols), bf16),
                *[VMEM(shape.shape, f32) for shape in spectrum_shapes],
            ],
            compiler_params=pltpu.CompilerParams(vmem_limit_bytes=28 << 20),
            cost_estimate=pl.CostEstimate(
                flops=3 * flops // 2, bytes_accessed=8 << 20, transcendentals=0
            ),
            name="march",
        )(
            held_scalars,
            *near_wave,
            *far_wave,
            pin(reference_index),
            pin(forward_x),
            pin(forward_y),
            pin(inverse_x),
        )
        if paired and depth == depths - 1:
            cross = pl.pallas_call(
                functools.partial(pair_mix_kernel, depth=depth),
                in_specs=[vmem] * 6,
                out_specs=vmem,
                out_shape=jax.ShapeDtypeStruct((2, ranks // 2, 2, tile, cols), bf16),
                scratch_shapes=blend_scratch,
                compiler_params=pltpu.CompilerParams(vmem_limit_bytes=16 << 20),
                cost_estimate=pl.CostEstimate(
                    flops=flops // 2, bytes_accessed=1 << 20, transcendentals=0
                ),
                name="mix",
            )(held_scalars, returned, near_slow, far_slow, bracket, kept_inverse)
        else:
            *near_wave, near_cross = mix(
                depth, False, held_scalars, returned, near_slow, bracket, kept_inverse
            )
            *far_wave, cross = mix(
                depth, True, held_scalars, returned, far_slow, bracket, kept_inverse, near_cross
            )
        crosses.append(cross)

    scale = bins ** (-0.5)
    def exchange(value):
        return lax.all_to_all(value, "freq", split_axis=0, concat_axis=0, tiled=True)

    if not paired:
        arrivals = [[exchange(cross)] for cross in crosses]
    else:
        arrivals = [[exchange(cross)] for cross in crosses[:-1]]
        by_core = crosses[-1]
        by_chip = jnp.stack([by_core[0], swap(by_core[1], 1)], axis=1)
        arrivals.append([by_chip[0]] + [swap(by_chip[step], 2 * step) for step in PAIR_ORDER])
    if tile % (2 * IMAGE_ROWS):
        summed = jnp.einsum(
            "dwcab,wcl->dabl",
            jnp.stack([arrived for (arrived,) in arrivals]),
            lag_weights,
            preferred_element_type=f32,
        )
        return summed * scale
    height = bins * 2 * IMAGE_ROWS
    weights = pl.pallas_call(
        lag_kernel,
        in_specs=[vmem],
        out_specs=[vmem] * (1 + paired),
        out_shape=[jax.ShapeDtypeStruct((height, IMAGE_ROWS * LAGS), bf16)] * (1 + paired),
        compiler_params=pltpu.CompilerParams(vmem_limit_bytes=16 << 20),
        name="lag",
    )(lag_weights.astype(f32))
    image = None
    for depth, arrived in enumerate(arrivals):
        aliased = image is not None
        count = len(arrived)
        image = pl.pallas_call(
            functools.partial(
                image_kernel, scale=scale, depth=depth, aliased=aliased, count=count
            ),
            in_specs=[vmem] * (count + 1) + [hbm] * aliased,
            out_specs=hbm,
            out_shape=jax.ShapeDtypeStruct((depths, tile, cols, LAGS), f32),
            scratch_shapes=[VMEM((tile, cols, LAGS), f32), dma((tile,))],
            input_output_aliases={count + 1: 0} if aliased else {},
            compiler_params=pltpu.CompilerParams(vmem_limit_bytes=28 << 20),
            name="image",
        )(*arrived, weights[count > 1], *([image] if aliased else []))
    return image


def solution(mesh):
    placed = (
        P("grp", "freq", None, None),
        P("grp", "freq", None, None),
        P(("grp", "freq"), None, None),
        P("grp"),
        P("grp", None),
        P("grp", None, None),
        P(),
        P("grp"),
    )
    return jax.shard_map(
        functools.partial(shards, ranks=mesh.shape["freq"]),
        mesh=mesh,
        in_specs=placed,
        out_specs=P("grp", "freq", None, None),
        check_vma=False,
    )
```
